256 devices in a mesh: row: 16 (over y, z_lo, core), col: 16 (over z_hi, x).
Axes of the slice: x: 4, y: 4, z: 8 (z_hi: 4, z_lo: 2; z = z_hi * 2 + z_lo), core: 2. Of those that a mesh axis runs over, the one named last changes fastest.
Arguments:
- pair: bfloat16 [256, 256, 128], P('row', 'col'), may hold values from -6 to 6
- pair_cot: bfloat16 [256, 256, 128], P('row', 'col'), may hold values from -6 to 6
- mask: int32 [256], replicated, may hold values 0 or 1
- chain_ids: int32 [256], replicated, may hold values from 0 to 3, never falling along the last dimension, each value on 1 to 128 neighbouring positions
- chain_bias: float32 [128], replicated, may hold values from -4 to 4
- in_weight: bfloat16 [2, 128, 512], replicated, may hold values from -0.5 to 0.5
- gate_weight: bfloat16 [2, 128, 128], replicated, may hold values from -0.5 to 0.5
- out_weight: bfloat16 [2, 128, 128], replicated, may hold values from -0.5 to 0.5
- in_gain: float32 [2, 128], replicated, may hold values from 0.1 to 1.9
- out_gain: float32 [2, 128], replicated, may hold values from 0.1 to 1.9
Outputs:
- new_pair: bfloat16 [256, 256, 128], P('row', 'col')
- pair_grad: float32 [256, 256, 128], P('row', 'col')
- in_weight_grad: float32 [2, 128, 512], replicated
- gate_weight_grad: float32 [2, 128, 128], replicated
- out_weight_grad: float32 [2, 128, 128], replicated
The draws below stay inside these ranges and needn't reach their ends.
Inputs may be any that keep to these rules, and one draw needn't show every extreme that they name: `chain_ids`: chain numbers never fall along the residues; each of the 4 chains has 1 to 128 residues, one exactly 128.
All inputs are finite; a program needn't handle non-finite values.
Results may differ from the reference program's by a relative error of at most 0.027.
Values may be sent and summed in bfloat16 or wider, within the bound.
No kernel may reach another device: no remote copies, remote signals or barrier semaphores. Data moves between devices by JAX's collectives and lax.ppermute only.
A program may use at most 64 MiB of HBM per device.

```python
import math
import jax
import jax.numpy as jnp
import numpy as np
from jax import lax

CZ = 128
HID = 128
RES = 256


def with_ends(values, rng, least, top_value):
    longest = values.shape.index(max(values.shape))
    spots = []
    for shift in (0, 1):
        where = [jax.random.randint(jax.random.fold_in(rng, axis), (), 0, length) for axis, length in enumerate(values.shape)]
        where[longest] = (where[longest] + shift) % values.shape[longest]
        spots.append(tuple(where))
    return values.at[spots[0]].set(least).at[spots[1]].set(top_value)


def block_levels(rng, extent, cuts, low, top_value):
    def one(axis_at, shards_of):
        heights = jax.random.uniform(jax.random.fold_in(jax.random.fold_in(rng, 6), axis_at), (shards_of,), jnp.float32, low / len(cuts), top_value / len(cuts))
        return jnp.repeat(jnp.exp(heights), extent[axis_at] // shards_of).reshape((-1,) + (1,) * (len(extent) - axis_at - 1))

    level = one(*cuts[0])
    for cut in cuts[1:]:
        level = level * one(*cut)
    return level


def split_up(amount, total, bound, skew):
    weights = [(1 << 20) // math.isqrt(rank ** skew) + 1 for rank in range(2, amount + 1)]
    spare, holding = total - bound - (amount - 1), [1] * (amount - 1)
    while spare > 0:
        candidates = [i for i in range(amount - 1) if holding[i] < bound]
        pool, left = sum([weights[i] for i in candidates]), spare
        for i in candidates:
            more = min(bound - holding[i], max(1, left * weights[i] // pool), spare)
            holding[i] = holding[i] + more
            spare = spare - more
    return np.array([bound] + holding)


def uneven(rng, count, total, reach, lean):
    if count == 2:
        one = jax.random.randint(rng, (), max(1, total - reach), min(reach, total - 1) + 1)
        return jnp.stack([one, total - one])
    lengths = jnp.asarray(split_up(count, total, reach, lean), jnp.int32)
    twos = (count - 1) // 2
    donor, receiver = lengths[1:1 + 2 * twos:2], lengths[2:2 + 2 * twos:2]
    slack = jnp.minimum(donor - 1, reach - receiver)
    shifted = jax.random.randint(jax.random.fold_in(rng, 1), (twos,), 0, 1 << 20) % (slack + 1)
    lengths = lengths.at[1:1 + 2 * twos:2].set(donor - shifted).at[2:2 + 2 * twos:2].set(receiver + shifted)
    return lengths[jax.random.permutation(jax.random.fold_in(rng, 2), count)]


def bell_draw(own_key, dims, scale, most, cuts=(), kind=jnp.bfloat16):
    level = block_levels(own_key, dims, cuts, -0.22, 0.18) if cuts else 1.0
    drawn = jax.random.normal(own_key, dims, jnp.float32) * scale * level
    return jnp.minimum(jnp.maximum(drawn, -most), most).astype(kind)


def setup_inputs(seed: int = 0) -> dict:
    splits = jax.random.split(jax.random.key(seed), 11)
    return {
        "pair": bell_draw(splits[0], (RES, RES, CZ), 1.0, 6.0, ((0, 16), (1, 16))),
        "pair_cot": bell_draw(splits[1], (RES, RES, CZ), 1.0, 6.0, ((0, 16), (1, 16))),
        "mask": with_ends((jax.random.randint(splits[2], (RES,), 0, 8) < 7).astype(jnp.int32), jax.random.fold_in(splits[2], 1), 0, 1),
        "chain_ids": jnp.searchsorted(jnp.cumsum(uneven(splits[3], 4, RES, RES // 2, 0)), jnp.arange(RES), side="right").astype(jnp.int32),
        "chain_bias": bell_draw(splits[4], (CZ,), 1.0, 4.0, (), jnp.float32),
        "in_weight": bell_draw(splits[5], (2, CZ, 4 * HID), CZ ** -0.5, 0.5),
        "gate_weight": bell_draw(splits[6], (2, CZ, CZ), CZ ** -0.5, 0.5),
        "out_weight": bell_draw(splits[7], (2, HID, CZ), HID ** -0.5, 0.5),
        "in_gain": jnp.clip(1.0 + 0.18 * jax.random.normal(splits[8], (2, CZ), jnp.float32), 0.1, 1.9),
        "out_gain": jnp.clip(1.0 + 0.18 * jax.random.normal(splits[9], (2, HID), jnp.float32), 0.1, 1.9),
    }


def layer_norm(value, gain):
    mean = lax.optimization_barrier(jnp.mean(value, axis=-1, keepdims=True))
    centered = value - mean
    var = lax.optimization_barrier(jnp.mean(centered * centered, axis=-1, keepdims=True))
    return centered * lax.rsqrt(var + 1e-05) * gain

def prepare(field, w_in, w_gate, gain, mask_rows, mask_cols):
    normed = layer_norm(field, gain).astype(jnp.bfloat16)
    proj = jnp.dot(normed, w_in, preferred_element_type=jnp.float32)
    width = w_in.shape[1] // 4
    pair_mask = mask_rows[:, None, None] * mask_cols[None, :, None]
    left = pair_mask * jax.nn.sigmoid(proj[..., 0:width]) * proj[..., width:2 * width]
    right = pair_mask * jax.nn.sigmoid(proj[..., 2 * width:3 * width]) * proj[..., 3 * width:4 * width]
    gating = jax.nn.sigmoid(jnp.dot(normed, w_gate, preferred_element_type=jnp.float32))
    return (left.astype(jnp.bfloat16), right.astype(jnp.bfloat16), gating)

def finish(product, gating, field, gain, w_out):
    normed = layer_norm(product, gain).astype(jnp.bfloat16)
    return field + gating * jnp.dot(normed, w_out, preferred_element_type=jnp.float32)

def contract(form, left, right):
    return jnp.einsum(form, left.astype(jnp.float32), right.astype(jnp.float32), precision=lax.Precision.HIGHEST)

def reference(pair, pair_cot, mask, chain_ids, chain_bias, in_weight, gate_weight, out_weight, in_gain, out_gain):
    mask_f = mask.astype(jnp.float32)
    same = (chain_ids[:, None] == chain_ids[None, :]).astype(jnp.float32)
    start = pair.astype(jnp.float32) + same[:, :, None] * chain_bias

    def pre0(field, wi, wg):
        return prepare(field, wi, wg, in_gain[0], mask_f, mask_f)

    def pre1(field, wi, wg):
        return prepare(field, wi, wg, in_gain[1], mask_f, mask_f)

    def fin0(xx, gg, zz, ww):
        return finish(xx, gg, zz, out_gain[0], ww)

    def fin1(xx, gg, zz, ww):
        return finish(xx, gg, zz, out_gain[1], ww)
    (left0, right0, gate0), back_pre0 = jax.vjp(pre0, start, in_weight[0], gate_weight[0])
    prod0 = contract('ikc,jkc->ijc', left0, right0)
    first, back_fin0 = jax.vjp(fin0, prod0, gate0, start, out_weight[0])
    (left1, right1, gate1), back_pre1 = jax.vjp(pre1, first, in_weight[1], gate_weight[1])
    prod1 = contract('kic,kjc->ijc', left1, right1)
    second, back_fin1 = jax.vjp(fin1, prod1, gate1, first, out_weight[1])
    new_pair = second.astype(jnp.bfloat16)
    gx1, gg1, gz_fin1, gwo1 = back_fin1(pair_cot.astype(jnp.float32))
    gx1 = gx1.astype(jnp.bfloat16)
    ga1 = contract('ijc,kjc->kic', gx1, right1).astype(jnp.bfloat16)
    gb1 = contract('kic,ijc->kjc', left1, gx1).astype(jnp.bfloat16)
    gz_pre1, gwi1, gwg1 = back_pre1((ga1, gb1, gg1))
    grad_first = gz_fin1 + gz_pre1
    gx0, gg0, gz_fin0, gwo0 = back_fin0(grad_first)
    gx0 = gx0.astype(jnp.bfloat16)
    ga0 = contract('ijc,jkc->ikc', gx0, right0).astype(jnp.bfloat16)
    gb0 = contract('ijc,ikc->jkc', gx0, left0).astype(jnp.bfloat16)
    gz_pre0, gwi0, gwg0 = back_pre0((ga0, gb0, gg0))
    pair_grad = gz_fin0 + gz_pre0
    in_weight_grad = jnp.stack([gwi0.astype(jnp.float32), gwi1.astype(jnp.float32)])
    gate_weight_grad = jnp.stack([gwg0.astype(jnp.float32), gwg1.astype(jnp.float32)])
    out_weight_grad = jnp.stack([gwo0.astype(jnp.float32), gwo1.astype(jnp.float32)])
    return (new_pair, pair_grad, in_weight_grad, gate_weight_grad, out_weight_grad)
```

```python
import functools

import jax
import jax.numpy as jnp
from jax import lax
from jax.experimental import pallas as pl
from jax.experimental.pallas import tpu as pltpu
from jax.sharding import Mesh, PartitionSpec as P

F32 = jnp.float32
BF16 = jnp.bfloat16
POS = 256
CH = 128
EPS = 1e-05
CHIPS = ("g", "q")
ALL = ("g", "h", "q")


def dot(a, b, ca, cb):
    return lax.dot_general(
        a.astype(BF16), b.astype(BF16), (((ca,), (cb,)), ((), ())), preferred_element_type=F32
    )


def swap_blocks(tiles):
    block = lax.broadcasted_iota(jnp.int32, tiles[0].shape, 1) // 16
    for d in (1, 2, 4):
        high = (block & d) != 0
        out = list(tiles)
        for t in range(8):
            if t & d == 0:
                lo, hi = tiles[t], tiles[t | d]
                out[t] = jnp.where(high, pltpu.roll(hi, 16 * d, 1), lo)
                out[t | d] = jnp.where(high, hi, pltpu.roll(lo, 128 - 16 * d, 1))
        tiles = out
    return tiles


def messages_to_matrix(src, off, w, dst):
    for half in range(2):
        for qh in range(2):
            tiles = [
                src[pl.ds((qh * 8 + t) * w + off + half, 16, stride=16 * w), :] for t in range(8)
            ]
            for t, tile in enumerate(swap_blocks(tiles)):
                dst[qh, pl.ds(half * 8 + t, 16, stride=16), :] = tile


def half_to_messages(src, dst, off, w):
    for half in range(2):
        for qh in range(2):
            tiles = [src[qh, pl.ds(half * 8 + t, 8, stride=16), :] for t in range(8)]
            for t, tile in enumerate(swap_blocks(tiles)):
                dst[pl.ds((qh * 8 + t) * w + off + half, 8, stride=16 * w), :] = tile


def put(ref, value):
    for qh in range(2):
        ref[qh] = value[:, qh * 128 : (qh + 1) * 128]


def get(ref):
    return jnp.concatenate([ref[0], ref[1]], axis=1)


def my_rows(ref):
    h = lax.axis_index("h")
    return jnp.concatenate(
        [
            jnp.concatenate(
                [ref[qh, pl.ds(pl.multiple_of((2 * g + h) * 16, 16), 16), :] for g in range(8)],
                axis=0,
            )
            for qh in range(2)
        ],
        axis=1,
    )


def channels_to_messages(v, dst, off, w):
    for g in range(8):
        for h in range(2):
            for half in range(2):
                dst[pl.ds((g * 32 + h * 16) * w + off + half, 16, stride=w), :] = v[
                    g * 16 : (g + 1) * 16, half * 128 : (half + 1) * 128
                ]


def messages_to_channels(src, off, w):
    return jnp.concatenate(
        [src[pl.ds(off + half, CH, stride=w), :] for half in range(2)], axis=1
    )


def column(row):
    square = jnp.broadcast_to(row, (CH, CH)).T
    return jnp.concatenate([square, square], axis=1)


def normalise(z):
    centered = z - jnp.mean(z, axis=0, keepdims=True)
    rstd = lax.rsqrt(jnp.mean(centered * centered, axis=0, keepdims=True) + EPS)
    return centered * rstd, rstd


def normalise_back(cot, hat, rstd):
    return rstd * (
        cot
        - jnp.mean(cot, axis=0, keepdims=True)
        - hat * jnp.mean(cot * hat, axis=0, keepdims=True)
    )


def prepare(z, gain, w_in, w_gate, m, n_ref, g_ref, send, send_ref):
    hat, _ = normalise(z)
    normed = (hat * gain).astype(BF16)
    n_ref[...] = normed
    p = dot(w_in, normed, 0, 0)
    a = m * jax.nn.sigmoid(p[0:128]) * p[128:256]
    b = m * jax.nn.sigmoid(p[256:384]) * p[384:512]
    g_ref[...] = jax.nn.sigmoid(dot(w_gate, normed, 0, 0))
    channels_to_messages(a, send, 0, 4)
    channels_to_messages(b, send, 2, 4)
    send_ref[...] = send[...].astype(BF16)


def prepare_back(recv, z, normed, gain, w_in, w_gate, m, dpg, dp):
    p = dot(w_in, normed, 0, 0)
    for k in range(2):
        cot = messages_to_channels(recv, 2 * k, 4) * m
        s = jax.nn.sigmoid(p[256 * k : 256 * k + 128])
        v = p[256 * k + 128 : 256 * k + 256]
        dp[256 * k : 256 * k + 128, :] = (cot * v * s * (1.0 - s)).astype(BF16)
        dp[256 * k + 128 : 256 * k + 256, :] = (cot * s).astype(BF16)
    dn = dot(w_in, dp[...], 1, 0) + dot(w_gate, dpg, 1, 0)
    hat, rstd = normalise(z)
    return normalise_back(dn * gain, hat, rstd)


def finish_back(x, dy, gain, w_out):
    hat, rstd = normalise(x)
    normed = (hat * gain).astype(BF16)
    gx = normalise_back(dot(w_out, dy, 1, 0) * gain, hat, rstd)
    return gx, dot(normed, dy, 1, 1)


def start_kernel(pair, mask, chain, bias, in_gain, w_in, w_gate, z_ref, n_ref, g_ref, m_ref, send_ref, send):
    row = 2 * lax.axis_index("g") + lax.axis_index("h")
    col = lax.axis_index("q")
    res = lax.broadcasted_iota(jnp.int32, (256, POS), 0)
    pos = lax.broadcasted_iota(jnp.int32, (256, POS), 1)
    both = jnp.concatenate(
        [
            jnp.broadcast_to(mask[...].astype(F32), (8, 256)),
            jnp.broadcast_to(chain[...].astype(F32), (8, 256)),
        ],
        axis=0,
    )
    of_row = dot(both, (res == row * 16 + pos // 16).astype(F32), 1, 0)
    of_col = dot(both, (res == col * 16 + pos % 16).astype(F32), 1, 0)
    m8 = of_row[0:8] * of_col[0:8]
    m_ref[...] = m8
    same = (of_row[8:9] == of_col[8:9]).astype(F32)
    z = pair[...].astype(F32).T + same * column(bias[...])
    z_ref[...] = z
    prepare(z, column(in_gain[0:1]), w_in[0], w_gate[0], m8[0:1], n_ref, g_ref, send, send_ref)


def middle_kernel(x_in, z0, g0, m, in_gain, out_gain, w_in, w_gate, w_out, z_ref, y_ref, n_ref, g_ref, send_ref, xs, send):
    xs[...] = x_in[...].astype(F32)
    hat, _ = normalise(messages_to_channels(xs, 0, 2))
    y = dot(w_out[0], hat * column(out_gain[0:1]), 0, 0)
    y_ref[...] = y
    z = z0[...] + g0[...] * y
    z_ref[...] = z
    prepare(z, column(in_gain[1:2]), w_in[1], w_gate[1], m[0:1], n_ref, g_ref, send, send_ref)


def turn_kernel(x_in, z1, g1, n1, cot_in, out_gain, w_out, new_ref, cot_ref, dpg_ref, gw_ref, send_ref, xs, send):
    xs[...] = x_in[...].astype(F32)
    x = messages_to_channels(xs, 0, 2)
    gain = column(out_gain[1:2])
    hat, _ = normalise(x)
    y = dot(w_out[1], hat * gain, 0, 0)
    g = g1[...]
    new_ref[...] = (z1[...] + g * y).T.astype(BF16)
    cot = cot_in[...].astype(F32).T
    cot_ref[...] = cot
    gx, gwo = finish_back(x, cot * g, gain, w_out[1])
    dpg = (cot * y * g * (1.0 - g)).astype(BF16)
    dpg_ref[...] = dpg
    gw_ref[0:128, :] = dot(n1[...], dpg, 1, 1)
    gw_ref[128:256, :] = gwo
    channels_to_messages(gx, send, 0, 2)
    send_ref[...] = send[...].astype(BF16)


def back_kernel(gab, n1, z1, m, dpg1, cot, gw1, x_in, g0, y0, n0, in_gain, out_gain, w_in, w_gate, w_out, dz_ref, dpg_ref, send_ref, rs, dp, xs, send):
    rs[...] = gab[...].astype(F32)
    dz = cot[...] + prepare_back(
        rs, z1[...], n1[...], column(in_gain[1:2]), w_in[1], w_gate[1], m[0:1], dpg1[...], dp
    )
    dz_ref[...] = dz
    w1 = [dot(n1[...], dp[128 * e : 128 * (e + 1), :], 1, 1) for e in range(4)]
    g = g0[...]
    dpg = (dz * y0[...] * g * (1.0 - g)).astype(BF16)
    dpg_ref[...] = dpg
    xs[...] = x_in[...].astype(F32)
    gx, gwo = finish_back(
        messages_to_channels(xs, 0, 2), dz * g, column(out_gain[0:1]), w_out[0]
    )
    gwg = dot(n0[...], dpg, 1, 1)
    channels_to_messages(gx, send, 0, 6)
    parts = w1 + [gw1[0:128, :], gw1[128:256, :], gwg, gwo]
    for k, part in enumerate(parts):
        send[pl.ds((k % 2) * 128 * 6 + 2 + k // 2, 128, stride=6), :] = part
    send_ref[...] = send[...].astype(BF16)


def end_kernel(gab, n0, z0, m, dpg0, dz1, in_gain, w_in, w_gate, grad_ref, send_ref, rs, dp, send):
    rs[...] = gab[...].astype(F32)
    dz = dz1[...] + prepare_back(
        rs, z0[...], n0[...], column(in_gain[0:1]), w_in[0], w_gate[0], m[0:1], dpg0[...], dp
    )
    grad_ref[...] = dz.T
    for e in range(4):
        send[pl.ds((e % 2) * 256 + e // 2, 128, stride=2), :] = dot(
            n0[...], dp[128 * e : 128 * (e + 1), :], 1, 1
        )
    send_ref[...] = send[...].astype(BF16)


def sum_kernel(recv, others, send_ref, rs, send):
    rs[...] = recv[...].astype(F32)
    for k in range(6):
        if k < 2:
            total = jnp.sum(rs[pl.ds(k, 256, stride=2), :], axis=0, keepdims=True)
        else:
            total = others[k - 2 : k - 1, :]
        send[pl.ds(k, 256, stride=6), :] = jnp.broadcast_to(total, (256, 128))
    send_ref[...] = send[...].astype(BF16)


def place_kernel(recv, in_ref, gate_ref, out_ref, rs):
    rs[...] = recv[...].astype(F32)
    rows = [rs[pl.ds(k, 256, stride=6), :] for k in range(6)]
    for u, base in ((0, 0), (1, 2)):
        for e in range(4):
            in_ref[u, :, 128 * e : 128 * (e + 1)] = rows[base + e // 2][
                128 * (e % 2) : 128 * (e % 2) + 128
            ]
    for u, k in ((0, 5), (1, 4)):
        gate_ref[u] = rows[k][0:128]
        out_ref[u] = rows[k][128:256]


def product_kernel(incoming, recv, a_ref, b_ref, send_ref, rs, mat, res, send):
    rs[...] = recv[...].astype(F32)
    messages_to_matrix(rs, 2, 4, mat)
    b = get(mat).astype(BF16)
    b_ref[...] = b
    messages_to_matrix(rs, 0, 4, mat)
    a = get(mat).astype(BF16)
    a_ref[...] = a
    if incoming:
        put(mat, dot(a, b, 0, 0))
        put(res, my_rows(mat))
    else:
        put(res, dot(my_rows(mat), b, 1, 1))
    half_to_messages(res, send, 0, 2)
    send_ref[...] = send[...].astype(BF16)


def product_back_kernel(incoming, w, recv, a_in, b_in, *refs):
    if w > 2:
        send_ref, sum_ref, rs, mat, res, send = refs
    else:
        send_ref, rs, mat, res, send = refs
    rs[...] = recv[...].astype(F32)
    messages_to_matrix(rs, 0, w, mat)
    gx = get(mat).astype(BF16)
    if incoming:
        put(mat, b_in[...].astype(F32))
        put(res, dot(my_rows(mat), gx, 1, 1))
    else:
        put(res, dot(my_rows(mat), b_in[...], 1, 0))
    half_to_messages(res, send, 0, 4)
    if incoming:
        put(mat, a_in[...].astype(F32))
        put(res, dot(my_rows(mat), gx, 1, 0))
    else:
        put(mat, dot(gx, a_in[...], 0, 0))
        put(res, my_rows(mat))
    half_to_messages(res, send, 2, 4)
    send_ref[...] = send[...].astype(BF16)
    if w > 2:
        sum_ref[...] = jnp.zeros((8, 128), F32)
        for k in range(2, w):
            sum_ref[k - 2 : k - 1, :] = jnp.sum(
                rs[pl.ds(k, 256, stride=w), :], axis=0, keepdims=True
            )


def call(kernel, name, outs, scratch, *args):
    return pl.pallas_call(
        kernel,
        name=name,
        out_shape=[jax.ShapeDtypeStruct(s, d) for s, d in outs],
        scratch_shapes=[pltpu.VMEM(s, d) for s, d in scratch],
        compiler_params=pltpu.CompilerParams(vmem_limit_bytes=24 * 1024 * 1024),
    )(*args)


def exchange(value, axes):
    return lax.all_to_all(value, axes, 0, 0, tiled=True)


def shards(pair, pair_cot, mask, chain_ids, chain_bias, w_in, w_gate, w_out, in_gain, out_gain):
    block = pair.shape
    pair = pair.reshape(POS, CH)
    cot_in = pair_cot.reshape(POS, CH)
    mask, chain, bias = mask[None, :], chain_ids[None, :], chain_bias[None, :]
    field, field16 = ((CH, POS), F32), ((CH, POS), BF16)
    matrix, matrix16, part = ((2, 256, 128), F32), ((256, 256), BF16), ((2, 128, 128), F32)

    def rows(n, dtype=F32):
        return ((n, 128), dtype)

    z0, n0, g0, m, send = call(
        start_kernel, "start", [field, field16, field, ((8, POS), F32), rows(1024, BF16)], [rows(1024)],
        pair, mask, chain, bias, in_gain, w_in, w_gate,
    )
    a0, b0, send = call(
        functools.partial(product_kernel, False), "outgoing", [matrix16, matrix16, rows(256, BF16)],
        [rows(1024), matrix, part, rows(256)], exchange(send, ALL),
    )
    x0 = exchange(send, CHIPS)
    z1, y0, n1, g1, send = call(
        middle_kernel, "middle", [field, field, field16, field, rows(1024, BF16)], [rows(256), rows(1024)],
        x0, z0, g0, m, in_gain, out_gain, w_in, w_gate, w_out,
    )
    a1, b1, send = call(
        functools.partial(product_kernel, True), "incoming", [matrix16, matrix16, rows(256, BF16)],
        [rows(1024), matrix, part, rows(256)], exchange(send, ALL),
    )
    new_pair, cot, dpg1, gw1, send = call(
        turn_kernel, "turn", [rows(POS, BF16), field, field16, rows(256), rows(512, BF16)],
        [rows(256), rows(512)], exchange(send, CHIPS), z1, g1, n1, cot_in, out_gain, w_out,
    )
    (send,) = call(
        functools.partial(product_back_kernel, True, 2), "incoming_back", [rows(512, BF16)],
        [rows(512), matrix, part, rows(512)], exchange(send, ALL), a1, b1,
    )
    dz1, dpg0, send = call(
        back_kernel, "back", [field, field16, rows(1536, BF16)],
        [rows(512), ((512, POS), BF16), rows(256), rows(1536)],
        exchange(send, CHIPS), n1, z1, m, dpg1, cot, gw1, x0, g0, y0, n0, in_gain, out_gain, w_in, w_gate, w_out,
    )
    send, sums = call(
        functools.partial(product_back_kernel, False, 6), "outgoing_back", [rows(512, BF16), rows(8)],
        [rows(1536), matrix, part, rows(512)], exchange(send, ALL), a0, b0,
    )
    pair_grad, send = call(
        end_kernel, "end", [rows(POS), rows(512, BF16)], [rows(512), ((512, POS), BF16), rows(512)],
        exchange(send, CHIPS), n0, z0, m, dpg0, dz1, in_gain, w_in, w_gate,
    )
    (send,) = call(
        sum_kernel, "sum", [rows(1536, BF16)], [rows(512), rows(1536)], exchange(send, ALL), sums
    )
    in_grad, gate_grad, out_grad = call(
        place_kernel, "place",
        [((2, 128, 512), F32), ((2, 128, 128), F32), ((2, 128, 128), F32)], [rows(1536)],
        exchange(send, ALL),
    )
    return (new_pair.reshape(block), pair_grad.reshape(block), in_grad, gate_grad, out_grad)


def solution(mesh):
    devices = mesh.devices.reshape(8, 2, 16)
    split = P(("g", "h"), "q", None)
    return jax.shard_map(
        shards,
        mesh=Mesh(devices, ALL),
        in_specs=(split, split) + (P(),) * 8,
        out_specs=(split, split, P(), P(), P()),
        check_vma=False,
    )
```

```python
import functools

import jax
import jax.numpy as jnp
from jax import lax
from jax.experimental import pallas as pl
from jax.experimental.pallas import tpu as pltpu
from jax.sharding import Mesh, PartitionSpec as P

F32 = jnp.float32
BF16 = jnp.bfloat16
POS = 256
CH = 128
EPS = 1e-05
CHIPS = ("g", "q")
ALL = ("g", "h", "q")


def dot(a, b, ca, cb):
    return lax.dot_general(
        a.astype(BF16), b.astype(BF16), (((ca,), (cb,)), ((), ())), preferred_element_type=F32
    )


def swap_blocks(tiles):
    block = lax.broadcasted_iota(jnp.int32, tiles[0].shape, 1) // 16
    for d in (1, 2, 4):
        high = (block & d) != 0
        out = list(tiles)
        for t in range(8):
            if t & d == 0:
                lo, hi = tiles[t], tiles[t | d]
                out[t] = jnp.where(high, pltpu.roll(hi, 16 * d, 1), lo)
                out[t | d] = jnp.where(high, hi, pltpu.roll(lo, 128 - 16 * d, 1))
        tiles = out
    return tiles


def messages_to_matrix(src, off, w, dst):
    for half in range(2):
        for qh in range(2):
            tiles = [
                src[pl.ds((qh * 8 + t) * w + off + half, 16, stride=16 * w), :] for t in range(8)
            ]
            for t, tile in enumerate(swap_blocks(tiles)):
                dst[qh, pl.ds(half * 8 + t, 16, stride=16), :] = tile


def half_to_messages(src, dst, off, w):
    for half in range(2):
        for qh in range(2):
            tiles = [src[qh, pl.ds(half * 8 + t, 8, stride=16), :] for t in range(8)]
            for t, tile in enumerate(swap_blocks(tiles)):
                dst[pl.ds((qh * 8 + t) * w + off + half, 8, stride=16 * w), :] = tile


def put(ref, value):
    for qh in range(2):
        ref[qh] = value[:, qh * 128 : (qh + 1) * 128]


def get(ref):
    return jnp.concatenate([ref[0], ref[1]], axis=1)


def my_rows(ref):
    h = lax.axis_index("h")
    return jnp.concatenate(
        [
            jnp.concatenate(
                [ref[qh, pl.ds(pl.multiple_of((2 * g + h) * 16, 16), 16), :] for g in range(8)],
                axis=0,
            )
            for qh in range(2)
        ],
        axis=1,
    )


def channels_to_messages(v, dst, off, w):
    for g in range(8):
        for h in range(2):
            for half in range(2):
                dst[pl.ds((g * 32 + h * 16) * w + off + half, 16, stride=w), :] = v[
                    g * 16 : (g + 1) * 16, half * 128 : (half + 1) * 128
                ]


def messages_to_channels(src, off, w):
    return jnp.concatenate(
        [src[pl.ds(off + half, CH, stride=w), :] for half in range(2)], axis=1
    )


def column(row):
    square = jnp.broadcast_to(row, (CH, CH)).T
    return jnp.concatenate([square, square], axis=1)


def normalise(z):
    centered = z - jnp.mean(z, axis=0, keepdims=True)
    rstd = lax.rsqrt(jnp.mean(centered * centered, axis=0, keepdims=True) + EPS)
    return centered * rstd, rstd


def normalise_back(cot, hat, rstd):
    return rstd * (
        cot
        - jnp.mean(cot, axis=0, keepdims=True)
        - hat * jnp.mean(cot * hat, axis=0, keepdims=True)
    )


def prepare(z, gain, w_in, w_gate, m, n_ref, g_ref, send, send_ref):
    hat, _ = normalise(z)
    normed = (hat * gain).astype(BF16)
    n_ref[...] = normed
    p = dot(w_in, normed, 0, 0)
    a = m * jax.nn.sigmoid(p[0:128]) * p[128:256]
    b = m * jax.nn.sigmoid(p[256:384]) * p[384:512]
    g_ref[...] = jax.nn.sigmoid(dot(w_gate, normed, 0, 0))
    channels_to_messages(a, send, 0, 4)
    channels_to_messages(b, send, 2, 4)
    send_ref[...] = send[...].astype(BF16)


def prepare_back(recv, w, z, normed, gain, w_in, w_gate, m, dpg, dp):
    p = dot(w_in, normed, 0, 0)
    for k in range(2):
        cot = messages_to_channels(recv, 2 * k, w) * m
        s = jax.nn.sigmoid(p[256 * k : 256 * k + 128])
        v = p[256 * k + 128 : 256 * k + 256]
        dp[256 * k : 256 * k + 128, :] = (cot * v * s * (1.0 - s)).astype(BF16)
        dp[256 * k + 128 : 256 * k + 256, :] = (cot * s).astype(BF16)
    dn = dot(w_in, dp[...], 1, 0) + dot(w_gate, dpg, 1, 0)
    hat, rstd = normalise(z)
    return normalise_back(dn * gain, hat, rstd)


def finish_back(x, dy, gain, w_out):
    hat, rstd = normalise(x)
    normed = (hat * gain).astype(BF16)
    gx = normalise_back(dot(w_out, dy, 1, 0) * gain, hat, rstd)
    return gx, dot(normed, dy, 1, 1)


def start_kernel(*refs):
    hbm, (z_ref, n_ref, g_ref, m_ref, gain_ref, send_ref), refs = refs[:8], refs[8:14], refs[14:]
    vmem, send, sem = refs[:8], refs[8], refs[9]
    copies = [
        pltpu.make_async_copy(src.at[0] if k > 5 else src, dst, sem.at[k])
        for k, (src, dst) in enumerate(zip(hbm, vmem))
    ]
    for copy in copies:
        copy.start()
    pair, mask, chain, bias, in_gain, out_gain, w_in, w_gate = vmem
    row = 2 * lax.axis_index("g") + lax.axis_index("h")
    col = lax.axis_index("q")
    res = lax.broadcasted_iota(jnp.int32, (256, POS), 0)
    pos = lax.broadcasted_iota(jnp.int32, (256, POS), 1)
    in_row = (res == row * 16 + pos // 16).astype(F32)
    in_col = (res == col * 16 + pos % 16).astype(F32)
    for copy in copies:
        copy.wait()
    both = jnp.concatenate(
        [
            jnp.broadcast_to(mask[...].astype(F32), (8, 256)),
            jnp.broadcast_to(chain[...].astype(F32), (8, 256)),
        ],
        axis=0,
    )
    of_row = dot(both, in_row, 1, 0)
    of_col = dot(both, in_col, 1, 0)
    m8 = of_row[0:8] * of_col[0:8]
    m_ref[...] = m8
    gain_ref[0:2, :] = in_gain[...]
    gain_ref[2:4, :] = out_gain[...]
    same = (of_row[8:9] == of_col[8:9]).astype(F32)
    z = pair[...].astype(F32).T + same * column(bias[...])
    z_ref[...] = z
    prepare(z, column(in_gain[0:1]), w_in[...], w_gate[...], m8[0:1], n_ref, g_ref, send, send_ref)


def middle_kernel(x_in, z0, g0, m, gains, w_in, w_gate, w_out, z_ref, y_ref, n_ref, g_ref, send_ref, xs, send):
    xs[...] = x_in[...].astype(F32)
    hat, _ = normalise(messages_to_channels(xs, 0, 2))
    y = dot(w_out[0], hat * column(gains[2:3]), 0, 0)
    y_ref[...] = y
    z = z0[...] + g0[...] * y
    z_ref[...] = z
    prepare(z, column(gains[1:2]), w_in[1], w_gate[1], m[0:1], n_ref, g_ref, send, send_ref)


def turn_kernel(x_in, z1, g1, n1, cot_in, gains, w_out, new_ref, cot_ref, dpg_ref, gw_ref, send_ref, xs, send):
    xs[...] = x_in[...].astype(F32)
    x = messages_to_channels(xs, 0, 2)
    gain = column(gains[3:4])
    hat, _ = normalise(x)
    y = dot(w_out[1], hat * gain, 0, 0)
    g = g1[...]
    new_ref[...] = (z1[...] + g * y).T.astype(BF16)
    cot = cot_in[...].astype(F32).T
    cot_ref[...] = cot
    gx, gwo = finish_back(x, cot * g, gain, w_out[1])
    dpg = (cot * y * g * (1.0 - g)).astype(BF16)
    dpg_ref[...] = dpg
    gw_ref[0:128, :] = dot(n1[...], dpg, 1, 1)
    gw_ref[128:256, :] = gwo
    channels_to_messages(gx, send, 0, 2)
    send_ref[...] = send[...].astype(BF16)


def back_kernel(gab, n1, z1, m, dpg1, cot, gw1, x_in, g0, y0, n0, gains, w_in, w_gate, w_out, dz_ref, dpg_ref, send_ref, mine_ref, other_ref, rs, dp, xs, send):
    rs[...] = gab[...].astype(F32)
    dz = cot[...] + prepare_back(
        rs, 4, z1[...], n1[...], column(gains[1:2]), w_in[1], w_gate[1], m[0:1], dpg1[...], dp
    )
    dz_ref[...] = dz
    w1 = [dot(n1[...], dp[128 * e : 128 * (e + 1), :], 1, 1) for e in range(4)]
    g = g0[...]
    dpg = (dz * y0[...] * g * (1.0 - g)).astype(BF16)
    dpg_ref[...] = dpg
    xs[...] = x_in[...].astype(F32)
    gx, gwo = finish_back(
        messages_to_channels(xs, 0, 2), dz * g, column(gains[2:3]), w_out[0]
    )
    gwg = dot(n0[...], dpg, 1, 1)
    channels_to_messages(gx, send, 0, 2)
    send_ref[...] = send[...].astype(BF16)
    h = lax.axis_index("h")
    late = [gw1[0:128, :], gw1[128:256, :], gwg, gwo]
    for k in range(4):
        block = slice(128 * k, 128 * (k + 1))
        mine_ref[block, :] = jnp.where(h == 0, w1[k], late[k])
        other_ref[block, :] = jnp.where(h == 0, late[k], w1[k]).astype(BF16)


def end_kernel(gab, n0, z0, m, dpg0, dz1, gains, w_in, w_gate, grad_ref, send_ref, sum_ref, rs, dp, send):
    rs[...] = gab[...].astype(F32)
    dz = dz1[...] + prepare_back(
        rs, 8, z0[...], n0[...], column(gains[0:1]), w_in[0], w_gate[0], m[0:1], dpg0[...], dp
    )
    grad_ref[...] = dz.T
    for e in range(4):
        part = dot(n0[...], dp[128 * e : 128 * (e + 1), :], 1, 1)
        h, k = e // 2, e % 2
        for g in range(8):
            send[pl.ds((g * 32 + h * 16) * 2 + k, 16, stride=2), :] = part[g * 16 : (g + 1) * 16]
    send_ref[...] = send[...].astype(BF16)
    sum_ref[...] = jnp.zeros((8, 128), F32)
    for k in range(4):
        sum_ref[k : k + 1, :] = jnp.sum(rs[pl.ds(4 + k, CH, stride=8), :], axis=0, keepdims=True)


def sum_kernel(recv, others, send_ref, rs, send):
    rs[...] = recv[...].astype(F32)
    for k in range(6):
        if k < 2:
            total = jnp.sum(rs[pl.ds(k, 256, stride=2), :], axis=0, keepdims=True)
        else:
            total = others[k - 2 : k - 1, :]
        send[pl.ds(k, CH, stride=6), :] = jnp.broadcast_to(total, (CH, 128))
    send_ref[...] = send[...].astype(BF16)


def place_kernel(mine, other, in_ref, gate_ref, out_ref, rs):
    h = lax.axis_index("h")
    here, there = mine[...].astype(F32), other[...].astype(F32)
    rs[0] = jnp.where(h == 0, here, there)
    rs[1] = jnp.where(h == 0, there, here)

    def block(core, k):
        return rs[core, pl.ds(k, CH, stride=6), :]

    for e in range(4):
        lanes = slice(128 * e, 128 * (e + 1))
        in_ref[0, :, lanes] = block(e // 2, e % 2)
        in_ref[1, :, lanes] = block(0, 2 + e)
    gate_ref[1] = block(1, 2)
    out_ref[1] = block(1, 3)
    gate_ref[0] = block(1, 4)
    out_ref[0] = block(1, 5)


def product_kernel(incoming, recv, a_ref, b_ref, send_ref, rs, mat, res, send):
    rs[...] = recv[...].astype(F32)
    messages_to_matrix(rs, 2, 4, mat)
    b = get(mat).astype(BF16)
    b_ref[...] = b
    messages_to_matrix(rs, 0, 4, mat)
    a = get(mat).astype(BF16)
    a_ref[...] = a
    if incoming:
        put(mat, dot(a, b, 0, 0))
        put(res, my_rows(mat))
    else:
        put(res, dot(my_rows(mat), b, 1, 1))
    half_to_messages(res, send, 0, 2)
    send_ref[...] = send[...].astype(BF16)


def product_back_kernel(incoming, recv, a_in, b_in, *refs):
    if incoming:
        w = 4
        send_ref, rs, mat, res, send = refs
    else:
        w = 8
        mine, other, send_ref, rs, mat, res, send = refs
        weights = mine[...] + other[...].astype(F32)
        for k in range(4):
            send[pl.ds(4 + k, CH, stride=w), :] = weights[128 * k : 128 * (k + 1)]
    rs[...] = recv[...].astype(F32)
    messages_to_matrix(rs, 0, 2, mat)
    gx = get(mat).astype(BF16)
    if incoming:
        put(mat, b_in[...].astype(F32))
        put(res, dot(my_rows(mat), gx, 1, 1))
    else:
        put(res, dot(my_rows(mat), b_in[...], 1, 0))
    half_to_messages(res, send, 0, w)
    if incoming:
        put(mat, a_in[...].astype(F32))
        put(res, dot(my_rows(mat), gx, 1, 0))
    else:
        put(mat, dot(gx, a_in[...], 0, 0))
        put(res, my_rows(mat))
    half_to_messages(res, send, 2, w)
    send_ref[...] = send[...].astype(BF16)


def call(kernel, name, outs, scratch, *args, **kwargs):
    return pl.pallas_call(
        kernel,
        name=name,
        out_shape=[jax.ShapeDtypeStruct(s, d) for s, d in outs],
        scratch_shapes=[s if not isinstance(s, tuple) else pltpu.VMEM(*s) for s in scratch],
        compiler_params=pltpu.CompilerParams(vmem_limit_bytes=24 * 1024 * 1024),
        **kwargs,
    )(*args)


def exchange(value, axes):
    return lax.all_to_all(value, axes, 0, 0, tiled=True)


def swap_cores(value):
    return lax.ppermute(value, "h", [(0, 1), (1, 0)])


def shards(pair, pair_cot, mask, chain_ids, chain_bias, w_in, w_gate, w_out, in_gain, out_gain):
    block = pair.shape
    pair = pair.reshape(POS, CH)
    cot_in = pair_cot.reshape(POS, CH)
    mask, chain, bias = mask[None, :], chain_ids[None, :], chain_bias[None, :]
    field, field16 = ((CH, POS), F32), ((CH, POS), BF16)
    matrix, matrix16, part = ((2, 256, 128), F32), ((256, 256), BF16), ((2, 128, 128), F32)

    def rows(n, dtype=F32):
        return ((n, 128), dtype)

    operands = (pair, mask, chain, bias, in_gain, out_gain, w_in, w_gate)
    z0, n0, g0, m, gains, send = call(
        start_kernel, "start", [field, field16, field, ((8, POS), F32), rows(4), rows(1024, BF16)],
        [(v.shape[1:] if k > 5 else v.shape, v.dtype) for k, v in enumerate(operands)]
        + [rows(1024), pltpu.SemaphoreType.DMA((8,))],
        *operands, in_specs=[pl.BlockSpec(memory_space=pltpu.HBM)] * 8,
    )
    a0, b0, send = call(
        functools.partial(product_kernel, False), "outgoing", [matrix16, matrix16, rows(256, BF16)],
        [rows(1024), matrix, part, rows(256)], exchange(send, ALL),
    )
    x0 = exchange(send, CHIPS)
    z1, y0, n1, g1, send = call(
        middle_kernel, "middle", [field, field, field16, field, rows(1024, BF16)], [rows(256), rows(1024)],
        x0, z0, g0, m, gains, w_in, w_gate, w_out,
    )
    a1, b1, send = call(
        functools.partial(product_kernel, True), "incoming", [matrix16, matrix16, rows(256, BF16)],
        [rows(1024), matrix, part, rows(256)], exchange(send, ALL),
    )
    new_pair, cot, dpg1, gw1, send = call(
        turn_kernel, "turn", [rows(POS, BF16), field, field16, rows(256), rows(512, BF16)],
        [rows(256), rows(512)], exchange(send, CHIPS), z1, g1, n1, cot_in, gains, w_out,
    )
    (send,) = call(
        functools.partial(product_back_kernel, True), "incoming_back", [rows(512, BF16)],
        [rows(512), matrix, part, rows(512)], exchange(send, ALL), a1, b1,
    )
    dz1, dpg0, send, mine, other = call(
        back_kernel, "back", [field, field16, rows(512, BF16), rows(512), rows(512, BF16)],
        [rows(512), ((512, POS), BF16), rows(256), rows(512)],
        exchange(send, CHIPS), n1, z1, m, dpg1, cot, gw1, x0, g0, y0, n0, gains, w_in, w_gate, w_out,
    )
    other = swap_cores(other)
    (send,) = call(
        functools.partial(product_back_kernel, False), "outgoing_back", [rows(1024, BF16)],
        [rows(512), matrix, part, rows(1024)], exchange(send, ALL), a0, b0, mine, other,
    )
    pair_grad, send, sums = call(
        end_kernel, "end", [rows(POS), rows(512, BF16), rows(8)],
        [rows(1024), ((512, POS), BF16), rows(512)],
        exchange(send, CHIPS), n0, z0, m, dpg0, dz1, gains, w_in, w_gate,
    )
    (send,) = call(
        sum_kernel, "sum", [rows(768, BF16)], [rows(512), rows(768)], exchange(send, ALL), sums
    )
    mine = exchange(send, CHIPS)
    in_grad, gate_grad, out_grad = call(
        place_kernel, "place",
        [((2, 128, 512), F32), ((2, 128, 128), F32), ((2, 128, 128), F32)], [((2, 768, 128), F32)],
        mine, swap_cores(mine),
    )
    return (new_pair.reshape(block), pair_grad.reshape(block), in_grad, gate_grad, out_grad)


def solution(mesh):
    devices = mesh.devices.reshape(8, 2, 16)
    split = P(("g", "h"), "q", None)
    return jax.shard_map(
        shards,
        mesh=Mesh(devices, ALL),
        in_specs=(split, split) + (P(),) * 8,
        out_specs=(split, split, P(), P(), P()),
        check_vma=False,
    )
```

```python
import functools

import jax
import jax.numpy as jnp
from jax import lax
from jax.experimental import pallas as pl
from jax.experimental.pallas import tpu as pltpu
from jax.sharding import Mesh, PartitionSpec as P

F32 = jnp.float32
BF16 = jnp.bfloat16
POS = 256
CH = 128
EPS = 1e-05
SIZES = {"y": 4, "zl": 2, "h": 2, "zh": 4, "x": 4}
CHIPS = ("y", "zl", "zh", "x")
PLANE = ("y", "h", "x")
LINE = ("zl", "zh")


def dot(a, b, ca, cb):
    return lax.dot_general(
        a.astype(BF16), b.astype(BF16), (((ca,), (cb,)), ((), ())), preferred_element_type=F32
    )


def swap_blocks(tiles):
    block = lax.broadcasted_iota(jnp.int32, tiles[0].shape, 1) // 16
    for d in (1, 2, 4):
        high = (block & d) != 0
        out = list(tiles)
        for t in range(8):
            if t & d == 0:
                lo, hi = tiles[t], tiles[t | d]
                out[t] = jnp.where(high, pltpu.roll(hi, 16 * d, 1), lo)
                out[t | d] = jnp.where(high, hi, pltpu.roll(lo, 128 - 16 * d, 1))
        tiles = out
    return tiles


def messages_to_matrix(mine, other, off, w, dst):
    first = lax.axis_index("h") == 0
    for half in range(2):
        for qh in range(2):
            even, odd = [], []
            for t in range(8):
                rows = pl.ds((qh * 8 + t) * w + off + half, 8, stride=16 * w)
                here, there = mine[rows, :], other[rows, :]
                even.append(jnp.where(first, here, there))
                odd.append(jnp.where(first, there, here))
            for core, tiles in enumerate((even, odd)):
                for t, tile in enumerate(swap_blocks(tiles)):
                    dst[qh, pl.ds(core * 16 + half * 8 + t, 8, stride=32), :] = tile


def half_to_messages(src, dst, off, w):
    for half in range(2):
        for qh in range(2):
            tiles = [src[qh, pl.ds(half * 8 + t, 8, stride=16), :] for t in range(8)]
            for t, tile in enumerate(swap_blocks(tiles)):
                dst[pl.ds((qh * 8 + t) * w + off + half, 8, stride=16 * w), :] = tile


def put(ref, value):
    for qh in range(2):
        ref[qh] = value[:, qh * 128 : (qh + 1) * 128]


def get(ref):
    return jnp.concatenate([ref[0], ref[1]], axis=1)


def my_rows(ref):
    h = lax.axis_index("h")
    return jnp.concatenate(
        [
            jnp.concatenate(
                [ref[qh, pl.ds(pl.multiple_of((2 * g + h) * 16, 16), 16), :] for g in range(8)],
                axis=0,
            )
            for qh in range(2)
        ],
        axis=1,
    )


def channels_to_messages(v, dst, off, w):
    for half in range(2):
        dst[pl.ds(off + half, CH, stride=w), :] = v[:, half * 128 : (half + 1) * 128]


def messages_to_channels(src, off, w):
    return jnp.concatenate(
        [src[pl.ds(off + half, CH, stride=w), :] for half in range(2)], axis=1
    )


def column(row):
    square = jnp.broadcast_to(row, (CH, CH)).T
    return jnp.concatenate([square, square], axis=1)


def normalise(z):
    centered = z - jnp.mean(z, axis=0, keepdims=True)
    rstd = lax.rsqrt(jnp.mean(centered * centered, axis=0, keepdims=True) + EPS)
    return centered * rstd, rstd


def normalise_back(cot, hat, rstd):
    return rstd * (
        cot
        - jnp.mean(cot, axis=0, keepdims=True)
        - hat * jnp.mean(cot * hat, axis=0, keepdims=True)
    )


def prepare(z, gain, w_in, w_gate, m, n_ref, g_ref, send, send_ref):
    hat, _ = normalise(z)
    normed = (hat * gain).astype(BF16)
    n_ref[...] = normed
    p = dot(w_in, normed, 0, 0)
    a = m * jax.nn.sigmoid(p[0:128]) * p[128:256]
    b = m * jax.nn.sigmoid(p[256:384]) * p[384:512]
    g_ref[...] = jax.nn.sigmoid(dot(w_gate, normed, 0, 0))
    channels_to_messages(a, send, 0, 4)
    channels_to_messages(b, send, 2, 4)
    send_ref[...] = send[...].astype(BF16)


def prepare_back(recv, z, normed, gain, w_in, w_gate, m, dpg, dp):
    p = dot(w_in, normed, 0, 0)
    for k in range(2):
        cot = messages_to_channels(recv, 2 * k, 4) * m
        s = jax.nn.sigmoid(p[256 * k : 256 * k + 128])
        v = p[256 * k + 128 : 256 * k + 256]
        dp[256 * k : 256 * k + 128, :] = (cot * v * s * (1.0 - s)).astype(BF16)
        dp[256 * k + 128 : 256 * k + 256, :] = (cot * s).astype(BF16)
    dn = dot(w_in, dp[...], 1, 0) + dot(w_gate, dpg, 1, 0)
    hat, rstd = normalise(z)
    return normalise_back(dn * gain, hat, rstd)


def finish_back(x, dy, gain, w_out):
    hat, rstd = normalise(x)
    normed = (hat * gain).astype(BF16)
    gx = normalise_back(dot(w_out, dy, 1, 0) * gain, hat, rstd)
    return gx, dot(normed, dy, 1, 1)


def start_kernel(*refs):
    hbm, (z_ref, n_ref, g_ref, m_ref, gain_ref, send_ref), refs = refs[:8], refs[8:14], refs[14:]
    vmem, send, sem = refs[:8], refs[8], refs[9]
    copies = [
        pltpu.make_async_copy(src.at[0] if k > 5 else src, dst, sem.at[k])
        for k, (src, dst) in enumerate(zip(hbm, vmem))
    ]
    for copy in copies:
        copy.start()
    pair, mask, chain, bias, in_gain, out_gain, w_in, w_gate = vmem
    row = (lax.axis_index("y") * 2 + lax.axis_index("zl")) * 2 + lax.axis_index("h")
    col = lax.axis_index("zh") * 4 + lax.axis_index("x")
    res = lax.broadcasted_iota(jnp.int32, (256, POS), 0)
    pos = lax.broadcasted_iota(jnp.int32, (256, POS), 1)
    in_row = (res == row * 16 + pos // 16).astype(F32)
    in_col = (res == col * 16 + pos % 16).astype(F32)
    for copy in copies:
        copy.wait()
    both = jnp.concatenate(
        [
            jnp.broadcast_to(mask[...].astype(F32), (8, 256)),
            jnp.broadcast_to(chain[...].astype(F32), (8, 256)),
        ],
        axis=0,
    )
    of_row = dot(both, in_row, 1, 0)
    of_col = dot(both, in_col, 1, 0)
    m8 = of_row[0:8] * of_col[0:8]
    m_ref[...] = m8
    gain_ref[0:2, :] = in_gain[...]
    gain_ref[2:4, :] = out_gain[...]
    same = (of_row[8:9] == of_col[8:9]).astype(F32)
    z = pair[...].astype(F32).T + same * column(bias[...])
    z_ref[...] = z
    prepare(z, column(in_gain[0:1]), w_in[...], w_gate[...], m8[0:1], n_ref, g_ref, send, send_ref)


def middle_kernel(x_in, z0, g0, m, gains, w_in, w_gate, w_out, z_ref, y_ref, n_ref, g_ref, send_ref, xs, send):
    xs[...] = x_in[...].astype(F32)
    hat, _ = normalise(messages_to_channels(xs, 0, 2))
    y = dot(w_out[0], hat * column(gains[2:3]), 0, 0)
    y_ref[...] = y
    z = z0[...] + g0[...] * y
    z_ref[...] = z
    prepare(z, column(gains[1:2]), w_in[1], w_gate[1], m[0:1], n_ref, g_ref, send, send_ref)


def turn_kernel(x_in, z1, g1, n1, cot_in, gains, w_out, new_ref, cot_ref, dpg_ref, gw_ref, send_ref, xs, send):
    xs[...] = x_in[...].astype(F32)
    x = messages_to_channels(xs, 0, 2)
    gain = column(gains[3:4])
    hat, _ = normalise(x)
    y = dot(w_out[1], hat * gain, 0, 0)
    g = g1[...]
    new_ref[...] = (z1[...] + g * y).T.astype(BF16)
    cot = cot_in[...].astype(F32).T
    cot_ref[...] = cot
    gx, gwo = finish_back(x, cot * g, gain, w_out[1])
    dpg = (cot * y * g * (1.0 - g)).astype(BF16)
    dpg_ref[...] = dpg
    gw_ref[0:128, :] = dot(n1[...], dpg, 1, 1)
    gw_ref[128:256, :] = gwo
    channels_to_messages(gx, send, 0, 2)
    send_ref[...] = send[...].astype(BF16)


def back_kernel(gab, n1, z1, m, dpg1, cot, gw1, x_in, g0, y0, n0, gains, w_in, w_gate, w_out, dz_ref, dpg_ref, send_ref, early_ref, rs, dp, xs, send):
    rs[...] = gab[...].astype(F32)
    dz = cot[...] + prepare_back(
        rs, z1[...], n1[...], column(gains[1:2]), w_in[1], w_gate[1], m[0:1], dpg1[...], dp
    )
    dz_ref[...] = dz
    w1 = [dot(n1[...], dp[128 * e : 128 * (e + 1), :], 1, 1) for e in range(4)]
    g = g0[...]
    dpg = (dz * y0[...] * g * (1.0 - g)).astype(BF16)
    dpg_ref[...] = dpg
    xs[...] = x_in[...].astype(F32)
    gx, gwo = finish_back(
        messages_to_channels(xs, 0, 2), dz * g, column(gains[2:3]), w_out[0]
    )
    gwg = dot(n0[...], dpg, 1, 1)
    channels_to_messages(gx, send, 0, 2)
    send_ref[...] = send[...].astype(BF16)
    for k, part in enumerate(w1 + [gw1[0:128, :], gw1[128:256, :], gwg, gwo]):
        early_ref[128 * k : 128 * (k + 1), :] = part.astype(BF16)


def end_kernel(gab, n0, z0, m, dpg0, dz1, gains, w_in, w_gate, early, grad_ref, send_ref, rs, dp):
    rs[...] = gab[...].astype(F32)
    dz = dz1[...] + prepare_back(
        rs, z0[...], n0[...], column(gains[0:1]), w_in[0], w_gate[0], m[0:1], dpg0[...], dp
    )
    grad_ref[...] = dz.T
    for e in range(4):
        part = dot(n0[...], dp[128 * e : 128 * (e + 1), :], 1, 1)
        send_ref[128 * e : 128 * (e + 1), :] = part.astype(BF16)
    send_ref[512:1536, :] = early[...]


def sum_kernel(recv, send_ref):
    total = recv[0:48, :].astype(F32)
    for k in range(1, recv.shape[0] // 48):
        total = total + recv[48 * k : 48 * (k + 1), :].astype(F32)
    total = total.astype(BF16)
    for k in range(send_ref.shape[0] // 48):
        send_ref[48 * k : 48 * (k + 1), :] = total


def place_kernel(recv, in_ref, gate_ref, out_ref):
    def block(k):
        return recv[128 * k : 128 * (k + 1), :].astype(F32)

    for e in range(4):
        lanes = slice(128 * e, 128 * (e + 1))
        in_ref[0, :, lanes] = block(e)
        in_ref[1, :, lanes] = block(4 + e)
    for k, (ref, u) in enumerate(((gate_ref, 1), (out_ref, 1), (gate_ref, 0), (out_ref, 0))):
        ref[u] = block(8 + k)


def product_kernel(incoming, mine, other, a_ref, b_ref, send_ref, ms, os, mat, res, send):
    ms[...] = mine[...].astype(F32)
    os[...] = other[...].astype(F32)
    messages_to_matrix(ms, os, 2, 4, mat)
    b = get(mat).astype(BF16)
    b_ref[...] = b
    messages_to_matrix(ms, os, 0, 4, mat)
    a = get(mat).astype(BF16)
    a_ref[...] = a
    if incoming:
        put(mat, dot(a, b, 0, 0))
        put(res, my_rows(mat))
    else:
        put(res, dot(my_rows(mat), b, 1, 1))
    half_to_messages(res, send, 0, 2)
    send_ref[...] = send[...].astype(BF16)


def product_back_kernel(incoming, mine, other, a_in, b_in, send_ref, ms, os, mat, res, send):
    ms[...] = mine[...].astype(F32)
    os[...] = other[...].astype(F32)
    messages_to_matrix(ms, os, 0, 2, mat)
    gx = get(mat).astype(BF16)
    if incoming:
        put(mat, b_in[...].astype(F32))
        put(res, dot(my_rows(mat), gx, 1, 1))
    else:
        put(res, dot(my_rows(mat), b_in[...], 1, 0))
    half_to_messages(res, send, 0, 4)
    if incoming:
        put(mat, a_in[...].astype(F32))
        put(res, dot(my_rows(mat), gx, 1, 0))
    else:
        put(mat, dot(gx, a_in[...], 0, 0))
        put(res, my_rows(mat))
    half_to_messages(res, send, 2, 4)
    send_ref[...] = send[...].astype(BF16)


def call(kernel, name, outs, scratch, *args, **kwargs):
    return pl.pallas_call(
        kernel,
        name=name,
        out_shape=[jax.ShapeDtypeStruct(s, d) for s, d in outs],
        scratch_shapes=[s if not isinstance(s, tuple) else pltpu.VMEM(*s) for s in scratch],
        compiler_params=pltpu.CompilerParams(vmem_limit_bytes=24 * 1024 * 1024),
        **kwargs,
    )(*args)


def exchange(value, axes=CHIPS):
    return lax.all_to_all(value, axes, 0, 0, tiled=True)


def swap_cores(value):
    return lax.ppermute(value, "h", [(0, 1), (1, 0)])


def exchange_both(value):
    mine = exchange(value)
    return mine, swap_cores(mine)


def shards(pair, pair_cot, mask, chain_ids, chain_bias, w_in, w_gate, w_out, in_gain, out_gain):
    block = pair.shape
    pair = pair.reshape(POS, CH)
    cot_in = pair_cot.reshape(POS, CH)
    mask, chain, bias = mask[None, :], chain_ids[None, :], chain_bias[None, :]
    field, field16 = ((CH, POS), F32), ((CH, POS), BF16)
    matrix, matrix16, part = ((2, 256, 128), F32), ((256, 256), BF16), ((2, 128, 128), F32)

    def rows(n, dtype=F32):
        return ((n, 128), dtype)

    operands = (pair, mask, chain, bias, in_gain, out_gain, w_in, w_gate)
    z0, n0, g0, m, gains, send = call(
        start_kernel, "start", [field, field16, field, ((8, POS), F32), rows(4), rows(512, BF16)],
        [(v.shape[1:] if k > 5 else v.shape, v.dtype) for k, v in enumerate(operands)]
        + [rows(512), pltpu.SemaphoreType.DMA((8,))],
        *operands, in_specs=[pl.BlockSpec(memory_space=pltpu.HBM)] * 8,
    )
    a0, b0, send = call(
        functools.partial(product_kernel, False), "outgoing", [matrix16, matrix16, rows(256, BF16)],
        [rows(512), rows(512), matrix, part, rows(256)], *exchange_both(send),
    )
    x0 = exchange(send)
    z1, y0, n1, g1, send = call(
        middle_kernel, "middle", [field, field, field16, field, rows(512, BF16)], [rows(256), rows(512)],
        x0, z0, g0, m, gains, w_in, w_gate, w_out,
    )
    a1, b1, send = call(
        functools.partial(product_kernel, True), "incoming", [matrix16, matrix16, rows(256, BF16)],
        [rows(512), rows(512), matrix, part, rows(256)], *exchange_both(send),
    )
    new_pair, cot, dpg1, gw1, send = call(
        turn_kernel, "turn", [rows(POS, BF16), field, field16, rows(256), rows(256, BF16)],
        [rows(256), rows(256)], exchange(send), z1, g1, n1, cot_in, gains, w_out,
    )
    (send,) = call(
        functools.partial(product_back_kernel, True), "incoming_back", [rows(512, BF16)],
        [rows(256), rows(256), matrix, part, rows(512)], *exchange_both(send), a1, b1,
    )
    dz1, dpg0, send, early = call(
        back_kernel, "back", [field, field16, rows(256, BF16), rows(1024, BF16)],
        [rows(512), ((512, POS), BF16), rows(256), rows(256)],
        exchange(send), n1, z1, m, dpg1, cot, gw1, x0, g0, y0, n0, gains, w_in, w_gate, w_out,
    )
    (send,) = call(
        functools.partial(product_back_kernel, False), "outgoing_back", [rows(512, BF16)],
        [rows(256), rows(256), matrix, part, rows(512)], *exchange_both(send), a0, b0,
    )
    pair_grad, send = call(
        end_kernel, "end", [rows(POS), rows(1536, BF16)], [rows(512), ((512, POS), BF16)],
        exchange(send), n0, z0, m, dpg0, dz1, gains, w_in, w_gate, early,
    )
    (send,) = call(sum_kernel, "plane_sum", [rows(384, BF16)], [], exchange(send, PLANE))
    (send,) = call(sum_kernel, "line_sum", [rows(1536, BF16)], [], exchange(send, LINE))
    in_grad, gate_grad, out_grad = call(
        place_kernel, "place",
        [((2, 128, 512), F32), ((2, 128, 128), F32), ((2, 128, 128), F32)], [], exchange(send, PLANE),
    )
    return (new_pair.reshape(block), pair_grad.reshape(block), in_grad, gate_grad, out_grad)


def solution(mesh):
    devices = mesh.devices.reshape(tuple(SIZES.values()))
    split = P(("y", "zl", "h"), ("zh", "x"), None)
    return jax.shard_map(
        shards,
        mesh=Mesh(devices, tuple(SIZES)),
        in_specs=(split, split) + (P(),) * 8,
        out_specs=(split, split, P(), P(), P()),
        check_vma=False,
    )
```

```python
import functools

import jax
import jax.numpy as jnp
from jax import lax
from jax.experimental import pallas as pl
from jax.experimental.pallas import tpu as pltpu
from jax.sharding import Mesh, PartitionSpec as P

F32 = jnp.float32
BF16 = jnp.bfloat16
POS = 256
CH = 128
EPS = 1e-05
SIZES = {"y": 4, "zl": 2, "h": 2, "zh": 4, "x": 4}
CHIPS = ("zh", "x", "y", "zl")
PLANE = ("h", "x", "y")
LINE = ("zl", "zh")


def dot(a, b, ca, cb):
    return lax.dot_general(
        a.astype(BF16), b.astype(BF16), (((ca,), (cb,)), ((), ())), preferred_element_type=F32
    )


def swap_blocks(tiles):
    block = lax.broadcasted_iota(jnp.int32, tiles[0].shape, 1) // 16
    for d in (1, 2, 4):
        high = (block & d) != 0
        out = list(tiles)
        for t in range(8):
            if t & d == 0:
                lo, hi = tiles[t], tiles[t | d]
                out[t] = jnp.where(high, pltpu.roll(hi, 16 * d, 1), lo)
                out[t | d] = jnp.where(high, hi, pltpu.roll(lo, 128 - 16 * d, 1))
        tiles = out
    return tiles


def messages_to_half(src, off, w, dst):
    for half in range(2):
        for p in range(2):
            tiles = [
                src[pl.ds((2 * t + p) * 8 * w + off + half, 8, stride=w), :] for t in range(8)
            ]
            for t, tile in enumerate(swap_blocks(tiles)):
                dst[p, pl.ds(half * 8 + t, 8, stride=16), :] = tile
    return jnp.concatenate([dst[0], dst[1]], axis=1).astype(BF16)


def half_to_messages(value, src, dst, off, w):
    for p in range(2):
        src[p] = value[p]
    for half in range(2):
        for p in range(2):
            tiles = [src[p, pl.ds(half * 8 + t, 8, stride=16), :] for t in range(8)]
            for t, tile in enumerate(swap_blocks(tiles)):
                dst[pl.ds((2 * t + p) * 8 * w + off + half, 8, stride=w), :] = tile


def halves(value):
    return value[:, 0:128], value[:, 128:256]


def by_parity(mine, other):
    first = lax.axis_index("h") == 0
    return jnp.where(first, mine, other), jnp.where(first, other, mine)


def own_columns(value):
    return by_parity(*halves(value))[0]


def other_columns(value):
    return by_parity(*halves(value))[1]


def channels_to_messages(v, dst, off, w):
    for half in range(2):
        dst[pl.ds(off + half, CH, stride=w), :] = v[:, half * 128 : (half + 1) * 128]


def messages_to_channels(src, off, w):
    return jnp.concatenate(
        [src[pl.ds(off + half, CH, stride=w), :] for half in range(2)], axis=1
    )


def column(row):
    square = jnp.broadcast_to(row, (CH, CH)).T
    return jnp.concatenate([square, square], axis=1)


def normalise(z):
    centered = z - jnp.mean(z, axis=0, keepdims=True)
    rstd = lax.rsqrt(jnp.mean(centered * centered, axis=0, keepdims=True) + EPS)
    return centered * rstd, rstd


def normalise_back(cot, hat, rstd):
    return rstd * (
        cot
        - jnp.mean(cot, axis=0, keepdims=True)
        - hat * jnp.mean(cot * hat, axis=0, keepdims=True)
    )


def prepare(z, gain, w_in, w_gate, m, n_ref, g_ref, send, send_ref, copies=()):
    hat, _ = normalise(z)
    normed = (hat * gain).astype(BF16)
    n_ref[...] = normed
    for copy in copies:
        copy.wait()
    p = dot(w_in[...], normed, 0, 0)
    a = m * jax.nn.sigmoid(p[0:128]) * p[128:256]
    b = m * jax.nn.sigmoid(p[256:384]) * p[384:512]
    g_ref[...] = jax.nn.sigmoid(dot(w_gate[...], normed, 0, 0))
    channels_to_messages(a, send, 0, 4)
    channels_to_messages(b, send, 2, 4)
    send_ref[...] = send[...].astype(BF16)


def prepare_back(recv, z, normed, gain, w_in, w_gate, m, dpg, dp):
    p = dot(w_in, normed, 0, 0)
    for k in range(2):
        cot = messages_to_channels(recv, 2 * k, 4) * m
        s = jax.nn.sigmoid(p[256 * k : 256 * k + 128])
        v = p[256 * k + 128 : 256 * k + 256]
        dp[256 * k : 256 * k + 128, :] = (cot * v * s * (1.0 - s)).astype(BF16)
        dp[256 * k + 128 : 256 * k + 256, :] = (cot * s).astype(BF16)
    dn = dot(w_in, dp[...], 1, 0) + dot(w_gate, dpg, 1, 0)
    hat, rstd = normalise(z)
    return normalise_back(dn * gain, hat, rstd)


def start_kernel(*refs):
    hbm, (z_ref, n_ref, g_ref, m_ref, gain_ref, send_ref), refs = refs[:8], refs[8:14], refs[14:]
    vmem, send, sem = refs[:8], refs[8], refs[9]
    copies = [
        pltpu.make_async_copy(src.at[0] if k > 5 else src, dst, sem.at[k])
        for k, (src, dst) in enumerate(zip(hbm, vmem))
    ]
    for copy in copies:
        copy.start()
    pair, mask, chain, bias, in_gain, out_gain, w_in, w_gate = vmem
    row = (lax.axis_index("y") * 2 + lax.axis_index("zl")) * 2 + lax.axis_index("h")
    col = lax.axis_index("zh") * 4 + lax.axis_index("x")
    res = lax.broadcasted_iota(jnp.int32, (256, POS), 0)
    pos = lax.broadcasted_iota(jnp.int32, (256, POS), 1)
    in_row = (res == row * 16 + pos // 16).astype(F32)
    in_col = (res == col * 16 + pos % 16).astype(F32)
    for copy in copies[:6]:
        copy.wait()
    both = jnp.concatenate(
        [
            jnp.broadcast_to(mask[...].astype(F32), (8, 256)),
            jnp.broadcast_to(chain[...].astype(F32), (8, 256)),
        ],
        axis=0,
    )
    of_row = dot(both, in_row, 1, 0)
    of_col = dot(both, in_col, 1, 0)
    m8 = of_row[0:8] * of_col[0:8]
    m_ref[...] = m8
    gain_ref[0:2, :] = in_gain[...]
    gain_ref[2:4, :] = out_gain[...]
    same = (of_row[8:9] == of_col[8:9]).astype(F32)
    z = pair[...].astype(F32).T + same * column(bias[...])
    z_ref[...] = z
    gain = column(in_gain[0:1])
    prepare(z, gain, w_in, w_gate, m8[0:1], n_ref, g_ref, send, send_ref, copies[6:])


def middle_kernel(x_in, z0, g0, m, gains, w_in, w_gate, w_out, z_ref, y_ref, n_ref, g_ref, send_ref, xs, send):
    xs[...] = x_in[...].astype(F32)
    hat, _ = normalise(messages_to_channels(xs, 0, 2))
    y = dot(w_out[0], hat * column(gains[2:3]), 0, 0)
    y_ref[...] = y
    z = z0[...] + g0[...] * y
    z_ref[...] = z
    prepare(z, column(gains[1:2]), w_in.at[1], w_gate.at[1], m[0:1], n_ref, g_ref, send, send_ref)


def turn_kernel(x_in, g1, cot_in, gains, w_out, cot_ref, y_ref, xn_ref, dy_ref, dpg_ref, send_ref, xs, send):
    xs[...] = x_in[...].astype(F32)
    gain = column(gains[3:4])
    hat, rstd = normalise(messages_to_channels(xs, 0, 2))
    xn = (hat * gain).astype(BF16)
    xn_ref[...] = xn
    y = dot(w_out[1], xn, 0, 0)
    y_ref[...] = y
    g = g1[...]
    cot = cot_in[...].astype(F32).T
    cot_ref[...] = cot
    dy = (cot * g).astype(BF16)
    dy_ref[...] = dy
    dpg_ref[...] = (cot * y * g * (1.0 - g)).astype(BF16)
    gx = normalise_back(dot(w_out[1], dy, 1, 0) * gain, hat, rstd)
    channels_to_messages(gx, send, 0, 2)
    send_ref[...] = send[...].astype(BF16)


def turn_rest_kernel(z1, y1, g1, n1, xn, dy, dpg, new_ref, gw_ref):
    new_ref[...] = (z1[...] + g1[...] * y1[...]).T.astype(BF16)
    gw_ref[0:128, :] = dot(n1[...], dpg[...], 1, 1).astype(BF16)
    gw_ref[128:256, :] = dot(xn[...], dy[...], 1, 1).astype(BF16)


def back_kernel(gab, n1, z1, m, dpg1, cot, x_in, g0, y0, gains, w_in, w_gate, w_out, dz_ref, dp_ref, dpg_ref, xn_ref, dy_ref, send_ref, rs, xs, send):
    rs[...] = gab[...].astype(F32)
    dz = cot[...] + prepare_back(
        rs, z1[...], n1[...], column(gains[1:2]), w_in[1], w_gate[1], m[0:1], dpg1[...], dp_ref
    )
    dz_ref[...] = dz
    g = g0[...]
    dpg_ref[...] = (dz * y0[...] * g * (1.0 - g)).astype(BF16)
    dy = (dz * g).astype(BF16)
    dy_ref[...] = dy
    xs[...] = x_in[...].astype(F32)
    gain = column(gains[2:3])
    hat, rstd = normalise(messages_to_channels(xs, 0, 2))
    xn_ref[...] = (hat * gain).astype(BF16)
    gx = normalise_back(dot(w_out[0], dy, 1, 0) * gain, hat, rstd)
    channels_to_messages(gx, send, 0, 2)
    send_ref[...] = send[...].astype(BF16)


def back_rest_kernel(n1, dp1, gw1, n0, dpg0, xn, dy, early_ref):
    for e in range(4):
        block = slice(128 * e, 128 * (e + 1))
        early_ref[block, :] = dot(n1[...], dp1[block, :], 1, 1).astype(BF16)
    early_ref[512:768, :] = gw1[...]
    early_ref[768:896, :] = dot(n0[...], dpg0[...], 1, 1).astype(BF16)
    early_ref[896:1024, :] = dot(xn[...], dy[...], 1, 1).astype(BF16)


def end_kernel(gab, n0, z0, m, dpg0, dz1, gains, w_in, w_gate, early, grad_ref, send_ref, rs, dp):
    rs[...] = gab[...].astype(F32)
    dz = dz1[...] + prepare_back(
        rs, z0[...], n0[...], column(gains[0:1]), w_in[0], w_gate[0], m[0:1], dpg0[...], dp
    )
    grad_ref[...] = dz.T
    for e in range(4):
        part = dot(n0[...], dp[128 * e : 128 * (e + 1), :], 1, 1)
        send_ref[128 * e : 128 * (e + 1), :] = part.astype(BF16)
    send_ref[512:1536, :] = early[...]


def sum_kernel(recv, send_ref):
    total = recv[0:48, :].astype(F32)
    for k in range(1, recv.shape[0] // 48):
        total = total + recv[48 * k : 48 * (k + 1), :].astype(F32)
    total = total.astype(BF16)
    for k in range(send_ref.shape[0] // 48):
        send_ref[48 * k : 48 * (k + 1), :] = total


def place_kernel(recv, grad, in_out, gate_out, out_out, grad_out, in_ref, gate_ref, out_ref, sem):
    copies = []

    def write(src, dst):
        copies.append(pltpu.make_async_copy(src, dst, sem.at[len(copies)]))
        copies[-1].start()

    def block(k):
        return recv[128 * k : 128 * (k + 1), :].astype(F32)

    write(grad, grad_out)
    for u in range(2):
        for e in range(4):
            in_ref[u, :, 128 * e : 128 * (e + 1)] = block(4 * u + e)
        write(in_ref.at[u], in_out.at[u])
    for k, u in ((8, 1), (10, 0)):
        gate_ref[u] = block(k)
        out_ref[u] = block(k + 1)
    write(gate_ref, gate_out)
    write(out_ref, out_out)
    for copy in copies:
        copy.wait()


def outgoing_mine_kernel(mine, a_ref, b_ref, x_ref, ms, mat):
    ms[...] = mine[...].astype(F32)
    a, b = messages_to_half(ms, 0, 4, mat), messages_to_half(ms, 2, 4, mat)
    a_ref[...] = a
    b_ref[...] = b
    x_ref[...] = dot(a, b, 1, 1)


def outgoing_kernel(other, a, x_mine, b_ref, send_ref, os, mat, send):
    os[...] = other[...].astype(F32)
    b = messages_to_half(os, 2, 4, mat)
    b_ref[...] = b
    half_to_messages(by_parity(x_mine[...], dot(a[...], b, 1, 1)), mat, send, 0, 2)
    send_ref[...] = send[...].astype(BF16)


def incoming_mine_kernel(mine, a_ref, b_ref, x_ref, ms, mat):
    ms[...] = mine[...].astype(F32)
    a, b = messages_to_half(ms, 0, 4, mat), messages_to_half(ms, 2, 4, mat)
    a_ref[...] = a
    b_ref[...] = b
    x_ref[...] = dot(own_columns(a), b, 0, 0)


def incoming_kernel(other, x_mine, send_ref, os, mat, send):
    os[...] = other[...].astype(F32)
    a, b = messages_to_half(os, 0, 4, mat), messages_to_half(os, 2, 4, mat)
    half_to_messages(halves(x_mine[...] + dot(own_columns(a), b, 0, 0)), mat, send, 0, 2)
    send_ref[...] = send[...].astype(BF16)


def incoming_back_mine_kernel(mine, a, b, ga_ref, gb_ref, ms, mat):
    ms[...] = mine[...].astype(F32)
    gx = messages_to_half(ms, 0, 2, mat)
    ga_ref[...] = dot(b[...], gx, 1, 1)
    gb_ref[...] = dot(own_columns(a[...]), gx, 1, 0)


def incoming_back_kernel(other, a, b, ga_mine, gb_mine, send_ref, os, mat, send):
    os[...] = other[...].astype(F32)
    gx = messages_to_half(os, 0, 2, mat)
    half_to_messages(by_parity(ga_mine[...], dot(b[...], gx, 1, 1)), mat, send, 0, 4)
    gb = gb_mine[...] + dot(other_columns(a[...]), gx, 1, 0)
    half_to_messages(halves(gb), mat, send, 2, 4)
    send_ref[...] = send[...].astype(BF16)


def other_rows_kernel(other_ab, a_ref, os, mat):
    os[...] = other_ab[...].astype(F32)
    a_ref[...] = messages_to_half(os, 0, 4, mat)


def outgoing_back_mine_kernel(mine, a, b, b_other, ga_ref, gb_ref, ms, mat, send):
    ms[...] = mine[...].astype(F32)
    gx = messages_to_half(ms, 0, 2, mat)
    even, odd = by_parity(b[...], b_other[...])
    ga = dot(gx, jnp.concatenate([even, odd], axis=0), 1, 0)
    half_to_messages(halves(ga), mat, send, 0, 2)
    ga_ref[...] = send[...]
    gb_ref[...] = dot(own_columns(gx), a[...], 0, 0)


def outgoing_back_kernel(other, ga, gb_mine, a_other, send_ref, os, mat, send):
    os[...] = other[...].astype(F32)
    gx = messages_to_half(os, 0, 2, mat)
    gb = gb_mine[...] + dot(own_columns(gx), a_other[...], 0, 0)
    half_to_messages(halves(gb), mat, send, 2, 4)
    for half in range(2):
        send[pl.ds(half, CH, stride=4), :] = ga[pl.ds(half, CH, stride=2), :]
    send_ref[...] = send[...].astype(BF16)


def call(kernel, name, outs, scratch, *args, **kwargs):
    return pl.pallas_call(
        kernel,
        name=name,
        out_shape=[jax.ShapeDtypeStruct(s, d) for s, d in outs],
        scratch_shapes=[s if not isinstance(s, tuple) else pltpu.VMEM(*s) for s in scratch],
        compiler_params=pltpu.CompilerParams(vmem_limit_bytes=24 * 1024 * 1024),
        cost_estimate=pl.CostEstimate(flops=2**24, bytes_accessed=2**20, transcendentals=0),
        **kwargs,
    )(*args)


def exchange(value, axes=CHIPS):
    return lax.all_to_all(value, axes, 0, 0, tiled=True)


def swap_cores(value):
    return lax.ppermute(value, "h", [(0, 1), (1, 0)])


def after(done, *values):
    return lax.optimization_barrier((done,) + values)[1:]


def shards(pair, pair_cot, mask, chain_ids, chain_bias, w_in, w_gate, w_out, in_gain, out_gain):
    block = pair.shape
    pair = pair.reshape(POS, CH)
    cot_in = pair_cot.reshape(POS, CH)
    mask, chain, bias = mask[None, :], chain_ids[None, :], chain_bias[None, :]
    field, field16 = ((CH, POS), F32), ((CH, POS), BF16)
    square, work = ((128, 128), F32), ((2, 128, 128), F32)

    def rows(n, dtype=F32):
        return ((n, 128), dtype)

    operands = [
        pltpu.with_memory_space_constraint(v, pltpu.HBM)
        for v in (pair, mask, chain, bias, in_gain, out_gain, w_in, w_gate)
    ]
    z0, n0, g0, m, gains, send = call(
        start_kernel, "start", [field, field16, field, ((8, POS), F32), rows(4), rows(512, BF16)],
        [(v.shape[1:] if k > 5 else v.shape, v.dtype) for k, v in enumerate(operands)]
        + [rows(512), pltpu.SemaphoreType.DMA((8,))],
        *operands, in_specs=[pl.BlockSpec(memory_space=pltpu.HBM)] * 8,
    )
    mine = exchange(send)
    other_ab = swap_cores(mine)
    a0, b0, x_mine = call(
        outgoing_mine_kernel, "outgoing_mine", [field16, field16, square], [rows(512), work], mine
    )
    b0_other, send = call(
        outgoing_kernel, "outgoing", [field16, rows(256, BF16)], [rows(512), work, rows(256)],
        other_ab, a0, x_mine,
    )
    x0 = exchange(send)
    z1, y0, n1, g1, send = call(
        middle_kernel, "middle", [field, field, field16, field, rows(512, BF16)], [rows(256), rows(512)],
        x0, z0, g0, m, gains, w_in, w_gate, w_out,
    )
    mine = exchange(send)
    other = swap_cores(mine)
    a1, b1, x_mine = call(
        incoming_mine_kernel, "incoming_mine", [field16, field16, field], [rows(512), work], mine
    )
    (a0_other,) = call(
        other_rows_kernel, "other_rows", [field16], [rows(512), work], *after(mine, other_ab)
    )
    (send,) = call(
        incoming_kernel, "incoming", [rows(256, BF16)], [rows(512), work, rows(256)],
        other, *after(a0_other, x_mine),
    )
    cot, y1, xn, dy, dpg1, send = call(
        turn_kernel, "turn", [field, field, field16, field16, field16, rows(256, BF16)],
        [rows(256), rows(256)], exchange(send), g1, cot_in, gains, w_out,
    )
    mine = exchange(send)
    other = swap_cores(mine)
    ga, gb = call(
        incoming_back_mine_kernel, "incoming_back_mine", [square, field], [rows(256), work], mine, a1, b1
    )
    new_pair, gw1 = call(
        turn_rest_kernel, "turn_rest", [rows(POS, BF16), rows(256, BF16)], [],
        *after(mine, z1, y1, g1, n1, xn, dy, dpg1),
    )
    (send,) = call(
        incoming_back_kernel, "incoming_back", [rows(512, BF16)], [rows(256), work, rows(512)],
        other, a1, b1, *after(gw1, ga, gb),
    )
    dz1, dp1, dpg0, xn, dy, send = call(
        back_kernel, "back", [field, ((512, POS), BF16), field16, field16, field16, rows(256, BF16)],
        [rows(512), rows(256), rows(256)],
        exchange(send), n1, z1, m, dpg1, cot, x0, g0, y0, gains, w_in, w_gate, w_out,
    )
    mine = exchange(send)
    other = swap_cores(mine)
    ga, gb = call(
        outgoing_back_mine_kernel, "outgoing_back_mine", [rows(256), field],
        [rows(256), work, rows(256)], mine, a0, b0, b0_other,
    )
    (early,) = call(
        back_rest_kernel, "back_rest", [rows(1024, BF16)], [], *after(mine, n1, dp1, gw1, n0, dpg0, xn, dy)
    )
    (send,) = call(
        outgoing_back_kernel, "outgoing_back", [rows(512, BF16)], [rows(256), work, rows(512)],
        other, *after(early, ga, gb), a0_other,
    )
    pair_grad, send = call(
        end_kernel, "end", [rows(POS), rows(1536, BF16)],
        [rows(512), ((512, POS), BF16)],
        exchange(send), n0, z0, m, dpg0, dz1, gains, w_in, w_gate, early,
    )
    (send,) = call(sum_kernel, "plane_sum", [rows(384, BF16)], [], exchange(send, PLANE))
    (send,) = call(sum_kernel, "line_sum", [rows(1536, BF16)], [], exchange(send, LINE))
    weights = [((2, 128, 512), F32), ((2, 128, 128), F32), ((2, 128, 128), F32)]
    in_grad, gate_grad, out_grad, pair_grad = call(
        place_kernel, "place", weights + [rows(POS)], weights + [pltpu.SemaphoreType.DMA((5,))],
        exchange(send, PLANE), pair_grad, out_specs=[pl.BlockSpec(memory_space=pltpu.HBM)] * 4,
    )
    return (new_pair.reshape(block), pair_grad.reshape(block), in_grad, gate_grad, out_grad)


def solution(mesh):
    devices = mesh.devices.reshape(tuple(SIZES.values()))
    split = P(("y", "zl", "h"), ("zh", "x"), None)
    return jax.shard_map(
        shards,
        mesh=Mesh(devices, tuple(SIZES)),
        in_specs=(split, split) + (P(),) * 8,
        out_specs=(split, split, P(), P(), P()),
        check_vma=False,
    )
```

```python
import functools

import jax
import jax.numpy as jnp
from jax import lax
from jax.experimental import pallas as pl
from jax.experimental.pallas import tpu as pltpu
from jax.sharding import Mesh, PartitionSpec as P

F32 = jnp.float32
BF16 = jnp.bfloat16
POS = 256
CH = 128
EPS = 1e-05
SIZES = {"y": 4, "zl": 2, "h": 2, "zh": 4, "x": 4}
CHIPS = ("zh", "x", "y", "zl")
PLANE = ("x", "y")
LINE = ("zl", "zh")


def dot(a, b, ca, cb):
    return lax.dot_general(
        a.astype(BF16), b.astype(BF16), (((ca,), (cb,)), ((), ())), preferred_element_type=F32
    )


def swap_blocks(tiles):
    block = lax.broadcasted_iota(jnp.int32, tiles[0].shape, 1) // 16
    for d in (1, 2, 4):
        high = (block & d) != 0
        out = list(tiles)
        for t in range(8):
            if t & d == 0:
                lo, hi = tiles[t], tiles[t | d]
                out[t] = jnp.where(high, pltpu.roll(hi, 16 * d, 1), lo)
                out[t | d] = jnp.where(high, hi, pltpu.roll(lo, 128 - 16 * d, 1))
        tiles = out
    return tiles


def messages_to_half(src, off, w, dst):
    for half in range(2):
        for p in range(2):
            tiles = [
                src[pl.ds((2 * t + p) * 8 * w + off + half, 8, stride=w), :] for t in range(8)
            ]
            for t, tile in enumerate(swap_blocks(tiles)):
                dst[p, pl.ds(half * 8 + t, 8, stride=16), :] = tile
    return jnp.concatenate([dst[0], dst[1]], axis=1).astype(BF16)


def half_to_messages(value, src, dst, off, w):
    for p in range(2):
        src[p] = value[p]
    for half in range(2):
        for p in range(2):
            tiles = [src[p, pl.ds(half * 8 + t, 8, stride=16), :] for t in range(8)]
            for t, tile in enumerate(swap_blocks(tiles)):
                dst[pl.ds((2 * t + p) * 8 * w + off + half, 8, stride=w), :] = tile


def halves(value):
    return value[:, 0:128], value[:, 128:256]


def by_parity(mine, other):
    first = lax.axis_index("h") == 0
    return jnp.where(first, mine, other), jnp.where(first, other, mine)


def own_columns(value):
    return by_parity(*halves(value))[0]


def other_columns(value):
    return by_parity(*halves(value))[1]


def channels_to_messages(v, dst, off, w):
    for half in range(2):
        dst[pl.ds(off + half, CH, stride=w), :] = v[:, half * 128 : (half + 1) * 128]


def messages_to_channels(src, off, w):
    return jnp.concatenate(
        [src[pl.ds(off + half, CH, stride=w), :] for half in range(2)], axis=1
    )


def column(row):
    square = jnp.broadcast_to(row, (CH, CH)).T
    return jnp.concatenate([square, square], axis=1)


def normalise(z):
    centered = z - jnp.mean(z, axis=0, keepdims=True)
    rstd = lax.rsqrt(jnp.mean(centered * centered, axis=0, keepdims=True) + EPS)
    return centered * rstd, rstd


def normalise_back(cot, hat, rstd):
    return rstd * (
        cot
        - jnp.mean(cot, axis=0, keepdims=True)
        - hat * jnp.mean(cot * hat, axis=0, keepdims=True)
    )


def prepare(z, gain, w_in, m, n_ref, send, send_ref, copies=()):
    hat, _ = normalise(z)
    normed = (hat * gain).astype(BF16)
    n_ref[...] = normed
    for copy in copies:
        copy.wait()
    p = dot(w_in[...], normed, 0, 0)
    a = m * jax.nn.sigmoid(p[0:128]) * p[128:256]
    b = m * jax.nn.sigmoid(p[256:384]) * p[384:512]
    channels_to_messages(a, send, 0, 4)
    channels_to_messages(b, send, 2, 4)
    send_ref[...] = send[...].astype(BF16)


def project_back(recv, normed, w_in, m, dp):
    p = dot(w_in, normed, 0, 0)
    for k in range(2):
        cot = messages_to_channels(recv, 2 * k, 4) * m
        s = jax.nn.sigmoid(p[256 * k : 256 * k + 128])
        v = p[256 * k + 128 : 256 * k + 256]
        dp[256 * k : 256 * k + 128, :] = (cot * v * s * (1.0 - s)).astype(BF16)
        dp[256 * k + 128 : 256 * k + 256, :] = (cot * s).astype(BF16)


def normed_back(dp, z, gain, w_in, w_gate, dpg):
    dn = dot(w_in, dp[...], 1, 0) + dot(w_gate, dpg, 1, 0)
    hat, rstd = normalise(z)
    return normalise_back(dn * gain, hat, rstd)


def start_kernel(*refs):
    hbm, (z_ref, n_ref, m_ref, gain_ref, send_ref), refs = refs[:7], refs[7:12], refs[12:]
    vmem, send, sem = refs[:7], refs[7], refs[8]
    copies = [
        pltpu.make_async_copy(src.at[0] if k > 5 else src, dst, sem.at[k])
        for k, (src, dst) in enumerate(zip(hbm, vmem))
    ]
    for copy in copies:
        copy.start()
    pair, mask, chain, bias, in_gain, out_gain, w_in = vmem
    row = (lax.axis_index("y") * 2 + lax.axis_index("zl")) * 2 + lax.axis_index("h")
    col = lax.axis_index("zh") * 4 + lax.axis_index("x")
    res = lax.broadcasted_iota(jnp.int32, (256, POS), 0)
    pos = lax.broadcasted_iota(jnp.int32, (256, POS), 1)
    in_row = (res == row * 16 + pos // 16).astype(F32)
    in_col = (res == col * 16 + pos % 16).astype(F32)
    for copy in copies[:6]:
        copy.wait()
    both = jnp.concatenate(
        [
            jnp.broadcast_to(mask[...].astype(F32), (8, 256)),
            jnp.broadcast_to(chain[...].astype(F32), (8, 256)),
        ],
        axis=0,
    )
    of_row = dot(both, in_row, 1, 0)
    of_col = dot(both, in_col, 1, 0)
    m8 = of_row[0:8] * of_col[0:8]
    m_ref[...] = m8
    gain_ref[0:2, :] = in_gain[...]
    gain_ref[2:4, :] = out_gain[...]
    same = (of_row[8:9] == of_col[8:9]).astype(F32)
    z = pair[...].astype(F32).T + same * column(bias[...])
    z_ref[...] = z
    gain = column(in_gain[0:1])
    prepare(z, gain, w_in, m8[0:1], n_ref, send, send_ref, copies[6:])


def gate_kernel(u, normed, w_gate, g_ref):
    g_ref[...] = jax.nn.sigmoid(dot(w_gate[u], normed[...], 0, 0))


def middle_kernel(x_in, z0, g0, m, gains, w_in, w_out, z_ref, y_ref, n_ref, send_ref, xs, send):
    xs[...] = x_in[...].astype(F32)
    hat, _ = normalise(messages_to_channels(xs, 0, 2))
    y = dot(w_out[0], hat * column(gains[2:3]), 0, 0)
    y_ref[...] = y
    z = z0[...] + g0[...] * y
    z_ref[...] = z
    prepare(z, column(gains[1:2]), w_in.at[1], m[0:1], n_ref, send, send_ref)


def turn_kernel(x_in, g1, cot_in, gains, w_out, cot_ref, y_ref, xn_ref, dy_ref, dpg_ref, send_ref, xs, send):
    xs[...] = x_in[...].astype(F32)
    gain = column(gains[3:4])
    hat, rstd = normalise(messages_to_channels(xs, 0, 2))
    xn = (hat * gain).astype(BF16)
    xn_ref[...] = xn
    y = dot(w_out[1], xn, 0, 0)
    y_ref[...] = y
    g = g1[...]
    cot = cot_in[...].astype(F32).T
    cot_ref[...] = cot
    dy = (cot * g).astype(BF16)
    dy_ref[...] = dy
    dpg_ref[...] = (cot * y * g * (1.0 - g)).astype(BF16)
    gx = normalise_back(dot(w_out[1], dy, 1, 0) * gain, hat, rstd)
    channels_to_messages(gx, send, 0, 2)
    send_ref[...] = send[...].astype(BF16)


def turn_rest_kernel(z1, y1, g1, n1, xn, dy, dpg, new_ref, gw_ref):
    new_ref[...] = (z1[...] + g1[...] * y1[...]).T.astype(BF16)
    gw_ref[0:128, :] = dot(n1[...], dpg[...], 1, 1).astype(BF16)
    gw_ref[128:256, :] = dot(xn[...], dy[...], 1, 1).astype(BF16)


def back_kernel(gab, n1, z1, m, dpg1, cot, x_in, g0, y0, gains, w_in, w_gate, w_out, dz_ref, dp_ref, dpg_ref, xn_ref, dy_ref, send_ref, rs, xs, send):
    rs[...] = gab[...].astype(F32)
    project_back(rs, n1[...], w_in[1], m[0:1], dp_ref)
    dz = cot[...] + normed_back(
        dp_ref, z1[...], column(gains[1:2]), w_in[1], w_gate[1], dpg1[...]
    )
    dz_ref[...] = dz
    g = g0[...]
    dpg_ref[...] = (dz * y0[...] * g * (1.0 - g)).astype(BF16)
    dy = (dz * g).astype(BF16)
    dy_ref[...] = dy
    xs[...] = x_in[...].astype(F32)
    gain = column(gains[2:3])
    hat, rstd = normalise(messages_to_channels(xs, 0, 2))
    xn_ref[...] = (hat * gain).astype(BF16)
    gx = normalise_back(dot(w_out[0], dy, 1, 0) * gain, hat, rstd)
    channels_to_messages(gx, send, 0, 2)
    send_ref[...] = send[...].astype(BF16)


def back_rest_kernel(n1, dp1, gw1, n0, dpg0, xn, dy, early_ref):
    for e in range(4):
        block = slice(128 * e, 128 * (e + 1))
        early_ref[block, :] = dot(n1[...], dp1[block, :], 1, 1).astype(BF16)
    early_ref[512:768, :] = gw1[...]
    early_ref[768:896, :] = dot(n0[...], dpg0[...], 1, 1).astype(BF16)
    early_ref[896:1024, :] = dot(xn[...], dy[...], 1, 1).astype(BF16)


def end_kernel(gab, n0, m, w_in, early, dp_ref, mine_ref, send_ref, rs):
    rs[...] = gab[...].astype(F32)
    project_back(rs, n0[...], w_in[0], m[0:1], dp_ref)
    first = lax.axis_index("h") == 0
    parts = [dot(n0[...], dp_ref[128 * e : 128 * (e + 1), :], 1, 1) for e in range(4)]
    parts += [early[128 * k : 128 * (k + 1), :].astype(F32) for k in range(8)]
    for k, (low, high) in enumerate([(0, 2), (1, 3), (4, 8), (5, 9), (6, 10), (7, 11)]):
        block = slice(128 * k, 128 * (k + 1))
        mine_ref[block, :] = jnp.where(first, parts[low], parts[high])
        send_ref[block, :] = jnp.where(first, parts[high], parts[low]).astype(BF16)


def end_rest_kernel(dp, z0, dpg0, dz1, gains, w_in, w_gate, grad_ref):
    dz = dz1[...] + normed_back(dp, z0[...], column(gains[0:1]), w_in[0], w_gate[0], dpg0[...])
    grad_ref[...] = dz.T


def core_sum_kernel(mine, other, send_ref):
    send_ref[...] = (mine[...] + other[...].astype(F32)).astype(BF16)


def sum_kernel(recv, send_ref):
    total = recv[0:48, :].astype(F32)
    for k in range(1, recv.shape[0] // 48):
        total = total + recv[48 * k : 48 * (k + 1), :].astype(F32)
    total = total.astype(BF16)
    for k in range(send_ref.shape[0] // 48):
        send_ref[48 * k : 48 * (k + 1), :] = total


def place_kernel(core_of, rows, *refs):
    in_out, gate_out, out_out, in_ref, gate_ref, out_ref, sem = refs[-7:]

    def block(k):
        return rows[128 * k : 128 * (k + 1), :].astype(F32)

    def write(src, dst, k):
        copy = pltpu.make_async_copy(src, dst, sem.at[k])
        copy.start()
        return copy

    def low():
        for e in range(2):
            in_ref[0, :, 128 * e : 128 * (e + 1)] = block(e)
        copies = [write(in_ref.at[0, :, 0:256], in_out.at[0, :, 0:256], 0)]
        for e in range(4):
            in_ref[1, :, 128 * e : 128 * (e + 1)] = block(2 + e)
        copies.append(write(in_ref.at[1], in_out.at[1], 1))
        for copy in copies:
            copy.wait()

    def high():
        for e in range(2):
            in_ref[0, :, 128 * (2 + e) : 128 * (3 + e)] = block(e)
        copies = [write(in_ref.at[0, :, 256:512], in_out.at[0, :, 256:512], 0)]
        for k, u in ((2, 1), (4, 0)):
            gate_ref[u] = block(k)
            out_ref[u] = block(k + 1)
        copies += [write(gate_ref, gate_out, 1), write(out_ref, out_out, 2)]
        for copy in copies:
            copy.wait()

    is_low = lax.axis_index("h") == core_of
    pl.when(is_low)(low)
    pl.when(jnp.logical_not(is_low))(high)


def outgoing_mine_kernel(mine, a_ref, b_ref, x_ref, ms, mat):
    ms[...] = mine[...].astype(F32)
    a, b = messages_to_half(ms, 0, 4, mat), messages_to_half(ms, 2, 4, mat)
    a_ref[...] = a
    b_ref[...] = b
    x_ref[...] = dot(a, b, 1, 1)


def outgoing_kernel(other, a, x_mine, b_ref, send_ref, os, mat, send):
    os[...] = other[...].astype(F32)
    b = messages_to_half(os, 2, 4, mat)
    b_ref[...] = b
    half_to_messages(by_parity(x_mine[...], dot(a[...], b, 1, 1)), mat, send, 0, 2)
    send_ref[...] = send[...].astype(BF16)


def incoming_mine_kernel(mine, a_ref, b_ref, x_ref, ms, mat):
    ms[...] = mine[...].astype(F32)
    a, b = messages_to_half(ms, 0, 4, mat), messages_to_half(ms, 2, 4, mat)
    a_ref[...] = a
    b_ref[...] = b
    x_ref[...] = dot(own_columns(a), b, 0, 0)


def incoming_kernel(other, x_mine, send_ref, os, mat, send):
    os[...] = other[...].astype(F32)
    a, b = messages_to_half(os, 0, 4, mat), messages_to_half(os, 2, 4, mat)
    half_to_messages(halves(x_mine[...] + dot(own_columns(a), b, 0, 0)), mat, send, 0, 2)
    send_ref[...] = send[...].astype(BF16)


def incoming_back_mine_kernel(mine, a, b, ga_ref, gb_ref, ms, mat):
    ms[...] = mine[...].astype(F32)
    gx = messages_to_half(ms, 0, 2, mat)
    ga_ref[...] = dot(b[...], gx, 1, 1)
    gb_ref[...] = dot(own_columns(a[...]), gx, 1, 0)


def incoming_back_kernel(other, a, b, ga_mine, gb_mine, send_ref, os, mat, send):
    os[...] = other[...].astype(F32)
    gx = messages_to_half(os, 0, 2, mat)
    half_to_messages(by_parity(ga_mine[...], dot(b[...], gx, 1, 1)), mat, send, 0, 4)
    gb = gb_mine[...] + dot(other_columns(a[...]), gx, 1, 0)
    half_to_messages(halves(gb), mat, send, 2, 4)
    send_ref[...] = send[...].astype(BF16)


def other_rows_kernel(other_ab, a_ref, os, mat):
    os[...] = other_ab[...].astype(F32)
    a_ref[...] = messages_to_half(os, 0, 4, mat)


def outgoing_back_mine_kernel(mine, a, b, b_other, ga_ref, gb_ref, ms, mat, send):
    ms[...] = mine[...].astype(F32)
    gx = messages_to_half(ms, 0, 2, mat)
    even, odd = by_parity(b[...], b_other[...])
    ga = dot(gx, jnp.concatenate([even, odd], axis=0), 1, 0)
    half_to_messages(halves(ga), mat, send, 0, 2)
    ga_ref[...] = send[...]
    gb_ref[...] = dot(own_columns(gx), a[...], 0, 0)


def outgoing_back_kernel(other, ga, gb_mine, a_other, send_ref, os, mat, send):
    os[...] = other[...].astype(F32)
    gx = messages_to_half(os, 0, 2, mat)
    gb = gb_mine[...] + dot(own_columns(gx), a_other[...], 0, 0)
    half_to_messages(halves(gb), mat, send, 2, 4)
    for half in range(2):
        send[pl.ds(half, CH, stride=4), :] = ga[pl.ds(half, CH, stride=2), :]
    send_ref[...] = send[...].astype(BF16)


def call(kernel, name, outs, scratch, *args, **kwargs):
    return pl.pallas_call(
        kernel,
        name=name,
        out_shape=[jax.ShapeDtypeStruct(s, d) for s, d in outs],
        scratch_shapes=[s if not isinstance(s, tuple) else pltpu.VMEM(*s) for s in scratch],
        compiler_params=pltpu.CompilerParams(vmem_limit_bytes=24 * 1024 * 1024),
        cost_estimate=pl.CostEstimate(flops=2**24, bytes_accessed=2**20, transcendentals=0),
        **kwargs,
    )(*args)


def exchange(value, axes=CHIPS):
    return lax.all_to_all(value, axes, 0, 0, tiled=True)


def swap_cores(value):
    return lax.ppermute(value, "h", [(0, 1), (1, 0)])


def after(done, *values):
    return lax.optimization_barrier((done,) + values)[1:]


def shards(pair, pair_cot, mask, chain_ids, chain_bias, w_in, w_gate, w_out, in_gain, out_gain):
    block = pair.shape
    pair = pair.reshape(POS, CH)
    cot_in = pair_cot.reshape(POS, CH)
    mask, chain, bias = mask[None, :], chain_ids[None, :], chain_bias[None, :]
    field, field16 = ((CH, POS), F32), ((CH, POS), BF16)
    square, work = ((128, 128), F32), ((2, 128, 128), F32)

    def rows(n, dtype=F32):
        return ((n, 128), dtype)

    operands = [
        pltpu.with_memory_space_constraint(v, pltpu.HBM)
        for v in (pair, mask, chain, bias, in_gain, out_gain, w_in)
    ]
    z0, n0, m, gains, send = call(
        start_kernel, "start", [field, field16, ((8, POS), F32), rows(4), rows(512, BF16)],
        [(v.shape[1:] if k > 5 else v.shape, v.dtype) for k, v in enumerate(operands)]
        + [rows(512), pltpu.SemaphoreType.DMA((7,))],
        *operands, in_specs=[pl.BlockSpec(memory_space=pltpu.HBM)] * 7,
    )
    mine = exchange(send)
    other_ab = swap_cores(mine)
    a0, b0, x_mine = call(
        outgoing_mine_kernel, "outgoing_mine", [field16, field16, square], [rows(512), work], mine
    )
    (g0,) = call(
        functools.partial(gate_kernel, 0), "gate0", [field], [], *after(mine, n0), w_gate
    )
    b0_other, send = call(
        outgoing_kernel, "outgoing", [field16, rows(256, BF16)], [rows(512), work, rows(256)],
        other_ab, a0, *after(g0, x_mine),
    )
    x0 = exchange(send)
    z1, y0, n1, send = call(
        middle_kernel, "middle", [field, field, field16, rows(512, BF16)], [rows(256), rows(512)],
        x0, z0, g0, m, gains, w_in, w_out,
    )
    mine = exchange(send)
    other = swap_cores(mine)
    a1, b1, x_mine = call(
        incoming_mine_kernel, "incoming_mine", [field16, field16, field], [rows(512), work], mine
    )
    (a0_other,) = call(
        other_rows_kernel, "other_rows", [field16], [rows(512), work], *after(mine, other_ab)
    )
    (g1,) = call(
        functools.partial(gate_kernel, 1), "gate1", [field], [], *after(mine, n1), w_gate
    )
    (send,) = call(
        incoming_kernel, "incoming", [rows(256, BF16)], [rows(512), work, rows(256)],
        other, *after((a0_other, g1), x_mine),
    )
    cot, y1, xn, dy, dpg1, send = call(
        turn_kernel, "turn", [field, field, field16, field16, field16, rows(256, BF16)],
        [rows(256), rows(256)], exchange(send), g1, cot_in, gains, w_out,
    )
    mine = exchange(send)
    other = swap_cores(mine)
    ga, gb = call(
        incoming_back_mine_kernel, "incoming_back_mine", [square, field], [rows(256), work], mine, a1, b1
    )
    new_pair, gw1 = call(
        turn_rest_kernel, "turn_rest", [rows(POS, BF16), rows(256, BF16)], [],
        *after(mine, z1, y1, g1, n1, xn, dy, dpg1),
    )
    (send,) = call(
        incoming_back_kernel, "incoming_back", [rows(512, BF16)], [rows(256), work, rows(512)],
        other, a1, b1, *after(gw1, ga, gb),
    )
    dz1, dp1, dpg0, xn, dy, send = call(
        back_kernel, "back", [field, ((512, POS), BF16), field16, field16, field16, rows(256, BF16)],
        [rows(512), rows(256), rows(256)],
        exchange(send), n1, z1, m, dpg1, cot, x0, g0, y0, gains, w_in, w_gate, w_out,
    )
    mine = exchange(send)
    other = swap_cores(mine)
    ga, gb = call(
        outgoing_back_mine_kernel, "outgoing_back_mine", [rows(256), field],
        [rows(256), work, rows(256)], mine, a0, b0, b0_other,
    )
    (early,) = call(
        back_rest_kernel, "back_rest", [rows(1024, BF16)], [], *after(mine, n1, dp1, gw1, n0, dpg0, xn, dy)
    )
    (send,) = call(
        outgoing_back_kernel, "outgoing_back", [rows(512, BF16)], [rows(256), work, rows(512)],
        other, *after(early, ga, gb), a0_other,
    )
    dp0, mine, send = call(
        end_kernel, "end", [((512, POS), BF16), rows(768), rows(768, BF16)], [rows(512)],
        exchange(send), n0, m, w_in, early,
    )
    other = swap_cores(send)
    (pair_grad,) = call(
        end_rest_kernel, "end_rest", [rows(POS)], [], dp0, z0, dpg0, dz1, gains, w_in, w_gate
    )
    (send,) = call(
        core_sum_kernel, "core_sum", [rows(768, BF16)], [], *after(pair_grad, mine), other
    )
    (send,) = call(sum_kernel, "plane_sum", [rows(384, BF16)], [], exchange(send, PLANE))
    (send,) = call(sum_kernel, "line_sum", [rows(768, BF16)], [], exchange(send, LINE))
    mine = exchange(send, PLANE)
    weights = [((2, 128, 512), F32), ((2, 128, 128), F32), ((2, 128, 128), F32)]
    hbm = [pl.BlockSpec(memory_space=pltpu.HBM)] * 3
    scratch = weights + [pltpu.SemaphoreType.DMA((3,))]
    other = swap_cores(mine)
    grads = call(
        functools.partial(place_kernel, 0), "place_mine", weights, scratch, mine, out_specs=hbm
    )
    in_grad, gate_grad, out_grad = call(
        functools.partial(place_kernel, 1), "place_other", weights, scratch, other, *grads,
        in_specs=[pl.BlockSpec(memory_space=pltpu.VMEM)] + hbm, out_specs=hbm,
        input_output_aliases={1: 0, 2: 1, 3: 2},
    )
    return (new_pair.reshape(block), pair_grad.reshape(block), in_grad, gate_grad, out_grad)


def solution(mesh):
    devices = mesh.devices.reshape(tuple(SIZES.values()))
    split = P(("y", "zl", "h"), ("zh", "x"), None)
    return jax.shard_map(
        shards,
        mesh=Mesh(devices, tuple(SIZES)),
        in_specs=(split, split) + (P(),) * 8,
        out_specs=(split, split, P(), P(), P()),
        check_vma=False,
    )
```

```python
import functools

import jax
import jax.numpy as jnp
from jax import lax
from jax.experimental import pallas as pl
from jax.experimental.pallas import tpu as pltpu
from jax.sharding import Mesh, PartitionSpec as P

F32 = jnp.float32
BF16 = jnp.bfloat16
POS = 256
CH = 128
EPS = 1e-05
SIZES = {"y": 4, "zl": 2, "h": 2, "zh": 4, "x": 4}
CHIPS = ("zh", "x", "y", "zl")
PLANE = ("x", "y")
LINE = ("zl", "zh")


def dot(a, b, ca, cb):
    return lax.dot_general(
        a.astype(BF16), b.astype(BF16), (((ca,), (cb,)), ((), ())), preferred_element_type=F32
    )


def swap_blocks(tiles):
    block = lax.broadcasted_iota(jnp.int32, tiles[0].shape, 1) // 16
    high = block >= 4
    out = list(tiles)
    for t in range(4):
        lo, hi = tiles[t], tiles[t + 4]
        crossed = pltpu.roll(jnp.where(high, lo, hi), 64, 1)
        out[t] = jnp.where(high, crossed, lo)
        out[t + 4] = jnp.where(high, hi, crossed)
    tiles, out = out, []
    for i in range(8):
        value = tiles[i]
        for t in range(4):
            if t != i % 4:
                moved = pltpu.roll(tiles[i - i % 4 + t], 16 * (t - i % 4) % 128, 1)
                value = jnp.where(block % 4 == t, moved, value)
        out.append(value)
    return out


def messages_to_half(src, off, w, dst):
    for half in range(2):
        tiles = [
            src[pl.ds(16 * t * w + off + half, 16, stride=w), :].astype(BF16) for t in range(8)
        ]
        for t, tile in enumerate(swap_blocks(tiles)):
            tile = tile.astype(F32)
            for p in range(2):
                dst[p, pl.ds(half * 8 + t, 8, stride=16), :] = tile[8 * p : 8 * (p + 1)]
    return jnp.concatenate([dst[0], dst[1]], axis=1).astype(BF16)


def half_to_messages(value, src, dst, off, w):
    for p in range(2):
        src[p] = value[p]
    for half in range(2):
        tiles = []
        for t in range(8):
            both = [src[p, pl.ds(half * 8 + t, 8, stride=16), :] for p in range(2)]
            tiles.append(jnp.concatenate(both, axis=0).astype(BF16))
        for t, tile in enumerate(swap_blocks(tiles)):
            dst[pl.ds(16 * t * w + off + half, 16, stride=w), :] = tile.astype(F32)


def halves(value):
    return value[:, 0:128], value[:, 128:256]


def by_parity(mine, other):
    first = lax.axis_index("h") == 0
    return jnp.where(first, mine, other), jnp.where(first, other, mine)


def own_columns(value):
    return by_parity(*halves(value))[0]


def other_columns(value):
    return by_parity(*halves(value))[1]


def channels_to_messages(v, dst, off, w):
    for half in range(2):
        dst[pl.ds(off + half, CH, stride=w), :] = v[:, half * 128 : (half + 1) * 128]


def messages_to_channels(src, off, w):
    return jnp.concatenate(
        [src[pl.ds(off + half, CH, stride=w), :] for half in range(2)], axis=1
    )


def column(row):
    square = jnp.broadcast_to(row, (CH, CH)).T
    return jnp.concatenate([square, square], axis=1)


def normalise(z):
    centered = z - jnp.mean(z, axis=0, keepdims=True)
    rstd = lax.rsqrt(jnp.mean(centered * centered, axis=0, keepdims=True) + EPS)
    return centered * rstd, rstd


def normalise_back(cot, hat, rstd):
    return rstd * (
        cot
        - jnp.mean(cot, axis=0, keepdims=True)
        - hat * jnp.mean(cot * hat, axis=0, keepdims=True)
    )


def prepare(z, gain, w_in, m, n_ref, send, send_ref, copies=()):
    hat, _ = normalise(z)
    normed = (hat * gain).astype(BF16)
    n_ref[...] = normed
    for copy in copies:
        copy.wait()
    p = dot(w_in[...], normed, 0, 0)
    a = m * jax.nn.sigmoid(p[0:128]) * p[128:256]
    b = m * jax.nn.sigmoid(p[256:384]) * p[384:512]
    channels_to_messages(a, send, 0, 4)
    channels_to_messages(b, send, 2, 4)
    send_ref[...] = send[...].astype(BF16)


def project_back(recv, factors, dp):
    for k in range(2):
        cot = messages_to_channels(recv, 2 * k, 4)
        for e in range(2 * k, 2 * k + 2):
            block = slice(128 * e, 128 * (e + 1))
            dp[block, :] = (cot * factors[block, :]).astype(BF16)


def normed_back(dp, z, gain, w_in, w_gate, dpg):
    dn = dot(w_in, dp[...], 1, 0) + dot(w_gate, dpg, 1, 0)
    hat, rstd = normalise(z)
    return normalise_back(dn * gain, hat, rstd)


def start_kernel(*refs):
    hbm, (z_ref, n_ref, m_ref, gain_ref, w_in, w_gate, send_ref), refs = refs[:8], refs[8:15], refs[15:]
    vmem, send, sem = refs[:6] + (w_in, w_gate), refs[6], refs[7]
    copies = [
        pltpu.make_async_copy(src.at[0] if k > 5 else src, dst, sem.at[k])
        for k, (src, dst) in enumerate(zip(hbm, vmem))
    ]
    for copy in copies:
        copy.start()
    pair, mask, chain, bias, in_gain, out_gain = vmem[:6]
    row = (lax.axis_index("y") * 2 + lax.axis_index("zl")) * 2 + lax.axis_index("h")
    col = lax.axis_index("zh") * 4 + lax.axis_index("x")
    res = lax.broadcasted_iota(jnp.int32, (256, POS), 0)
    pos = lax.broadcasted_iota(jnp.int32, (256, POS), 1)
    in_row = (res == row * 16 + pos // 16).astype(F32)
    in_col = (res == col * 16 + pos % 16).astype(F32)
    for copy in copies[:6]:
        copy.wait()
    both = jnp.concatenate(
        [
            jnp.broadcast_to(mask[...].astype(F32), (8, 256)),
            jnp.broadcast_to(chain[...].astype(F32), (8, 256)),
        ],
        axis=0,
    )
    of_row = dot(both, in_row, 1, 0)
    of_col = dot(both, in_col, 1, 0)
    m8 = of_row[0:8] * of_col[0:8]
    m_ref[...] = m8
    gain_ref[0:2, :] = in_gain[...]
    gain_ref[2:4, :] = out_gain[...]
    same = (of_row[8:9] == of_col[8:9]).astype(F32)
    z = pair[...].astype(F32).T + same * column(bias[...])
    z_ref[...] = z
    gain = column(in_gain[0:1])
    prepare(z, gain, w_in, m8[0:1], n_ref, send, send_ref, copies[6:7])
    copies[7].wait()


def side_kernel(normed, m, w_in, w_gate, g_ref, factor_ref):
    p = dot(w_in[...], normed[...], 0, 0)
    for k in range(2):
        s = jax.nn.sigmoid(p[256 * k : 256 * k + 128])
        ms = m[0:1] * s
        factor_ref[256 * k : 256 * k + 128, :] = ms * (1.0 - s) * p[256 * k + 128 : 256 * k + 256]
        factor_ref[256 * k + 128 : 256 * k + 256, :] = ms
    g_ref[...] = jax.nn.sigmoid(dot(w_gate[...], normed[...], 0, 0))


def middle_kernel(x_in, z0, g0, m, gains, w_in, w_gate, w_out, z_ref, y_ref, n_ref, w_in_ref, w_gate_ref, send_ref, xs, send):
    w_in_ref[...] = w_in[1]
    w_gate_ref[...] = w_gate[1]
    xs[...] = x_in[...].astype(F32)
    hat, _ = normalise(messages_to_channels(xs, 0, 2))
    y = dot(w_out[0], hat * column(gains[2:3]), 0, 0)
    y_ref[...] = y
    z = z0[...] + g0[...] * y
    z_ref[...] = z
    prepare(z, column(gains[1:2]), w_in.at[1], m[0:1], n_ref, send, send_ref)


def turn_kernel(x_in, g1, cot_in, gains, w_out, cot_ref, y_ref, xn_ref, dy_ref, dpg_ref, send_ref, xs, send):
    xs[...] = x_in[...].astype(F32)
    gain = column(gains[3:4])
    hat, rstd = normalise(messages_to_channels(xs, 0, 2))
    xn = (hat * gain).astype(BF16)
    xn_ref[...] = xn
    y = dot(w_out[1], xn, 0, 0)
    y_ref[...] = y
    g = g1[...]
    cot = cot_in[...].astype(F32).T
    cot_ref[...] = cot
    dy = (cot * g).astype(BF16)
    dy_ref[...] = dy
    dpg_ref[...] = (cot * y * g * (1.0 - g)).astype(BF16)
    gx = normalise_back(dot(w_out[1], dy, 1, 0) * gain, hat, rstd)
    channels_to_messages(gx, send, 0, 2)
    send_ref[...] = send[...].astype(BF16)


def turn_rest_kernel(z1, y1, g1, n1, xn, dy, dpg, new_ref, gw_ref):
    new_ref[...] = (z1[...] + g1[...] * y1[...]).T.astype(BF16)
    gw_ref[0:128, :] = dot(n1[...], dpg[...], 1, 1).astype(BF16)
    gw_ref[128:256, :] = dot(xn[...], dy[...], 1, 1).astype(BF16)


def back_kernel(gab, factors, z1, dpg1, cot, x_in, g0, y0, gains, w_in, w_gate, w_out, dz_ref, dp_ref, dpg_ref, xn_ref, dy_ref, send_ref, rs, xs, send):
    rs[...] = gab[...].astype(F32)
    project_back(rs, factors, dp_ref)
    dz = cot[...] + normed_back(
        dp_ref, z1[...], column(gains[1:2]), w_in[1], w_gate[1], dpg1[...]
    )
    dz_ref[...] = dz
    g = g0[...]
    dpg_ref[...] = (dz * y0[...] * g * (1.0 - g)).astype(BF16)
    dy = (dz * g).astype(BF16)
    dy_ref[...] = dy
    xs[...] = x_in[...].astype(F32)
    gain = column(gains[2:3])
    hat, rstd = normalise(messages_to_channels(xs, 0, 2))
    xn_ref[...] = (hat * gain).astype(BF16)
    gx = normalise_back(dot(w_out[0], dy, 1, 0) * gain, hat, rstd)
    channels_to_messages(gx, send, 0, 2)
    send_ref[...] = send[...].astype(BF16)


def back_rest_kernel(n1, dp1, gw1, n0, dpg0, xn, dy, early_ref):
    for e in range(4):
        block = slice(128 * e, 128 * (e + 1))
        early_ref[block, :] = dot(n1[...], dp1[block, :], 1, 1).astype(BF16)
    early_ref[512:768, :] = gw1[...]
    early_ref[768:896, :] = dot(n0[...], dpg0[...], 1, 1).astype(BF16)
    early_ref[896:1024, :] = dot(xn[...], dy[...], 1, 1).astype(BF16)


def end_kernel(gab, factors, n0, early, dp_ref, mine_ref, send_ref, rs):
    rs[...] = gab[...].astype(F32)
    project_back(rs, factors, dp_ref)
    first = lax.axis_index("h") == 0
    parts = [dot(n0[...], dp_ref[128 * e : 128 * (e + 1), :], 1, 1) for e in range(4)]
    parts += [early[128 * k : 128 * (k + 1), :].astype(F32) for k in range(8)]
    for k, (low, high) in enumerate([(0, 2), (1, 3), (4, 8), (5, 9), (6, 10), (7, 11)]):
        block = slice(128 * k, 128 * (k + 1))
        mine_ref[block, :] = jnp.where(first, parts[low], parts[high])
        send_ref[block, :] = jnp.where(first, parts[high], parts[low]).astype(BF16)


def end_rest_kernel(dp, z0, dpg0, dz1, gains, w_in, w_gate, grad_ref):
    dz = dz1[...] + normed_back(dp, z0[...], column(gains[0:1]), w_in[0], w_gate[0], dpg0[...])
    grad_ref[...] = dz.T


def core_sum_kernel(mine, other, send_ref):
    send_ref[...] = (mine[...] + other[...].astype(F32)).astype(BF16)


def sum_kernel(recv, send_ref):
    total = recv[0:48, :].astype(F32)
    for k in range(1, recv.shape[0] // 48):
        total = total + recv[48 * k : 48 * (k + 1), :].astype(F32)
    total = total.astype(BF16)
    for k in range(send_ref.shape[0] // 48):
        send_ref[48 * k : 48 * (k + 1), :] = total


def place_kernel(core_of, rows, *refs):
    in_out, gate_out, out_out, in_ref, gate_ref, out_ref, sem = refs[-7:]

    def block(k):
        return rows[128 * k : 128 * (k + 1), :].astype(F32)

    def write(src, dst, k):
        copy = pltpu.make_async_copy(src, dst, sem.at[k])
        copy.start()
        return copy

    def low():
        for e in range(2):
            in_ref[0, :, 128 * e : 128 * (e + 1)] = block(e)
        copies = [write(in_ref.at[0, :, 0:256], in_out.at[0, :, 0:256], 0)]
        for e in range(4):
            in_ref[1, :, 128 * e : 128 * (e + 1)] = block(2 + e)
        copies.append(write(in_ref.at[1], in_out.at[1], 1))
        for copy in copies:
            copy.wait()

    def high():
        for e in range(2):
            in_ref[0, :, 128 * (2 + e) : 128 * (3 + e)] = block(e)
        copies = [write(in_ref.at[0, :, 256:512], in_out.at[0, :, 256:512], 0)]
        for k, u in ((2, 1), (4, 0)):
            gate_ref[u] = block(k)
            out_ref[u] = block(k + 1)
        copies += [write(gate_ref, gate_out, 1), write(out_ref, out_out, 2)]
        for copy in copies:
            copy.wait()

    is_low = lax.axis_index("h") == core_of
    pl.when(is_low)(low)
    pl.when(jnp.logical_not(is_low))(high)


def outgoing_mine_kernel(mine, a_ref, b_ref, x_ref, ms, mat):
    ms[...] = mine[...].astype(F32)
    a, b = messages_to_half(ms, 0, 4, mat), messages_to_half(ms, 2, 4, mat)
    a_ref[...] = a
    b_ref[...] = b
    x_ref[...] = dot(a, b, 1, 1)


def outgoing_kernel(other, a, x_mine, b_ref, send_ref, os, mat, send):
    os[...] = other[...].astype(F32)
    b = messages_to_half(os, 2, 4, mat)
    b_ref[...] = b
    half_to_messages(by_parity(x_mine[...], dot(a[...], b, 1, 1)), mat, send, 0, 2)
    send_ref[...] = send[...].astype(BF16)


def incoming_mine_kernel(mine, a_ref, b_ref, x_ref, ms, mat):
    ms[...] = mine[...].astype(F32)
    a, b = messages_to_half(ms, 0, 4, mat), messages_to_half(ms, 2, 4, mat)
    a_ref[...] = a
    b_ref[...] = b
    x_ref[...] = dot(own_columns(a), b, 0, 0)


def incoming_kernel(other, x_mine, send_ref, os, mat, send):
    os[...] = other[...].astype(F32)
    a, b = messages_to_half(os, 0, 4, mat), messages_to_half(os, 2, 4, mat)
    half_to_messages(halves(x_mine[...] + dot(own_columns(a), b, 0, 0)), mat, send, 0, 2)
    send_ref[...] = send[...].astype(BF16)


def incoming_back_mine_kernel(mine, a, b, ga_ref, gb_ref, ms, mat):
    ms[...] = mine[...].astype(F32)
    gx = messages_to_half(ms, 0, 2, mat)
    ga_ref[...] = dot(b[...], gx, 1, 1)
    gb_ref[...] = dot(own_columns(a[...]), gx, 1, 0)


def incoming_back_kernel(other, a, b, ga_mine, gb_mine, send_ref, os, mat, send):
    os[...] = other[...].astype(F32)
    gx = messages_to_half(os, 0, 2, mat)
    half_to_messages(by_parity(ga_mine[...], dot(b[...], gx, 1, 1)), mat, send, 0, 4)
    gb = gb_mine[...] + dot(other_columns(a[...]), gx, 1, 0)
    half_to_messages(halves(gb), mat, send, 2, 4)
    send_ref[...] = send[...].astype(BF16)


def other_rows_kernel(other_ab, a_ref, os, mat):
    os[...] = other_ab[...].astype(F32)
    a_ref[...] = messages_to_half(os, 0, 4, mat)


def outgoing_back_mine_kernel(mine, a, b, b_other, ga_ref, gb_ref, ms, mat, send):
    ms[...] = mine[...].astype(F32)
    gx = messages_to_half(ms, 0, 2, mat)
    even, odd = by_parity(b[...], b_other[...])
    ga = dot(gx, jnp.concatenate([even, odd], axis=0), 1, 0)
    half_to_messages(halves(ga), mat, send, 0, 2)
    ga_ref[...] = send[...]
    gb_ref[...] = dot(own_columns(gx), a[...], 0, 0)


def outgoing_back_kernel(other, ga, gb_mine, a_other, send_ref, os, mat, send):
    os[...] = other[...].astype(F32)
    gx = messages_to_half(os, 0, 2, mat)
    gb = gb_mine[...] + dot(own_columns(gx), a_other[...], 0, 0)
    half_to_messages(halves(gb), mat, send, 2, 4)
    for half in range(2):
        send[pl.ds(half, CH, stride=4), :] = ga[pl.ds(half, CH, stride=2), :]
    send_ref[...] = send[...].astype(BF16)


def call(kernel, name, outs, scratch, *args, **kwargs):
    return pl.pallas_call(
        kernel,
        name=name,
        out_shape=[jax.ShapeDtypeStruct(s, d) for s, d in outs],
        scratch_shapes=[s if not isinstance(s, tuple) else pltpu.VMEM(*s) for s in scratch],
        compiler_params=pltpu.CompilerParams(vmem_limit_bytes=24 * 1024 * 1024),
        cost_estimate=pl.CostEstimate(flops=2**24, bytes_accessed=2**20, transcendentals=0),
        **kwargs,
    )(*args)


def exchange(value, axes=CHIPS):
    return lax.all_to_all(value, axes, 0, 0, tiled=True)


def swap_cores(value):
    return lax.ppermute(value, "h", [(0, 1), (1, 0)])


def after(done, *values):
    return lax.optimization_barrier((done,) + values)[1:]


def shards(pair, pair_cot, mask, chain_ids, chain_bias, w_in, w_gate, w_out, in_gain, out_gain):
    block = pair.shape
    pair = pair.reshape(POS, CH)
    cot_in = pair_cot.reshape(POS, CH)
    mask, chain, bias = mask[None, :], chain_ids[None, :], chain_bias[None, :]
    field, field16 = ((CH, POS), F32), ((CH, POS), BF16)
    square, work = ((128, 128), F32), ((2, 128, 128), F32)

    def rows(n, dtype=F32):
        return ((n, 128), dtype)

    operands = [
        pltpu.with_memory_space_constraint(v, pltpu.HBM)
        for v in (pair, mask, chain, bias, in_gain, out_gain, w_in, w_gate)
    ]
    z0, n0, m, gains, w_in0, w_gate0, send = call(
        start_kernel, "start",
        [field, field16, ((8, POS), F32), rows(4), ((128, 512), BF16), rows(128, BF16), rows(512, BF16)],
        [(v.shape, v.dtype) for v in operands[:6]] + [rows(512), pltpu.SemaphoreType.DMA((8,))],
        *operands, in_specs=[pl.BlockSpec(memory_space=pltpu.HBM)] * 8,
    )
    mine = exchange(send)
    other_ab = swap_cores(mine)
    a0, b0, x_mine = call(
        outgoing_mine_kernel, "outgoing_mine", [field16, field16, square], [rows(512), work], mine
    )
    factors = ((512, POS), F32)
    g0, factors0 = call(
        side_kernel, "side0", [field, factors], [], *after(mine, n0), m, w_in0, w_gate0
    )
    b0_other, send = call(
        outgoing_kernel, "outgoing", [field16, rows(256, BF16)], [rows(512), work, rows(256)],
        other_ab, a0, *after(g0, x_mine),
    )
    x0 = exchange(send)
    z1, y0, n1, w_in1, w_gate1, send = call(
        middle_kernel, "middle", [field, field, field16, ((128, 512), BF16), rows(128, BF16), rows(512, BF16)],
        [rows(256), rows(512)], x0, z0, g0, m, gains, w_in, w_gate, w_out,
    )
    mine = exchange(send)
    other = swap_cores(mine)
    a1, b1, x_mine = call(
        incoming_mine_kernel, "incoming_mine", [field16, field16, field], [rows(512), work], mine
    )
    (a0_other,) = call(
        other_rows_kernel, "other_rows", [field16], [rows(512), work], *after(mine, other_ab)
    )
    g1, factors1 = call(
        side_kernel, "side1", [field, factors], [], *after(mine, n1), m, w_in1, w_gate1
    )
    (send,) = call(
        incoming_kernel, "incoming", [rows(256, BF16)], [rows(512), work, rows(256)],
        other, *after((a0_other, g1), x_mine),
    )
    cot, y1, xn, dy, dpg1, send = call(
        turn_kernel, "turn", [field, field, field16, field16, field16, rows(256, BF16)],
        [rows(256), rows(256)], exchange(send), g1, cot_in, gains, w_out,
    )
    mine = exchange(send)
    other = swap_cores(mine)
    ga, gb = call(
        incoming_back_mine_kernel, "incoming_back_mine", [square, field], [rows(256), work], mine, a1, b1
    )
    new_pair, gw1 = call(
        turn_rest_kernel, "turn_rest", [rows(POS, BF16), rows(256, BF16)], [],
        *after(mine, z1, y1, g1, n1, xn, dy, dpg1),
    )
    (send,) = call(
        incoming_back_kernel, "incoming_back", [rows(512, BF16)], [rows(256), work, rows(512)],
        other, a1, b1, *after(gw1, ga, gb),
    )
    dz1, dp1, dpg0, xn, dy, send = call(
        back_kernel, "back", [field, ((512, POS), BF16), field16, field16, field16, rows(256, BF16)],
        [rows(512), rows(256), rows(256)],
        exchange(send), factors1, z1, dpg1, cot, x0, g0, y0, gains, w_in, w_gate, w_out,
    )
    mine = exchange(send)
    other = swap_cores(mine)
    ga, gb = call(
        outgoing_back_mine_kernel, "outgoing_back_mine", [rows(256), field],
        [rows(256), work, rows(256)], mine, a0, b0, b0_other,
    )
    (early,) = call(
        back_rest_kernel, "back_rest", [rows(1024, BF16)], [], *after(mine, n1, dp1, gw1, n0, dpg0, xn, dy)
    )
    (send,) = call(
        outgoing_back_kernel, "outgoing_back", [rows(512, BF16)], [rows(256), work, rows(512)],
        other, *after(early, ga, gb), a0_other,
    )
    dp0, mine, send = call(
        end_kernel, "end", [((512, POS), BF16), rows(768), rows(768, BF16)], [rows(512)],
        exchange(send), factors0, n0, early,
    )
    other = swap_cores(send)
    (pair_grad,) = call(
        end_rest_kernel, "end_rest", [rows(POS)], [], dp0, z0, dpg0, dz1, gains, w_in, w_gate
    )
    (send,) = call(
        core_sum_kernel, "core_sum", [rows(768, BF16)], [], *after(pair_grad, mine), other
    )
    (send,) = call(sum_kernel, "plane_sum", [rows(384, BF16)], [], exchange(send, PLANE))
    (send,) = call(sum_kernel, "line_sum", [rows(768, BF16)], [], exchange(send, LINE))
    mine = exchange(send, PLANE)
    weights = [((2, 128, 512), F32), ((2, 128, 128), F32), ((2, 128, 128), F32)]
    hbm = [pl.BlockSpec(memory_space=pltpu.HBM)] * 3
    scratch = weights + [pltpu.SemaphoreType.DMA((3,))]
    other = swap_cores(mine)
    grads = call(
        functools.partial(place_kernel, 0), "place_mine", weights, scratch, mine, out_specs=hbm
    )
    in_grad, gate_grad, out_grad = call(
        functools.partial(place_kernel, 1), "place_other", weights, scratch, other, *grads,
        in_specs=[pl.BlockSpec(memory_space=pltpu.VMEM)] + hbm, out_specs=hbm,
        input_output_aliases={1: 0, 2: 1, 3: 2},
    )
    return (new_pair.reshape(block), pair_grad.reshape(block), in_grad, gate_grad, out_grad)


def solution(mesh):
    devices = mesh.devices.reshape(tuple(SIZES.values()))
    split = P(("y", "zl", "h"), ("zh", "x"), None)
    return jax.shard_map(
        shards,
        mesh=Mesh(devices, tuple(SIZES)),
        in_specs=(split, split) + (P(),) * 8,
        out_specs=(split, split, P(), P(), P()),
        check_vma=False,
    )
```

```python
import functools

import jax
import jax.numpy as jnp
from jax import lax
from jax.experimental import pallas as pl
from jax.experimental.pallas import tpu as pltpu
from jax.sharding import Mesh, PartitionSpec as P

F32 = jnp.float32
BF16 = jnp.bfloat16
POS = 256
CH = 128
EPS = 1e-05
SIZES = {"y": 4, "zl": 2, "h": 2, "zh": 4, "x": 4}
CHIPS = ("zh", "x", "y", "zl")
PLANE = ("x", "y")
LINE = ("zl", "zh")


def dot(a, b, ca, cb):
    return lax.dot_general(
        a.astype(BF16), b.astype(BF16), (((ca,), (cb,)), ((), ())), preferred_element_type=F32
    )


def swap_blocks(tiles):
    block = lax.broadcasted_iota(jnp.int32, tiles[0].shape, 1) // 16
    high = block >= 4
    out = list(tiles)
    for t in range(4):
        lo, hi = tiles[t], tiles[t + 4]
        crossed = pltpu.roll(jnp.where(high, lo, hi), 64, 1)
        out[t] = jnp.where(high, crossed, lo)
        out[t + 4] = jnp.where(high, hi, crossed)
    tiles, out = out, []
    for i in range(8):
        value = tiles[i]
        for t in range(4):
            if t != i % 4:
                moved = pltpu.roll(tiles[i - i % 4 + t], 16 * (t - i % 4) % 128, 1)
                value = jnp.where(block % 4 == t, moved, value)
        out.append(value)
    return out


def messages_to_half(src, off, w, dst):
    for half in range(2):
        tiles = [
            src[pl.ds(16 * t * w + off + half, 16, stride=w), :].astype(BF16) for t in range(8)
        ]
        for t, tile in enumerate(swap_blocks(tiles)):
            tile = tile.astype(F32)
            for p in range(2):
                dst[p, pl.ds(half * 8 + t, 8, stride=16), :] = tile[8 * p : 8 * (p + 1)]
    return jnp.concatenate([dst[0], dst[1]], axis=1).astype(BF16)


def half_to_messages(value, src, dst, off, w):
    for p in range(2):
        src[p] = value[p]
    for half in range(2):
        tiles = []
        for t in range(8):
            both = [src[p, pl.ds(half * 8 + t, 8, stride=16), :] for p in range(2)]
            tiles.append(jnp.concatenate(both, axis=0).astype(BF16))
        for t, tile in enumerate(swap_blocks(tiles)):
            dst[pl.ds(16 * t * w + off + half, 16, stride=w), :] = tile.astype(F32)


def halves(value):
    return value[:, 0:128], value[:, 128:256]


def by_parity(mine, other):
    first = lax.axis_index("h") == 0
    return jnp.where(first, mine, other), jnp.where(first, other, mine)


def own_columns(value):
    return by_parity(*halves(value))[0]


def other_columns(value):
    return by_parity(*halves(value))[1]


def channels_to_messages(v, dst, off, w):
    for half in range(2):
        dst[pl.ds(off + half, CH, stride=w), :] = v[:, half * 128 : (half + 1) * 128]


def messages_to_channels(src, off, w):
    return jnp.concatenate(
        [src[pl.ds(off + half, CH, stride=w), :] for half in range(2)], axis=1
    )


def column(row):
    square = jnp.broadcast_to(row, (CH, CH)).T
    return jnp.concatenate([square, square], axis=1)


def normalise(z):
    centered = z - jnp.mean(z, axis=0, keepdims=True)
    rstd = lax.rsqrt(jnp.mean(centered * centered, axis=0, keepdims=True) + EPS)
    return centered * rstd, rstd


def normalise_back(cot, hat, rstd):
    return rstd * (
        cot
        - jnp.mean(cot, axis=0, keepdims=True)
        - hat * jnp.mean(cot * hat, axis=0, keepdims=True)
    )


def prepare(z, gain, w_in, m, n_ref, send, send_ref, copies=()):
    hat, rstd = normalise(z)
    normed = (hat * gain).astype(BF16)
    n_ref[...] = normed
    for copy in copies:
        copy.wait()
    p = dot(w_in[...], normed, 0, 0)
    a = m * jax.nn.sigmoid(p[0:128]) * p[128:256]
    b = m * jax.nn.sigmoid(p[256:384]) * p[384:512]
    channels_to_messages(a, send, 0, 4)
    channels_to_messages(b, send, 2, 4)
    send_ref[...] = send[...].astype(BF16)
    return hat, rstd


def project_back(recv, factors, dp):
    for k in range(2):
        cot = messages_to_channels(recv, 2 * k, 4)
        for e in range(2 * k, 2 * k + 2):
            block = slice(128 * e, 128 * (e + 1))
            dp[block, :] = (cot * factors[block, :]).astype(BF16)


def normed_back(dp, hat, rstd, gain, w_in, w_gate, dpg):
    dn = dot(w_in, dp[...], 1, 0) + dot(w_gate, dpg, 1, 0)
    return normalise_back(dn * gain, hat, rstd)


def start_kernel(*refs):
    hbm, (z_ref, n_ref, m_ref, gain_ref, w_in, w_gate, send_ref), refs = refs[:8], refs[8:15], refs[15:]
    vmem, send, sem = refs[:6] + (w_in, w_gate), refs[6], refs[7]
    copies = [
        pltpu.make_async_copy(src.at[0] if k > 5 else src, dst, sem.at[k])
        for k, (src, dst) in enumerate(zip(hbm, vmem))
    ]
    for copy in copies:
        copy.start()
    pair, mask, chain, bias, in_gain, out_gain = vmem[:6]
    row = (lax.axis_index("y") * 2 + lax.axis_index("zl")) * 2 + lax.axis_index("h")
    col = lax.axis_index("zh") * 4 + lax.axis_index("x")
    res = lax.broadcasted_iota(jnp.int32, (256, POS), 0)
    pos = lax.broadcasted_iota(jnp.int32, (256, POS), 1)
    in_row = (res == row * 16 + pos // 16).astype(F32)
    in_col = (res == col * 16 + pos % 16).astype(F32)
    for copy in copies[:6]:
        copy.wait()
    both = jnp.concatenate(
        [
            jnp.broadcast_to(mask[...].astype(F32), (8, 256)),
            jnp.broadcast_to(chain[...].astype(F32), (8, 256)),
        ],
        axis=0,
    )
    of_row = dot(both, in_row, 1, 0)
    of_col = dot(both, in_col, 1, 0)
    m8 = of_row[0:8] * of_col[0:8]
    m_ref[...] = m8
    gain_ref[0:2, :] = in_gain[...]
    gain_ref[2:4, :] = out_gain[...]
    same = (of_row[8:9] == of_col[8:9]).astype(F32)
    z = pair[...].astype(F32).T + same * column(bias[...])
    z_ref[...] = z
    gain = column(in_gain[0:1])
    prepare(z, gain, w_in, m8[0:1], n_ref, send, send_ref, copies[6:7])
    copies[7].wait()


def side_kernel(normed, m, w_in, w_gate, g_ref, factor_ref):
    p = dot(w_in[...], normed[...], 0, 0)
    for k in range(2):
        s = jax.nn.sigmoid(p[256 * k : 256 * k + 128])
        ms = m[0:1] * s
        factor_ref[256 * k : 256 * k + 128, :] = ms * (1.0 - s) * p[256 * k + 128 : 256 * k + 256]
        factor_ref[256 * k + 128 : 256 * k + 256, :] = ms
    g_ref[...] = jax.nn.sigmoid(dot(w_gate[...], normed[...], 0, 0))


def columns_kernel(gains, col_ref):
    for k in range(4):
        col_ref[k] = column(gains[k : k + 1])


def middle_kernel(x_in, z0, g0, m, gains, w_in, w_gate, w_out, z_ref, y_ref, n_ref, w_in_ref, w_gate_ref, hats_ref, rstd_ref, xn_ref, send_ref, xs, send):
    w_in_ref[...] = w_in[1]
    w_gate_ref[...] = w_gate[1]
    xs[...] = x_in[...].astype(F32)
    hat, rstd = normalise(messages_to_channels(xs, 0, 2))
    xn = (hat * gains[2]).astype(BF16)
    y = dot(w_out[0], xn, 0, 0)
    y_ref[...] = y
    z = z0[...] + g0[...] * y
    z_ref[...] = z
    hats_ref[0] = hat
    xn_ref[...] = xn
    rstd_ref[0:8, :] = jnp.broadcast_to(rstd, (8, POS))
    hat, rstd = prepare(z, gains[1], w_in.at[1], m[0:1], n_ref, send, send_ref)
    hats_ref[1] = hat
    rstd_ref[8:16, :] = jnp.broadcast_to(rstd, (8, POS))


def turn_kernel(x_in, g1, cot_in, gains, w_out, cot_ref, y_ref, xn_ref, dy_ref, dpg_ref, send_ref, xs, send):
    xs[...] = x_in[...].astype(F32)
    gain = gains[3]
    hat, rstd = normalise(messages_to_channels(xs, 0, 2))
    xn = (hat * gain).astype(BF16)
    xn_ref[...] = xn
    y = dot(w_out[1], xn, 0, 0)
    y_ref[...] = y
    g = g1[...]
    cot = cot_in[...].astype(F32).T
    cot_ref[...] = cot
    dy = (cot * g).astype(BF16)
    dy_ref[...] = dy
    dpg_ref[...] = (cot * y * g * (1.0 - g)).astype(BF16)
    gx = normalise_back(dot(w_out[1], dy, 1, 0) * gain, hat, rstd)
    channels_to_messages(gx, send, 0, 2)
    send_ref[...] = send[...].astype(BF16)


def turn_rest_kernel(z1, y1, g1, n1, xn, dy, dpg, new_ref, gw_ref):
    new_ref[...] = (z1[...] + g1[...] * y1[...]).T.astype(BF16)
    gw_ref[0:128, :] = dot(n1[...], dpg[...], 1, 1).astype(BF16)
    gw_ref[128:256, :] = dot(xn[...], dy[...], 1, 1).astype(BF16)


def back_kernel(gab, factors, hats, rstds, dpg1, cot, g0, y0, gains, w_in, w_gate, w_out, dz_ref, dp_ref, dpg_ref, dy_ref, send_ref, rs, send):
    rs[...] = gab[...].astype(F32)
    project_back(rs, factors, dp_ref)
    dz = cot[...] + normed_back(
        dp_ref, hats[1], rstds[8:9], gains[1], w_in[1], w_gate[1], dpg1[...]
    )
    dz_ref[...] = dz
    g = g0[...]
    dpg_ref[...] = (dz * y0[...] * g * (1.0 - g)).astype(BF16)
    dy = (dz * g).astype(BF16)
    dy_ref[...] = dy
    gx = normalise_back(dot(w_out[0], dy, 1, 0) * gains[2], hats[0], rstds[0:1])
    channels_to_messages(gx, send, 0, 2)
    send_ref[...] = send[...].astype(BF16)


def back_rest_kernel(n1, dp1, gw1, n0, dpg0, xn, dy, early_ref):
    for e in range(4):
        block = slice(128 * e, 128 * (e + 1))
        early_ref[block, :] = dot(n1[...], dp1[block, :], 1, 1).astype(BF16)
    early_ref[512:768, :] = gw1[...]
    early_ref[768:896, :] = dot(n0[...], dpg0[...], 1, 1).astype(BF16)
    early_ref[896:1024, :] = dot(xn[...], dy[...], 1, 1).astype(BF16)


def end_kernel(gab, factors, n0, early, dp_ref, mine_ref, send_ref, rs):
    rs[...] = gab[...].astype(F32)
    project_back(rs, factors, dp_ref)
    first = lax.axis_index("h") == 0
    parts = [dot(n0[...], dp_ref[128 * e : 128 * (e + 1), :], 1, 1) for e in range(4)]
    parts += [early[128 * k : 128 * (k + 1), :].astype(F32) for k in range(8)]
    for k, (low, high) in enumerate([(0, 2), (1, 3), (4, 8), (5, 9), (6, 10), (7, 11)]):
        block = slice(128 * k, 128 * (k + 1))
        mine_ref[block, :] = jnp.where(first, parts[low], parts[high])
        send_ref[block, :] = jnp.where(first, parts[high], parts[low]).astype(BF16)


def end_rest_kernel(dp, z0, dpg0, dz1, gains, w_in, w_gate, grad_ref):
    dz = dz1[...] + normed_back(
        dp, *normalise(z0[...]), gains[0], w_in[0], w_gate[0], dpg0[...]
    )
    grad_ref[...] = dz.T


def core_sum_kernel(mine, other, send_ref):
    send_ref[...] = (mine[...] + other[...].astype(F32)).astype(BF16)


def sum_kernel(recv, send_ref):
    total = recv[0:48, :].astype(F32)
    for k in range(1, recv.shape[0] // 48):
        total = total + recv[48 * k : 48 * (k + 1), :].astype(F32)
    total = total.astype(BF16)
    for k in range(send_ref.shape[0] // 48):
        send_ref[48 * k : 48 * (k + 1), :] = total


def place_kernel(core_of, rows, *refs):
    in_out, gate_out, out_out, in_ref, gate_ref, out_ref, sem = refs[-7:]

    def block(k):
        return rows[128 * k : 128 * (k + 1), :].astype(F32)

    def write(src, dst, k):
        copy = pltpu.make_async_copy(src, dst, sem.at[k])
        copy.start()
        return copy

    def low():
        for e in range(2):
            in_ref[0, :, 128 * e : 128 * (e + 1)] = block(e)
        copies = [write(in_ref.at[0, :, 0:256], in_out.at[0, :, 0:256], 0)]
        for e in range(4):
            in_ref[1, :, 128 * e : 128 * (e + 1)] = block(2 + e)
        copies.append(write(in_ref.at[1], in_out.at[1], 1))
        for copy in copies:
            copy.wait()

    def high():
        for e in range(2):
            in_ref[0, :, 128 * (2 + e) : 128 * (3 + e)] = block(e)
        copies = [write(in_ref.at[0, :, 256:512], in_out.at[0, :, 256:512], 0)]
        for k, u in ((2, 1), (4, 0)):
            gate_ref[u] = block(k)
            out_ref[u] = block(k + 1)
        copies += [write(gate_ref, gate_out, 1), write(out_ref, out_out, 2)]
        for copy in copies:
            copy.wait()

    is_low = lax.axis_index("h") == core_of
    pl.when(is_low)(low)
    pl.when(jnp.logical_not(is_low))(high)


def outgoing_mine_kernel(mine, a_ref, b_ref, x_ref, ms, mat):
    ms[...] = mine[...].astype(F32)
    a, b = messages_to_half(ms, 0, 4, mat), messages_to_half(ms, 2, 4, mat)
    a_ref[...] = a
    b_ref[...] = b
    x_ref[...] = dot(a, b, 1, 1)


def outgoing_kernel(other, a, x_mine, b_ref, send_ref, os, mat, send):
    os[...] = other[...].astype(F32)
    b = messages_to_half(os, 2, 4, mat)
    b_ref[...] = b
    half_to_messages(by_parity(x_mine[...], dot(a[...], b, 1, 1)), mat, send, 0, 2)
    send_ref[...] = send[...].astype(BF16)


def incoming_mine_kernel(mine, a_ref, b_ref, x_ref, ms, mat):
    ms[...] = mine[...].astype(F32)
    a, b = messages_to_half(ms, 0, 4, mat), messages_to_half(ms, 2, 4, mat)
    a_ref[...] = a
    b_ref[...] = b
    x_ref[...] = dot(own_columns(a), b, 0, 0)


def incoming_kernel(other, x_mine, send_ref, os, mat, send):
    os[...] = other[...].astype(F32)
    a, b = messages_to_half(os, 0, 4, mat), messages_to_half(os, 2, 4, mat)
    half_to_messages(halves(x_mine[...] + dot(own_columns(a), b, 0, 0)), mat, send, 0, 2)
    send_ref[...] = send[...].astype(BF16)


def incoming_back_mine_kernel(mine, a, b, ga_ref, gb_ref, ms, mat):
    ms[...] = mine[...].astype(F32)
    gx = messages_to_half(ms, 0, 2, mat)
    ga_ref[...] = dot(b[...], gx, 1, 1)
    gb_ref[...] = dot(own_columns(a[...]), gx, 1, 0)


def incoming_back_kernel(other, a, b, ga_mine, gb_mine, send_ref, os, mat, send):
    os[...] = other[...].astype(F32)
    gx = messages_to_half(os, 0, 2, mat)
    half_to_messages(by_parity(ga_mine[...], dot(b[...], gx, 1, 1)), mat, send, 0, 4)
    gb = gb_mine[...] + dot(other_columns(a[...]), gx, 1, 0)
    half_to_messages(halves(gb), mat, send, 2, 4)
    send_ref[...] = send[...].astype(BF16)


def other_rows_kernel(other_ab, a_ref, os, mat):
    os[...] = other_ab[...].astype(F32)
    a_ref[...] = messages_to_half(os, 0, 4, mat)


def outgoing_back_mine_kernel(mine, a, b, b_other, ga_ref, gb_ref, ms, mat, send):
    ms[...] = mine[...].astype(F32)
    gx = messages_to_half(ms, 0, 2, mat)
    even, odd = by_parity(b[...], b_other[...])
    ga = dot(gx, jnp.concatenate([even, odd], axis=0), 1, 0)
    half_to_messages(halves(ga), mat, send, 0, 2)
    ga_ref[...] = send[...]
    gb_ref[...] = dot(own_columns(gx), a[...], 0, 0)


def outgoing_back_kernel(other, ga, gb_mine, a_other, send_ref, os, mat, send):
    os[...] = other[...].astype(F32)
    gx = messages_to_half(os, 0, 2, mat)
    gb = gb_mine[...] + dot(own_columns(gx), a_other[...], 0, 0)
    half_to_messages(halves(gb), mat, send, 2, 4)
    for half in range(2):
        send[pl.ds(half, CH, stride=4), :] = ga[pl.ds(half, CH, stride=2), :]
    send_ref[...] = send[...].astype(BF16)


def call(kernel, name, outs, scratch, *args, **kwargs):
    return pl.pallas_call(
        kernel,
        name=name,
        out_shape=[jax.ShapeDtypeStruct(s, d) for s, d in outs],
        scratch_shapes=[s if not isinstance(s, tuple) else pltpu.VMEM(*s) for s in scratch],
        compiler_params=pltpu.CompilerParams(vmem_limit_bytes=24 * 1024 * 1024),
        cost_estimate=pl.CostEstimate(flops=2**24, bytes_accessed=2**20, transcendentals=0),
        **kwargs,
    )(*args)


def exchange(value, axes=CHIPS):
    return lax.all_to_all(value, axes, 0, 0, tiled=True)


def swap_cores(value):
    return lax.ppermute(value, "h", [(0, 1), (1, 0)])


def after(done, *values):
    return lax.optimization_barrier((done,) + values)[1:]


def shards(pair, pair_cot, mask, chain_ids, chain_bias, w_in, w_gate, w_out, in_gain, out_gain):
    block = pair.shape
    pair = pair.reshape(POS, CH)
    cot_in = pair_cot.reshape(POS, CH)
    mask, chain, bias = mask[None, :], chain_ids[None, :], chain_bias[None, :]
    field, field16 = ((CH, POS), F32), ((CH, POS), BF16)
    square, work = ((128, 128), F32), ((2, 128, 128), F32)

    def rows(n, dtype=F32):
        return ((n, 128), dtype)

    operands = [
        pltpu.with_memory_space_constraint(v, pltpu.HBM)
        for v in (pair, mask, chain, bias, in_gain, out_gain, w_in, w_gate)
    ]
    z0, n0, m, gains, w_in0, w_gate0, send = call(
        start_kernel, "start",
        [field, field16, ((8, POS), F32), rows(4), ((128, 512), BF16), rows(128, BF16), rows(512, BF16)],
        [(v.shape, v.dtype) for v in operands[:6]] + [rows(512), pltpu.SemaphoreType.DMA((8,))],
        *operands, in_specs=[pl.BlockSpec(memory_space=pltpu.HBM)] * 8,
    )
    mine = exchange(send)
    other_ab = swap_cores(mine)
    a0, b0, x_mine = call(
        outgoing_mine_kernel, "outgoing_mine", [field16, field16, square], [rows(512), work], mine
    )
    factors = ((512, POS), F32)
    g0, factors0 = call(
        side_kernel, "side0", [field, factors], [], *after(mine, n0), m, w_in0, w_gate0
    )
    (gains,) = call(columns_kernel, "columns", [((4, CH, POS), F32)], [], *after(mine, gains))
    b0_other, send = call(
        outgoing_kernel, "outgoing", [field16, rows(256, BF16)], [rows(512), work, rows(256)],
        other_ab, a0, *after((g0, gains), x_mine),
    )
    x0 = exchange(send)
    z1, y0, n1, w_in1, w_gate1, hats, rstds, xn0, send = call(
        middle_kernel, "middle", [field, field, field16, ((128, 512), BF16), rows(128, BF16), ((2, CH, POS), F32), ((16, POS), F32),
         field16, rows(512, BF16)],
        [rows(256), rows(512)], x0, z0, g0, m, gains, w_in, w_gate, w_out,
    )
    mine = exchange(send)
    other = swap_cores(mine)
    a1, b1, x_mine = call(
        incoming_mine_kernel, "incoming_mine", [field16, field16, field], [rows(512), work], mine
    )
    (a0_other,) = call(
        other_rows_kernel, "other_rows", [field16], [rows(512), work], *after(mine, other_ab)
    )
    g1, factors1 = call(
        side_kernel, "side1", [field, factors], [], *after(mine, n1), m, w_in1, w_gate1
    )
    (send,) = call(
        incoming_kernel, "incoming", [rows(256, BF16)], [rows(512), work, rows(256)],
        other, *after((a0_other, g1), x_mine),
    )
    cot, y1, xn, dy, dpg1, send = call(
        turn_kernel, "turn", [field, field, field16, field16, field16, rows(256, BF16)],
        [rows(256), rows(256)], exchange(send), g1, cot_in, gains, w_out,
    )
    mine = exchange(send)
    other = swap_cores(mine)
    ga, gb = call(
        incoming_back_mine_kernel, "incoming_back_mine", [square, field], [rows(256), work], mine, a1, b1
    )
    new_pair, gw1 = call(
        turn_rest_kernel, "turn_rest", [rows(POS, BF16), rows(256, BF16)], [],
        *after(mine, z1, y1, g1, n1, xn, dy, dpg1),
    )
    (send,) = call(
        incoming_back_kernel, "incoming_back", [rows(512, BF16)], [rows(256), work, rows(512)],
        other, a1, b1, *after(gw1, ga, gb),
    )
    dz1, dp1, dpg0, dy, send = call(
        back_kernel, "back", [field, ((512, POS), BF16), field16, field16, rows(256, BF16)],
        [rows(512), rows(256)],
        exchange(send), factors1, hats, rstds, dpg1, cot, g0, y0, gains, w_in, w_gate, w_out,
    )
    mine = exchange(send)
    other = swap_cores(mine)
    ga, gb = call(
        outgoing_back_mine_kernel, "outgoing_back_mine", [rows(256), field],
        [rows(256), work, rows(256)], mine, a0, b0, b0_other,
    )
    (early,) = call(
        back_rest_kernel, "back_rest", [rows(1024, BF16)], [], *after(mine, n1, dp1, gw1, n0, dpg0, xn0, dy)
    )
    (send,) = call(
        outgoing_back_kernel, "outgoing_back", [rows(512, BF16)], [rows(256), work, rows(512)],
        other, *after(early, ga, gb), a0_other,
    )
    dp0, mine, send = call(
        end_kernel, "end", [((512, POS), BF16), rows(768), rows(768, BF16)], [rows(512)],
        exchange(send), factors0, n0, early,
    )
    other = swap_cores(send)
    (pair_grad,) = call(
        end_rest_kernel, "end_rest", [rows(POS)], [], dp0, z0, dpg0, dz1, gains, w_in, w_gate
    )
    (send,) = call(
        core_sum_kernel, "core_sum", [rows(768, BF16)], [], *after(pair_grad, mine), other
    )
    (send,) = call(sum_kernel, "plane_sum", [rows(384, BF16)], [], exchange(send, PLANE))
    (send,) = call(sum_kernel, "line_sum", [rows(768, BF16)], [], exchange(send, LINE))
    mine = exchange(send, PLANE)
    weights = [((2, 128, 512), F32), ((2, 128, 128), F32), ((2, 128, 128), F32)]
    hbm = [pl.BlockSpec(memory_space=pltpu.HBM)] * 3
    scratch = weights + [pltpu.SemaphoreType.DMA((3,))]
    other = swap_cores(mine)
    grads = call(
        functools.partial(place_kernel, 0), "place_mine", weights, scratch, mine, out_specs=hbm
    )
    in_grad, gate_grad, out_grad = call(
        functools.partial(place_kernel, 1), "place_other", weights, scratch, other, *grads,
        in_specs=[pl.BlockSpec(memory_space=pltpu.VMEM)] + hbm, out_specs=hbm,
        input_output_aliases={1: 0, 2: 1, 3: 2},
    )
    return (new_pair.reshape(block), pair_grad.reshape(block), in_grad, gate_grad, out_grad)


def solution(mesh):
    devices = mesh.devices.reshape(tuple(SIZES.values()))
    split = P(("y", "zl", "h"), ("zh", "x"), None)
    return jax.shard_map(
        shards,
        mesh=Mesh(devices, tuple(SIZES)),
        in_specs=(split, split) + (P(),) * 8,
        out_specs=(split, split, P(), P(), P()),
        check_vma=False,
    )
```

```python
import functools

import jax
import jax.numpy as jnp
from jax import lax
from jax.experimental import pallas as pl
from jax.experimental.pallas import tpu as pltpu
from jax.sharding import Mesh, PartitionSpec as P

F32 = jnp.float32
BF16 = jnp.bfloat16
POS = 256
CH = 128
EPS = 1e-05
SIZES = {"y": 4, "zl": 2, "h": 2, "zh": 4, "x": 4}
CHIPS = ("zh", "x", "y", "zl")
PLANE = ("x", "y")
LINE = ("zl", "zh")


def dot(a, b, ca, cb):
    return lax.dot_general(
        a.astype(BF16), b.astype(BF16), (((ca,), (cb,)), ((), ())), preferred_element_type=F32
    )


def swap_blocks(tiles):
    block = lax.broadcasted_iota(jnp.int32, tiles[0].shape, 1) // 16
    high = block >= 4
    out = list(tiles)
    for t in range(4):
        lo, hi = tiles[t], tiles[t + 4]
        crossed = pltpu.roll(jnp.where(high, lo, hi), 64, 1)
        out[t] = jnp.where(high, crossed, lo)
        out[t + 4] = jnp.where(high, hi, crossed)
    tiles, out = out, []
    for i in range(8):
        value = tiles[i]
        for t in range(4):
            if t != i % 4:
                moved = pltpu.roll(tiles[i - i % 4 + t], 16 * (t - i % 4) % 128, 1)
                value = jnp.where(block % 4 == t, moved, value)
        out.append(value)
    return out


def messages_to_half(src, off, w, dst):
    for half in range(2):
        tiles = [
            src[pl.ds(16 * t * w + off + half, 16, stride=w), :].astype(BF16) for t in range(8)
        ]
        for t, tile in enumerate(swap_blocks(tiles)):
            tile = tile.astype(F32)
            for p in range(2):
                dst[p, pl.ds(half * 8 + t, 8, stride=16), :] = tile[8 * p : 8 * (p + 1)]
    return jnp.concatenate([dst[0], dst[1]], axis=1).astype(BF16)


def half_to_messages(value, src, dst, off, w):
    for p in range(2):
        src[p] = value[p]
    for half in range(2):
        tiles = []
        for t in range(8):
            both = [src[p, pl.ds(half * 8 + t, 8, stride=16), :] for p in range(2)]
            tiles.append(jnp.concatenate(both, axis=0).astype(BF16))
        for t, tile in enumerate(swap_blocks(tiles)):
            dst[pl.ds(16 * t * w + off + half, 16, stride=w), :] = tile.astype(F32)


def halves(value):
    return value[:, 0:128], value[:, 128:256]


def by_parity(mine, other):
    first = lax.axis_index("h") == 0
    return jnp.where(first, mine, other), jnp.where(first, other, mine)


def own_columns(value):
    return by_parity(*halves(value))[0]


def other_columns(value):
    return by_parity(*halves(value))[1]


def channels_to_messages(v, dst, off, w):
    for half in range(2):
        dst[pl.ds(off + half, CH, stride=w), :] = v[:, half * 128 : (half + 1) * 128]


def messages_to_channels(src, off, w):
    return jnp.concatenate(
        [src[pl.ds(off + half, CH, stride=w), :] for half in range(2)], axis=1
    )


def column(row):
    square = jnp.broadcast_to(row, (CH, CH)).T
    return jnp.concatenate([square, square], axis=1)


def normalise(z):
    centered = z - jnp.mean(z, axis=0, keepdims=True)
    rstd = lax.rsqrt(jnp.mean(centered * centered, axis=0, keepdims=True) + EPS)
    return centered * rstd, rstd


def normalise_back(cot, hat, rstd):
    return rstd * (
        cot
        - jnp.mean(cot, axis=0, keepdims=True)
        - hat * jnp.mean(cot * hat, axis=0, keepdims=True)
    )


def prepare(z, gain, w_in, m, n_ref, send, send_ref, copies=()):
    hat, rstd = normalise(z)
    normed = (hat * gain).astype(BF16)
    n_ref[...] = normed
    for copy in copies:
        copy.wait()
    p = dot(w_in[...], normed, 0, 0)
    a = m * jax.nn.sigmoid(p[0:128]) * p[128:256]
    b = m * jax.nn.sigmoid(p[256:384]) * p[384:512]
    channels_to_messages(a, send, 0, 4)
    channels_to_messages(b, send, 2, 4)
    send_ref[...] = send[...].astype(BF16)
    return hat, rstd


def project_back(recv, factors, dp):
    for k in range(2):
        cot = messages_to_channels(recv, 2 * k, 4)
        for e in range(2 * k, 2 * k + 2):
            block = slice(128 * e, 128 * (e + 1))
            dp[block, :] = (cot * factors[block, :]).astype(BF16)


def normed_back(dp, hat, rstd, gain, w_in, w_gate, dpg):
    dn = dot(w_in, dp[...], 1, 0) + dot(w_gate, dpg, 1, 0)
    return normalise_back(dn * gain, hat, rstd)


def start_kernel(*refs):
    hbm, (z_ref, n_ref, m_ref, gain_ref, w_in, w_gate, send_ref), refs = refs[:8], refs[8:15], refs[15:]
    vmem, send, sem = refs[:6] + (w_in, w_gate), refs[6], refs[7]
    copies = [
        pltpu.make_async_copy(src.at[0] if k > 5 else src, dst, sem.at[k])
        for k, (src, dst) in enumerate(zip(hbm, vmem))
    ]
    for copy in copies:
        copy.start()
    pair, mask, chain, bias, in_gain, out_gain = vmem[:6]
    row = (lax.axis_index("y") * 2 + lax.axis_index("zl")) * 2 + lax.axis_index("h")
    col = lax.axis_index("zh") * 4 + lax.axis_index("x")
    res = lax.broadcasted_iota(jnp.int32, (256, POS), 0)
    pos = lax.broadcasted_iota(jnp.int32, (256, POS), 1)
    in_row = (res == row * 16 + pos // 16).astype(F32)
    in_col = (res == col * 16 + pos % 16).astype(F32)
    for copy in copies[:6]:
        copy.wait()
    both = jnp.concatenate(
        [
            jnp.broadcast_to(mask[...].astype(F32), (8, 256)),
            jnp.broadcast_to(chain[...].astype(F32), (8, 256)),
        ],
        axis=0,
    )
    of_row = dot(both, in_row, 1, 0)
    of_col = dot(both, in_col, 1, 0)
    m8 = of_row[0:8] * of_col[0:8]
    m_ref[...] = m8
    gain_ref[0:2, :] = in_gain[...]
    gain_ref[2:4, :] = out_gain[...]
    same = (of_row[8:9] == of_col[8:9]).astype(F32)
    z = pair[...].astype(F32).T + same * column(bias[...])
    z_ref[...] = z
    gain = column(in_gain[0:1])
    prepare(z, gain, w_in, m8[0:1], n_ref, send, send_ref, copies[6:7])
    copies[7].wait()


def side_kernel(normed, m, w_in, w_gate, g_ref, factor_ref):
    p = dot(w_in[...], normed[...], 0, 0)
    for k in range(2):
        s = jax.nn.sigmoid(p[256 * k : 256 * k + 128])
        ms = m[0:1] * s
        factor_ref[256 * k : 256 * k + 128, :] = ms * (1.0 - s) * p[256 * k + 128 : 256 * k + 256]
        factor_ref[256 * k + 128 : 256 * k + 256, :] = ms
    g_ref[...] = jax.nn.sigmoid(dot(w_gate[...], normed[...], 0, 0))


def columns_kernel(gains, col_ref):
    for k in range(4):
        col_ref[k] = column(gains[k : k + 1])


def middle_kernel(x_in, z0, g0, m, gains, w_in, w_gate, w_out, z_ref, y_ref, n_ref, w_in_ref, w_gate_ref, hats_ref, rstd_ref, xn_ref, send_ref, xs, send):
    w_in_ref[...] = w_in[1]
    w_gate_ref[...] = w_gate[1]
    xs[...] = x_in[...].astype(F32)
    hat, rstd = normalise(messages_to_channels(xs, 0, 2))
    xn = (hat * gains[2]).astype(BF16)
    y = dot(w_out[0], xn, 0, 0)
    y_ref[...] = y
    z = z0[...] + g0[...] * y
    z_ref[...] = z
    hats_ref[0] = hat
    xn_ref[...] = xn
    rstd_ref[0:8, :] = jnp.broadcast_to(rstd, (8, POS))
    hat, rstd = prepare(z, gains[1], w_in.at[1], m[0:1], n_ref, send, send_ref)
    hats_ref[1] = hat
    rstd_ref[8:16, :] = jnp.broadcast_to(rstd, (8, POS))


def turn_kernel(x_in, g1, cot_in, gains, w_out, cot_ref, y_ref, xn_ref, dy_ref, dpg_ref, send_ref, xs, send):
    xs[...] = x_in[...].astype(F32)
    gain = gains[3]
    hat, rstd = normalise(messages_to_channels(xs, 0, 2))
    xn = (hat * gain).astype(BF16)
    xn_ref[...] = xn
    y = dot(w_out[1], xn, 0, 0)
    y_ref[...] = y
    g = g1[...]
    cot = cot_in[...].astype(F32).T
    cot_ref[...] = cot
    dy = (cot * g).astype(BF16)
    dy_ref[...] = dy
    dpg_ref[...] = (cot * y * g * (1.0 - g)).astype(BF16)
    gx = normalise_back(dot(w_out[1], dy, 1, 0) * gain, hat, rstd)
    channels_to_messages(gx, send, 0, 2)
    send_ref[...] = send[...].astype(BF16)


def turn_rest_kernel(z1, y1, g1, n1, xn, dy, dpg, new_ref, gw_ref):
    new_ref[...] = (z1[...] + g1[...] * y1[...]).T.astype(BF16)
    gw_ref[0:128, :] = dot(n1[...], dpg[...], 1, 1).astype(BF16)
    gw_ref[128:256, :] = dot(xn[...], dy[...], 1, 1).astype(BF16)


def back_kernel(gab, factors, hats, rstds, dpg1, cot, g0, y0, gains, w_in, w_gate, w_out, dz_ref, dp_ref, dpg_ref, dy_ref, send_ref, rs, send):
    rs[...] = gab[...].astype(F32)
    project_back(rs, factors, dp_ref)
    dz = cot[...] + normed_back(
        dp_ref, hats[1], rstds[8:9], gains[1], w_in[1], w_gate[1], dpg1[...]
    )
    dz_ref[...] = dz
    g = g0[...]
    dpg_ref[...] = (dz * y0[...] * g * (1.0 - g)).astype(BF16)
    dy = (dz * g).astype(BF16)
    dy_ref[...] = dy
    gx = normalise_back(dot(w_out[0], dy, 1, 0) * gains[2], hats[0], rstds[0:1])
    channels_to_messages(gx, send, 0, 2)
    send_ref[...] = send[...].astype(BF16)


def back_rest_kernel(n1, dp1, gw1, n0, dpg0, xn, dy, early_ref):
    for e in range(4):
        block = slice(128 * e, 128 * (e + 1))
        early_ref[block, :] = dot(n1[...], dp1[block, :], 1, 1).astype(BF16)
    early_ref[512:768, :] = gw1[...]
    early_ref[768:896, :] = dot(n0[...], dpg0[...], 1, 1).astype(BF16)
    early_ref[896:1024, :] = dot(xn[...], dy[...], 1, 1).astype(BF16)


def end_kernel(gab, factors, n0, early, dp_ref, mine_ref, send_ref, rs):
    rs[...] = gab[...].astype(F32)
    project_back(rs, factors, dp_ref)
    first = lax.axis_index("h") == 0
    parts = [dot(n0[...], dp_ref[128 * e : 128 * (e + 1), :], 1, 1) for e in range(4)]
    parts += [early[128 * k : 128 * (k + 1), :].astype(F32) for k in range(8)]
    for k, (low, high) in enumerate([(0, 2), (1, 3), (4, 8), (5, 9), (6, 10), (7, 11)]):
        block = slice(128 * k, 128 * (k + 1))
        mine_ref[block, :] = jnp.where(first, parts[low], parts[high])
        send_ref[block, :] = jnp.where(first, parts[high], parts[low]).astype(BF16)


def end_rest_kernel(dp, z0, dpg0, dz1, gains, w_in, w_gate, grad_ref):
    dz = dz1[...] + normed_back(
        dp, *normalise(z0[...]), gains[0], w_in[0], w_gate[0], dpg0[...]
    )
    grad_ref[...] = dz.T


def core_sum_kernel(mine, other, send_ref):
    send_ref[...] = (mine[...] + other[...].astype(F32)).astype(BF16)


def sum_kernel(recv, send_ref):
    total = recv[0:48, :].astype(F32)
    for k in range(1, recv.shape[0] // 48):
        total = total + recv[48 * k : 48 * (k + 1), :].astype(F32)
    total = total.astype(BF16)
    for k in range(send_ref.shape[0] // 48):
        send_ref[48 * k : 48 * (k + 1), :] = total


def place_kernel(rows, in_out, gate_out, out_out, in_ref, gate_ref, out_ref, sem):
    copies = []

    def write(src, dst):
        copies.append(pltpu.make_async_copy(src, dst, sem.at[len(copies)]))
        copies[-1].start()

    def block(k):
        return rows[128 * k : 128 * (k + 1), :].astype(F32)

    for u, blocks in enumerate(((0, 1, 6, 7), (2, 3, 4, 5))):
        for e, k in enumerate(blocks):
            in_ref[u, :, 128 * e : 128 * (e + 1)] = block(k)
        write(in_ref.at[u], in_out.at[u])
    for k, u in ((8, 1), (10, 0)):
        gate_ref[u] = block(k)
        out_ref[u] = block(k + 1)
    write(gate_ref, gate_out)
    write(out_ref, out_out)
    for copy in copies:
        copy.wait()


def outgoing_mine_kernel(mine, a_ref, b_ref, x_ref, ms, mat):
    ms[...] = mine[...].astype(F32)
    a, b = messages_to_half(ms, 0, 4, mat), messages_to_half(ms, 2, 4, mat)
    a_ref[...] = a
    b_ref[...] = b
    x_ref[...] = dot(a, b, 1, 1)


def outgoing_kernel(other, a, x_mine, b_ref, send_ref, os, mat, send):
    os[...] = other[...].astype(F32)
    b = messages_to_half(os, 2, 4, mat)
    b_ref[...] = b
    half_to_messages(by_parity(x_mine[...], dot(a[...], b, 1, 1)), mat, send, 0, 2)
    send_ref[...] = send[...].astype(BF16)


def incoming_mine_kernel(mine, a_ref, b_ref, x_ref, ms, mat):
    ms[...] = mine[...].astype(F32)
    a, b = messages_to_half(ms, 0, 4, mat), messages_to_half(ms, 2, 4, mat)
    a_ref[...] = a
    b_ref[...] = b
    x_ref[...] = dot(own_columns(a), b, 0, 0)


def incoming_kernel(other, x_mine, send_ref, os, mat, send):
    os[...] = other[...].astype(F32)
    a, b = messages_to_half(os, 0, 4, mat), messages_to_half(os, 2, 4, mat)
    half_to_messages(halves(x_mine[...] + dot(own_columns(a), b, 0, 0)), mat, send, 0, 2)
    send_ref[...] = send[...].astype(BF16)


def incoming_back_mine_kernel(mine, a, b, ga_ref, gb_ref, ms, mat):
    ms[...] = mine[...].astype(F32)
    gx = messages_to_half(ms, 0, 2, mat)
    ga_ref[...] = dot(b[...], gx, 1, 1)
    gb_ref[...] = dot(own_columns(a[...]), gx, 1, 0)


def incoming_back_kernel(other, a, b, ga_mine, gb_mine, send_ref, os, mat, send):
    os[...] = other[...].astype(F32)
    gx = messages_to_half(os, 0, 2, mat)
    half_to_messages(by_parity(ga_mine[...], dot(b[...], gx, 1, 1)), mat, send, 0, 4)
    gb = gb_mine[...] + dot(other_columns(a[...]), gx, 1, 0)
    half_to_messages(halves(gb), mat, send, 2, 4)
    send_ref[...] = send[...].astype(BF16)


def other_rows_kernel(other_ab, a_ref, os, mat):
    os[...] = other_ab[...].astype(F32)
    a_ref[...] = messages_to_half(os, 0, 4, mat)


def outgoing_back_mine_kernel(mine, a, b, b_other, ga_ref, gb_ref, ms, mat, send):
    ms[...] = mine[...].astype(F32)
    gx = messages_to_half(ms, 0, 2, mat)
    even, odd = by_parity(b[...], b_other[...])
    ga = dot(gx, jnp.concatenate([even, odd], axis=0), 1, 0)
    half_to_messages(halves(ga), mat, send, 0, 2)
    ga_ref[...] = send[...]
    gb_ref[...] = dot(own_columns(gx), a[...], 0, 0)


def outgoing_back_kernel(other, ga, gb_mine, a_other, send_ref, os, mat, send):
    os[...] = other[...].astype(F32)
    gx = messages_to_half(os, 0, 2, mat)
    gb = gb_mine[...] + dot(own_columns(gx), a_other[...], 0, 0)
    half_to_messages(halves(gb), mat, send, 2, 4)
    for half in range(2):
        send[pl.ds(half, CH, stride=4), :] = ga[pl.ds(half, CH, stride=2), :]
    send_ref[...] = send[...].astype(BF16)


def call(kernel, name, outs, scratch, *args, **kwargs):
    return pl.pallas_call(
        kernel,
        name=name,
        out_shape=[jax.ShapeDtypeStruct(s, d) for s, d in outs],
        scratch_shapes=[s if not isinstance(s, tuple) else pltpu.VMEM(*s) for s in scratch],
        compiler_params=pltpu.CompilerParams(vmem_limit_bytes=24 * 1024 * 1024),
        cost_estimate=pl.CostEstimate(flops=2**24, bytes_accessed=2**20, transcendentals=0),
        **kwargs,
    )(*args)


def exchange(value, axes=CHIPS):
    return lax.all_to_all(value, axes, 0, 0, tiled=True)


def swap_cores(value):
    return lax.ppermute(value, "h", [(0, 1), (1, 0)])


def after(done, *values):
    return lax.optimization_barrier((done,) + values)[1:]


def shards(pair, pair_cot, mask, chain_ids, chain_bias, w_in, w_gate, w_out, in_gain, out_gain):
    block = pair.shape
    pair = pair.reshape(POS, CH)
    cot_in = pair_cot.reshape(POS, CH)
    mask, chain, bias = mask[None, :], chain_ids[None, :], chain_bias[None, :]
    field, field16 = ((CH, POS), F32), ((CH, POS), BF16)
    square, work = ((128, 128), F32), ((2, 128, 128), F32)

    def rows(n, dtype=F32):
        return ((n, 128), dtype)

    operands = [
        pltpu.with_memory_space_constraint(v, pltpu.HBM)
        for v in (pair, mask, chain, bias, in_gain, out_gain, w_in, w_gate)
    ]
    z0, n0, m, gains, w_in0, w_gate0, send = call(
        start_kernel, "start",
        [field, field16, ((8, POS), F32), rows(4), ((128, 512), BF16), rows(128, BF16), rows(512, BF16)],
        [(v.shape, v.dtype) for v in operands[:6]] + [rows(512), pltpu.SemaphoreType.DMA((8,))],
        *operands, in_specs=[pl.BlockSpec(memory_space=pltpu.HBM)] * 8,
    )
    mine = exchange(send)
    other_ab = swap_cores(mine)
    a0, b0, x_mine = call(
        outgoing_mine_kernel, "outgoing_mine", [field16, field16, square], [rows(512), work], mine
    )
    factors = ((512, POS), F32)
    g0, factors0 = call(
        side_kernel, "side0", [field, factors], [], *after(mine, n0), m, w_in0, w_gate0
    )
    (gains,) = call(columns_kernel, "columns", [((4, CH, POS), F32)], [], *after(mine, gains))
    b0_other, send = call(
        outgoing_kernel, "outgoing", [field16, rows(256, BF16)], [rows(512), work, rows(256)],
        other_ab, a0, *after((g0, gains), x_mine),
    )
    x0 = exchange(send)
    z1, y0, n1, w_in1, w_gate1, hats, rstds, xn0, send = call(
        middle_kernel, "middle", [field, field, field16, ((128, 512), BF16), rows(128, BF16), ((2, CH, POS), F32), ((16, POS), F32),
         field16, rows(512, BF16)],
        [rows(256), rows(512)], x0, z0, g0, m, gains, w_in, w_gate, w_out,
    )
    mine = exchange(send)
    other = swap_cores(mine)
    a1, b1, x_mine = call(
        incoming_mine_kernel, "incoming_mine", [field16, field16, field], [rows(512), work], mine
    )
    (a0_other,) = call(
        other_rows_kernel, "other_rows", [field16], [rows(512), work], *after(mine, other_ab)
    )
    g1, factors1 = call(
        side_kernel, "side1", [field, factors], [], *after(mine, n1), m, w_in1, w_gate1
    )
    (send,) = call(
        incoming_kernel, "incoming", [rows(256, BF16)], [rows(512), work, rows(256)],
        other, *after((a0_other, g1), x_mine),
    )
    cot, y1, xn, dy, dpg1, send = call(
        turn_kernel, "turn", [field, field, field16, field16, field16, rows(256, BF16)],
        [rows(256), rows(256)], exchange(send), g1, cot_in, gains, w_out,
    )
    mine = exchange(send)
    other = swap_cores(mine)
    ga, gb = call(
        incoming_back_mine_kernel, "incoming_back_mine", [square, field], [rows(256), work], mine, a1, b1
    )
    new_pair, gw1 = call(
        turn_rest_kernel, "turn_rest", [rows(POS, BF16), rows(256, BF16)], [],
        *after(mine, z1, y1, g1, n1, xn, dy, dpg1),
    )
    (send,) = call(
        incoming_back_kernel, "incoming_back", [rows(512, BF16)], [rows(256), work, rows(512)],
        other, a1, b1, *after(gw1, ga, gb),
    )
    dz1, dp1, dpg0, dy, send = call(
        back_kernel, "back", [field, ((512, POS), BF16), field16, field16, rows(256, BF16)],
        [rows(512), rows(256)],
        exchange(send), factors1, hats, rstds, dpg1, cot, g0, y0, gains, w_in, w_gate, w_out,
    )
    mine = exchange(send)
    other = swap_cores(mine)
    ga, gb = call(
        outgoing_back_mine_kernel, "outgoing_back_mine", [rows(256), field],
        [rows(256), work, rows(256)], mine, a0, b0, b0_other,
    )
    (early,) = call(
        back_rest_kernel, "back_rest", [rows(1024, BF16)], [], *after(mine, n1, dp1, gw1, n0, dpg0, xn0, dy)
    )
    (send,) = call(
        outgoing_back_kernel, "outgoing_back", [rows(512, BF16)], [rows(256), work, rows(512)],
        other, *after(early, ga, gb), a0_other,
    )
    dp0, mine, send = call(
        end_kernel, "end", [((512, POS), BF16), rows(768), rows(768, BF16)], [rows(512)],
        exchange(send), factors0, n0, early,
    )
    other = swap_cores(send)
    (pair_grad,) = call(
        end_rest_kernel, "end_rest", [rows(POS)], [], dp0, z0, dpg0, dz1, gains, w_in, w_gate
    )
    (send,) = call(
        core_sum_kernel, "core_sum", [rows(768, BF16)], [], *after(pair_grad, mine), other
    )
    (send,) = call(sum_kernel, "plane_sum", [rows(384, BF16)], [], exchange(send, PLANE))
    (send,) = call(sum_kernel, "line_sum", [rows(1536, BF16)], [], exchange(send, LINE))
    weights = [((2, 128, 512), F32), ((2, 128, 128), F32), ((2, 128, 128), F32)]
    in_grad, gate_grad, out_grad = call(
        place_kernel, "place", weights, weights + [pltpu.SemaphoreType.DMA((4,))],
        exchange(send, ("h",) + PLANE), out_specs=[pl.BlockSpec(memory_space=pltpu.HBM)] * 3,
    )
    return (new_pair.reshape(block), pair_grad.reshape(block), in_grad, gate_grad, out_grad)


def solution(mesh):
    devices = mesh.devices.reshape(tuple(SIZES.values()))
    split = P(("y", "zl", "h"), ("zh", "x"), None)
    return jax.shard_map(
        shards,
        mesh=Mesh(devices, tuple(SIZES)),
        in_specs=(split, split) + (P(),) * 8,
        out_specs=(split, split, P(), P(), P()),
        check_vma=False,
    )
```

```python
import functools

import jax
import jax.numpy as jnp
from jax import lax
from jax.experimental import pallas as pl
from jax.experimental.pallas import tpu as pltpu
from jax.sharding import Mesh, PartitionSpec as P

F32 = jnp.float32
BF16 = jnp.bfloat16
POS = 256
CH = 128
EPS = 1e-05
SIZES = {"y": 4, "zl": 2, "h": 2, "zh": 4, "x": 4}
CHIPS = ("zh", "x", "y", "zl")
PLANE = ("x", "y")
LINE = ("zl", "zh")


def dot(a, b, ca, cb):
    return lax.dot_general(
        a.astype(BF16), b.astype(BF16), (((ca,), (cb,)), ((), ())), preferred_element_type=F32
    )


def swap_blocks(tiles):
    block = lax.broadcasted_iota(jnp.int32, tiles[0].shape, 1) // 16
    high = block >= 4
    out = list(tiles)
    for t in range(4):
        lo, hi = tiles[t], tiles[t + 4]
        crossed = pltpu.roll(jnp.where(high, lo, hi), 64, 1)
        out[t] = jnp.where(high, crossed, lo)
        out[t + 4] = jnp.where(high, hi, crossed)
    tiles, out = out, []
    for i in range(8):
        value = tiles[i]
        for t in range(4):
            if t != i % 4:
                moved = pltpu.roll(tiles[i - i % 4 + t], 16 * (t - i % 4) % 128, 1)
                value = jnp.where(block % 4 == t, moved, value)
        out.append(value)
    return out


def swap_at_once(tiles):
    block = lax.broadcasted_iota(jnp.int32, tiles[0].shape, 1) // 16
    out = []
    for i in range(8):
        value = tiles[i]
        for t in range(8):
            if t != i:
                value = jnp.where(block == t, pltpu.roll(tiles[t], 16 * ((t - i) % 8), 1), value)
        out.append(value)
    return out


def messages_to_half(src, off, w, dst, swap=swap_blocks):
    for half in range(2):
        tiles = [
            src[pl.ds(16 * t * w + off + half, 16, stride=w), :].astype(BF16) for t in range(8)
        ]
        for t, tile in enumerate(swap(tiles)):
            tile = tile.astype(F32)
            for p in range(2):
                dst[p, pl.ds(half * 8 + t, 8, stride=16), :] = tile[8 * p : 8 * (p + 1)]
    return jnp.concatenate([dst[0], dst[1]], axis=1).astype(BF16)


def half_to_messages(value, src, dst, off, w, swap=swap_blocks):
    for p in range(2):
        src[p] = value[p]
    for half in range(2):
        tiles = []
        for t in range(8):
            both = [src[p, pl.ds(half * 8 + t, 8, stride=16), :] for p in range(2)]
            tiles.append(jnp.concatenate(both, axis=0).astype(BF16))
        for t, tile in enumerate(swap(tiles)):
            dst[pl.ds(16 * t * w + off + half, 16, stride=w), :] = tile.astype(F32)


def halves(value):
    return value[:, 0:128], value[:, 128:256]


def by_parity(mine, other):
    first = lax.axis_index("h") == 0
    return jnp.where(first, mine, other), jnp.where(first, other, mine)


def own_columns(value):
    return by_parity(*halves(value))[0]


def other_columns(value):
    return by_parity(*halves(value))[1]


def channels_to_messages(v, dst, off, w):
    for half in range(2):
        dst[pl.ds(off + half, CH, stride=w), :] = v[:, half * 128 : (half + 1) * 128]


def messages_to_channels(src, off, w):
    return jnp.concatenate(
        [src[pl.ds(off + half, CH, stride=w), :] for half in range(2)], axis=1
    )


def column(row):
    square = jnp.broadcast_to(row, (CH, CH)).T
    return jnp.concatenate([square, square], axis=1)


def normalise(z):
    centered = z - jnp.mean(z, axis=0, keepdims=True)
    rstd = lax.rsqrt(jnp.mean(centered * centered, axis=0, keepdims=True) + EPS)
    return centered * rstd, rstd


def normalise_back(cot, hat, rstd):
    return rstd * (
        cot
        - jnp.mean(cot, axis=0, keepdims=True)
        - hat * jnp.mean(cot * hat, axis=0, keepdims=True)
    )


def prepare(z, gain, w_in, m, n_ref, send, send_ref, copies=()):
    hat, _ = normalise(z)
    normed = (hat * gain).astype(BF16)
    n_ref[...] = normed
    for copy in copies:
        copy.wait()
    p = dot(w_in[...], normed, 0, 0)
    a = m * jax.nn.sigmoid(p[0:128]) * p[128:256]
    b = m * jax.nn.sigmoid(p[256:384]) * p[384:512]
    channels_to_messages(a, send, 0, 4)
    channels_to_messages(b, send, 2, 4)
    send_ref[...] = send[...].astype(BF16)


def project_back(recv, factors, dp):
    for k in range(2):
        cot = messages_to_channels(recv, 2 * k, 4)
        for e in range(2 * k, 2 * k + 2):
            block = slice(128 * e, 128 * (e + 1))
            dp[block, :] = (cot * factors[block, :]).astype(BF16)


def normed_back(dp, z, gain, w_in, w_gate, dpg):
    dn = dot(w_in, dp[...], 1, 0) + dot(w_gate, dpg, 1, 0)
    hat, rstd = normalise(z)
    return normalise_back(dn * gain, hat, rstd)


def start_kernel(*refs):
    hbm, (z_ref, n_ref, m_ref, gain_ref, w_in, w_gate, send_ref), refs = refs[:8], refs[8:15], refs[15:]
    vmem, send, sem = refs[:6] + (w_in, w_gate), refs[6], refs[7]
    copies = [
        pltpu.make_async_copy(src.at[0] if k > 5 else src, dst, sem.at[k])
        for k, (src, dst) in enumerate(zip(hbm, vmem))
    ]
    for copy in copies:
        copy.start()
    pair, mask, chain, bias, in_gain, out_gain = vmem[:6]
    row = (lax.axis_index("y") * 2 + lax.axis_index("zl")) * 2 + lax.axis_index("h")
    col = lax.axis_index("zh") * 4 + lax.axis_index("x")
    res = lax.broadcasted_iota(jnp.int32, (256, POS), 0)
    pos = lax.broadcasted_iota(jnp.int32, (256, POS), 1)
    in_row = (res == row * 16 + pos // 16).astype(F32)
    in_col = (res == col * 16 + pos % 16).astype(F32)
    for copy in copies[:6]:
        copy.wait()
    both = jnp.concatenate(
        [
            jnp.broadcast_to(mask[...].astype(F32), (8, 256)),
            jnp.broadcast_to(chain[...].astype(F32), (8, 256)),
        ],
        axis=0,
    )
    of_row = dot(both, in_row, 1, 0)
    of_col = dot(both, in_col, 1, 0)
    m8 = of_row[0:8] * of_col[0:8]
    m_ref[...] = m8
    gain_ref[0:2, :] = in_gain[...]
    gain_ref[2:4, :] = out_gain[...]
    same = (of_row[8:9] == of_col[8:9]).astype(F32)
    z = pair[...].astype(F32).T + same * column(bias[...])
    z_ref[...] = z
    gain = column(in_gain[0:1])
    prepare(z, gain, w_in, m8[0:1], n_ref, send, send_ref, copies[6:7])
    copies[7].wait()


def side_kernel(normed, m, w_in, w_gate, g_ref, factor_ref):
    p = dot(w_in[...], normed[...], 0, 0)
    for k in range(2):
        s = jax.nn.sigmoid(p[256 * k : 256 * k + 128])
        ms = m[0:1] * s
        factor_ref[256 * k : 256 * k + 128, :] = ms * (1.0 - s) * p[256 * k + 128 : 256 * k + 256]
        factor_ref[256 * k + 128 : 256 * k + 256, :] = ms
    g_ref[...] = jax.nn.sigmoid(dot(w_gate[...], normed[...], 0, 0))


def middle_kernel(x_in, z0, g0, m, gains, w_in, w_gate, w_out, z_ref, y_ref, n_ref, w_in_ref, w_gate_ref, send_ref, xs, send):
    w_in_ref[...] = w_in[1]
    w_gate_ref[...] = w_gate[1]
    xs[...] = x_in[...].astype(F32)
    hat, _ = normalise(messages_to_channels(xs, 0, 2))
    y = dot(w_out[0], hat * column(gains[2:3]), 0, 0)
    y_ref[...] = y
    z = z0[...] + g0[...] * y
    z_ref[...] = z
    prepare(z, column(gains[1:2]), w_in.at[1], m[0:1], n_ref, send, send_ref)


def turn_kernel(x_in, g1, cot_in, gains, w_out, cot_ref, y_ref, xn_ref, dy_ref, dpg_ref, send_ref, xs, send):
    xs[...] = x_in[...].astype(F32)
    gain = column(gains[3:4])
    hat, rstd = normalise(messages_to_channels(xs, 0, 2))
    xn = (hat * gain).astype(BF16)
    xn_ref[...] = xn
    y = dot(w_out[1], xn, 0, 0)
    y_ref[...] = y
    g = g1[...]
    cot = cot_in[...].astype(F32).T
    cot_ref[...] = cot
    dy = (cot * g).astype(BF16)
    dy_ref[...] = dy
    dpg_ref[...] = (cot * y * g * (1.0 - g)).astype(BF16)
    gx = normalise_back(dot(w_out[1], dy, 1, 0) * gain, hat, rstd)
    channels_to_messages(gx, send, 0, 2)
    send_ref[...] = send[...].astype(BF16)


def turn_rest_kernel(z1, y1, g1, n1, xn, dy, dpg, new_ref, gw_ref):
    new_ref[...] = (z1[...] + g1[...] * y1[...]).T.astype(BF16)
    gw_ref[0:128, :] = dot(n1[...], dpg[...], 1, 1).astype(BF16)
    gw_ref[128:256, :] = dot(xn[...], dy[...], 1, 1).astype(BF16)


def back_kernel(gab, factors, z1, dpg1, cot, x_in, g0, y0, gains, w_in, w_gate, w_out, dz_ref, dp_ref, dpg_ref, xn_ref, dy_ref, send_ref, rs, xs, send):
    rs[...] = gab[...].astype(F32)
    project_back(rs, factors, dp_ref)
    dz = cot[...] + normed_back(
        dp_ref, z1[...], column(gains[1:2]), w_in[1], w_gate[1], dpg1[...]
    )
    dz_ref[...] = dz
    g = g0[...]
    dpg_ref[...] = (dz * y0[...] * g * (1.0 - g)).astype(BF16)
    dy = (dz * g).astype(BF16)
    dy_ref[...] = dy
    xs[...] = x_in[...].astype(F32)
    gain = column(gains[2:3])
    hat, rstd = normalise(messages_to_channels(xs, 0, 2))
    xn_ref[...] = (hat * gain).astype(BF16)
    gx = normalise_back(dot(w_out[0], dy, 1, 0) * gain, hat, rstd)
    channels_to_messages(gx, send, 0, 2)
    send_ref[...] = send[...].astype(BF16)


def back_rest_kernel(n1, dp1, gw1, n0, dpg0, xn, dy, early_ref):
    for e in range(4):
        block = slice(128 * e, 128 * (e + 1))
        early_ref[block, :] = dot(n1[...], dp1[block, :], 1, 1).astype(BF16)
    early_ref[512:768, :] = gw1[...]
    early_ref[768:896, :] = dot(n0[...], dpg0[...], 1, 1).astype(BF16)
    early_ref[896:1024, :] = dot(xn[...], dy[...], 1, 1).astype(BF16)


def end_kernel(gab, factors, n0, early, dp_ref, mine_ref, send_ref, rs):
    rs[...] = gab[...].astype(F32)
    project_back(rs, factors, dp_ref)
    first = lax.axis_index("h") == 0
    parts = [dot(n0[...], dp_ref[128 * e : 128 * (e + 1), :], 1, 1) for e in range(4)]
    parts += [early[128 * k : 128 * (k + 1), :].astype(F32) for k in range(8)]
    for k, (low, high) in enumerate([(0, 2), (1, 3), (4, 8), (5, 9), (6, 10), (7, 11)]):
        block = slice(128 * k, 128 * (k + 1))
        mine_ref[block, :] = jnp.where(first, parts[low], parts[high])
        send_ref[block, :] = jnp.where(first, parts[high], parts[low]).astype(BF16)


def end_rest_kernel(dp, z0, dpg0, dz1, gains, w_in, w_gate, grad_ref):
    dz = dz1[...] + normed_back(dp, z0[...], column(gains[0:1]), w_in[0], w_gate[0], dpg0[...])
    grad_ref[...] = dz.T


def core_sum_kernel(mine, other, send_ref):
    send_ref[...] = (mine[...] + other[...].astype(F32)).astype(BF16)


def sum_kernel(recv, send_ref):
    total = recv[0:48, :].astype(F32)
    for k in range(1, recv.shape[0] // 48):
        total = total + recv[48 * k : 48 * (k + 1), :].astype(F32)
    total = total.astype(BF16)
    for k in range(send_ref.shape[0] // 48):
        send_ref[48 * k : 48 * (k + 1), :] = total


def place_kernel(core_of, rows, *refs):
    in_out, gate_out, out_out, in_ref, gate_ref, out_ref, sem = refs[-7:]

    def block(k):
        return rows[128 * k : 128 * (k + 1), :].astype(F32)

    def write(src, dst, k):
        copy = pltpu.make_async_copy(src, dst, sem.at[k])
        copy.start()
        return copy

    def low():
        for e in range(2):
            in_ref[0, :, 128 * e : 128 * (e + 1)] = block(e)
        copies = [write(in_ref.at[0, :, 0:256], in_out.at[0, :, 0:256], 0)]
        for e in range(4):
            in_ref[1, :, 128 * e : 128 * (e + 1)] = block(2 + e)
        copies.append(write(in_ref.at[1], in_out.at[1], 1))
        for copy in copies:
            copy.wait()

    def high():
        for e in range(2):
            in_ref[0, :, 128 * (2 + e) : 128 * (3 + e)] = block(e)
        copies = [write(in_ref.at[0, :, 256:512], in_out.at[0, :, 256:512], 0)]
        for k, u in ((2, 1), (4, 0)):
            gate_ref[u] = block(k)
            out_ref[u] = block(k + 1)
        copies += [write(gate_ref, gate_out, 1), write(out_ref, out_out, 2)]
        for copy in copies:
            copy.wait()

    is_low = lax.axis_index("h") == core_of
    pl.when(is_low)(low)
    pl.when(jnp.logical_not(is_low))(high)


def outgoing_mine_kernel(mine, a_ref, b_ref, x_ref, ms, mat):
    ms[...] = mine[...].astype(F32)
    a, b = messages_to_half(ms, 0, 4, mat), messages_to_half(ms, 2, 4, mat)
    a_ref[...] = a
    b_ref[...] = b
    x_ref[...] = dot(a, b, 1, 1)


def outgoing_kernel(other, a, x_mine, b_ref, send_ref, os, mat, send):
    os[...] = other[...].astype(F32)
    b = messages_to_half(os, 2, 4, mat, swap_at_once)
    b_ref[...] = b
    half_to_messages(by_parity(x_mine[...], dot(a[...], b, 1, 1)), mat, send, 0, 2, swap_at_once)
    send_ref[...] = send[...].astype(BF16)


def incoming_mine_kernel(mine, a_ref, b_ref, x_ref, ms, mat):
    ms[...] = mine[...].astype(F32)
    a, b = messages_to_half(ms, 0, 4, mat), messages_to_half(ms, 2, 4, mat)
    a_ref[...] = a
    b_ref[...] = b
    x_ref[...] = dot(own_columns(a), b, 0, 0)


def incoming_kernel(other, x_mine, send_ref, os, mat, send):
    os[...] = other[...].astype(F32)
    a, b = messages_to_half(os, 0, 4, mat), messages_to_half(os, 2, 4, mat)
    half_to_messages(halves(x_mine[...] + dot(own_columns(a), b, 0, 0)), mat, send, 0, 2)
    send_ref[...] = send[...].astype(BF16)


def incoming_back_mine_kernel(mine, a, b, ga_ref, gb_ref, ms, mat):
    ms[...] = mine[...].astype(F32)
    gx = messages_to_half(ms, 0, 2, mat)
    ga_ref[...] = dot(b[...], gx, 1, 1)
    gb_ref[...] = dot(own_columns(a[...]), gx, 1, 0)


def incoming_back_kernel(other, a, b, ga_mine, gb_mine, send_ref, os, mat, send):
    os[...] = other[...].astype(F32)
    gx = messages_to_half(os, 0, 2, mat)
    half_to_messages(by_parity(ga_mine[...], dot(b[...], gx, 1, 1)), mat, send, 0, 4)
    gb = gb_mine[...] + dot(other_columns(a[...]), gx, 1, 0)
    half_to_messages(halves(gb), mat, send, 2, 4)
    send_ref[...] = send[...].astype(BF16)


def other_rows_kernel(other_ab, a_ref, os, mat):
    os[...] = other_ab[...].astype(F32)
    a_ref[...] = messages_to_half(os, 0, 4, mat)


def outgoing_back_mine_kernel(mine, a, b, b_other, ga_ref, gb_ref, ms, mat, send):
    ms[...] = mine[...].astype(F32)
    gx = messages_to_half(ms, 0, 2, mat)
    even, odd = by_parity(b[...], b_other[...])
    ga = dot(gx, jnp.concatenate([even, odd], axis=0), 1, 0)
    half_to_messages(halves(ga), mat, send, 0, 2)
    ga_ref[...] = send[...]
    gb_ref[...] = dot(own_columns(gx), a[...], 0, 0)


def outgoing_back_kernel(other, ga, gb_mine, a_other, send_ref, os, mat, send):
    os[...] = other[...].astype(F32)
    gx = messages_to_half(os, 0, 2, mat, swap_at_once)
    gb = gb_mine[...] + dot(own_columns(gx), a_other[...], 0, 0)
    half_to_messages(halves(gb), mat, send, 2, 4, swap_at_once)
    for half in range(2):
        send[pl.ds(half, CH, stride=4), :] = ga[pl.ds(half, CH, stride=2), :]
    send_ref[...] = send[...].astype(BF16)


def call(kernel, name, outs, scratch, *args, **kwargs):
    return pl.pallas_call(
        kernel,
        name=name,
        out_shape=[jax.ShapeDtypeStruct(s, d) for s, d in outs],
        scratch_shapes=[s if not isinstance(s, tuple) else pltpu.VMEM(*s) for s in scratch],
        compiler_params=pltpu.CompilerParams(vmem_limit_bytes=24 * 1024 * 1024),
        cost_estimate=pl.CostEstimate(flops=2**24, bytes_accessed=2**20, transcendentals=0),
        **kwargs,
    )(*args)


def exchange(value, axes=CHIPS):
    return lax.all_to_all(value, axes, 0, 0, tiled=True)


def swap_cores(value):
    return lax.ppermute(value, "h", [(0, 1), (1, 0)])


def after(done, *values):
    return lax.optimization_barrier((done,) + values)[1:]


def shards(pair, pair_cot, mask, chain_ids, chain_bias, w_in, w_gate, w_out, in_gain, out_gain):
    block = pair.shape
    pair = pair.reshape(POS, CH)
    cot_in = pair_cot.reshape(POS, CH)
    mask, chain, bias = mask[None, :], chain_ids[None, :], chain_bias[None, :]
    field, field16 = ((CH, POS), F32), ((CH, POS), BF16)
    square, work = ((128, 128), F32), ((2, 128, 128), F32)

    def rows(n, dtype=F32):
        return ((n, 128), dtype)

    operands = [
        pltpu.with_memory_space_constraint(v, pltpu.HBM)
        for v in (pair, mask, chain, bias, in_gain, out_gain, w_in, w_gate)
    ]
    z0, n0, m, gains, w_in0, w_gate0, send = call(
        start_kernel, "start",
        [field, field16, ((8, POS), F32), rows(4), ((128, 512), BF16), rows(128, BF16), rows(512, BF16)],
        [(v.shape, v.dtype) for v in operands[:6]] + [rows(512), pltpu.SemaphoreType.DMA((8,))],
        *operands, in_specs=[pl.BlockSpec(memory_space=pltpu.HBM)] * 8,
    )
    mine = exchange(send)
    other_ab = swap_cores(mine)
    a0, b0, x_mine = call(
        outgoing_mine_kernel, "outgoing_mine", [field16, field16, square], [rows(512), work], mine
    )
    factors = ((512, POS), F32)
    g0, factors0 = call(
        side_kernel, "side0", [field, factors], [], *after(mine, n0), m, w_in0, w_gate0
    )
    b0_other, send = call(
        outgoing_kernel, "outgoing", [field16, rows(256, BF16)], [rows(512), work, rows(256)],
        other_ab, a0, *after(g0, x_mine),
    )
    x0 = exchange(send)
    z1, y0, n1, w_in1, w_gate1, send = call(
        middle_kernel, "middle", [field, field, field16, ((128, 512), BF16), rows(128, BF16), rows(512, BF16)],
        [rows(256), rows(512)], x0, z0, g0, m, gains, w_in, w_gate, w_out,
    )
    mine = exchange(send)
    other = swap_cores(mine)
    a1, b1, x_mine = call(
        incoming_mine_kernel, "incoming_mine", [field16, field16, field], [rows(512), work], mine
    )
    (a0_other,) = call(
        other_rows_kernel, "other_rows", [field16], [rows(512), work], *after(mine, other_ab)
    )
    g1, factors1 = call(
        side_kernel, "side1", [field, factors], [], *after(mine, n1), m, w_in1, w_gate1
    )
    (send,) = call(
        incoming_kernel, "incoming", [rows(256, BF16)], [rows(512), work, rows(256)],
        other, *after((a0_other, g1), x_mine),
    )
    cot, y1, xn, dy, dpg1, send = call(
        turn_kernel, "turn", [field, field, field16, field16, field16, rows(256, BF16)],
        [rows(256), rows(256)], exchange(send), g1, cot_in, gains, w_out,
    )
    mine = exchange(send)
    other = swap_cores(mine)
    ga, gb = call(
        incoming_back_mine_kernel, "incoming_back_mine", [square, field], [rows(256), work], mine, a1, b1
    )
    new_pair, gw1 = call(
        turn_rest_kernel, "turn_rest", [rows(POS, BF16), rows(256, BF16)], [],
        *after(mine, z1, y1, g1, n1, xn, dy, dpg1),
    )
    (send,) = call(
        incoming_back_kernel, "incoming_back", [rows(512, BF16)], [rows(256), work, rows(512)],
        other, a1, b1, *after(gw1, ga, gb),
    )
    dz1, dp1, dpg0, xn, dy, send = call(
        back_kernel, "back", [field, ((512, POS), BF16), field16, field16, field16, rows(256, BF16)],
        [rows(512), rows(256), rows(256)],
        exchange(send), factors1, z1, dpg1, cot, x0, g0, y0, gains, w_in, w_gate, w_out,
    )
    mine = exchange(send)
    other = swap_cores(mine)
    ga, gb = call(
        outgoing_back_mine_kernel, "outgoing_back_mine", [rows(256), field],
        [rows(256), work, rows(256)], mine, a0, b0, b0_other,
    )
    (early,) = call(
        back_rest_kernel, "back_rest", [rows(1024, BF16)], [], *after(mine, n1, dp1, gw1, n0, dpg0, xn, dy)
    )
    (send,) = call(
        outgoing_back_kernel, "outgoing_back", [rows(512, BF16)], [rows(256), work, rows(512)],
        other, *after(early, ga, gb), a0_other,
    )
    dp0, mine, send = call(
        end_kernel, "end", [((512, POS), BF16), rows(768), rows(768, BF16)], [rows(512)],
        exchange(send), factors0, n0, early,
    )
    other = swap_cores(send)
    (pair_grad,) = call(
        end_rest_kernel, "end_rest", [rows(POS)], [], dp0, z0, dpg0, dz1, gains, w_in, w_gate
    )
    (send,) = call(
        core_sum_kernel, "core_sum", [rows(768, BF16)], [], *after(pair_grad, mine), other
    )
    (send,) = call(sum_kernel, "plane_sum", [rows(384, BF16)], [], exchange(send, PLANE))
    (send,) = call(sum_kernel, "line_sum", [rows(768, BF16)], [], exchange(send, LINE))
    mine = exchange(send, PLANE)
    weights = [((2, 128, 512), F32), ((2, 128, 128), F32), ((2, 128, 128), F32)]
    hbm = [pl.BlockSpec(memory_space=pltpu.HBM)] * 3
    scratch = weights + [pltpu.SemaphoreType.DMA((3,))]
    other = swap_cores(mine)
    grads = call(
        functools.partial(place_kernel, 0), "place_mine", weights, scratch, mine, out_specs=hbm
    )
    in_grad, gate_grad, out_grad = call(
        functools.partial(place_kernel, 1), "place_other", weights, scratch, other, *grads,
        in_specs=[pl.BlockSpec(memory_space=pltpu.VMEM)] + hbm, out_specs=hbm,
        input_output_aliases={1: 0, 2: 1, 3: 2},
    )
    return (new_pair.reshape(block), pair_grad.reshape(block), in_grad, gate_grad, out_grad)


def solution(mesh):
    devices = mesh.devices.reshape(tuple(SIZES.values()))
    split = P(("y", "zl", "h"), ("zh", "x"), None)
    return jax.shard_map(
        shards,
        mesh=Mesh(devices, tuple(SIZES)),
        in_specs=(split, split) + (P(),) * 8,
        out_specs=(split, split, P(), P(), P()),
        check_vma=False,
    )
```
